32 devices in a mesh: dp: 8 (over z, x), cls: 4 (over y, core).
Axes of the slice: x: 2, y: 2, z: 4, core: 2. Of those that a mesh axis runs over, the one named last changes fastest.
Arguments:
- images: bfloat16 [1024, 64, 512], P('dp'), may hold values from -12 to 12
- pose_slot: int32 [1024], P('dp'), may hold values from 0 to 1023, as said below
- references: bfloat16 [256, 64, 512], P('cls'), may hold values from -4 to 4
- rotation_response: float32 [36, 512], replicated, may hold values from -1 to 1
- shell_weight: float32 [64], replicated, may hold values from 0.003 to 0.03
- class_lists: int32 [1024, 2], P('dp'), may hold values from 0 to 255, as said below
- class_counts: int32 [256], P('cls'), may hold values from 0 to 19999
Outputs:
- class_gradient: float32 [4, 64, 64, 512], P('cls', 'dp')
- log_evidence: float32 [1024], P('dp')
The draws below stay inside these ranges and needn't reach their ends.
Inputs may be any that keep to these rules, and one draw needn't show every extreme that they name: `pose_slot`: the particles of each micrograph block of 128 rows land exactly 16 in every pose block of 128 positions; each position is taken once. `class_lists`: each row names 2 different classes. Within each pose block of 128 rows every class that the block names is named by exactly 2 of its rows.
All inputs are finite; a program needn't handle non-finite values.
Results may differ from the reference program's by a relative error of at most 0.04.
Values may be sent and summed in bfloat16 or wider, within the bound.
A program may use at most 192 MiB of HBM per device.

```python
import math
import jax
import jax.numpy as jnp
from jax import lax

NSHELL = 64
NANG = 256
K = 256
NROT = 36
LIST = 2
P_BLK = 128
MOST = 2
P_SIZE = 1024
KCOL = 64
N_DP = 8
N_CLS = 4


def pose_table(key):
    block_count = P_SIZE // P_BLK
    per_pair = P_BLK // block_count
    source_key, target_key = jax.random.split(jax.random.fold_in(key, 7))
    source_perm = jax.vmap(lambda sub_key: jax.random.permutation(sub_key, P_BLK))(jax.random.split(source_key, block_count))
    target_perm = jax.vmap(lambda sub_key: jax.random.permutation(sub_key, P_BLK))(jax.random.split(target_key, block_count))
    local_pos = jnp.arange(P_BLK, dtype=jnp.int32)[None, :]
    source_block = jnp.arange(block_count, dtype=jnp.int32)[:, None]
    dest_block = jnp.broadcast_to(local_pos // per_pair, (block_count, P_BLK))
    arrival = source_block * per_pair + local_pos % per_pair
    slot_value = dest_block * P_BLK + target_perm[dest_block, arrival]
    inverse_perm = jnp.argsort(source_perm, axis=1)
    return jnp.take_along_axis(slot_value, inverse_perm, axis=1).reshape(P_SIZE).astype(jnp.int32)


def list_table(key):
    block_count = P_SIZE // P_BLK
    used_classes = P_BLK * LIST // MOST
    base_key = jax.random.fold_in(key, 9)
    heat_level = jax.random.randint(jax.random.fold_in(base_key, 1), (K,), 0, 2)

    def one_block(block_key):
        rank_key, perm_key = jax.random.split(block_key)
        noise_rank = jax.random.randint(rank_key, (K,), 0, 1 << 16)
        class_score = (heat_level * (1 << 15) + noise_rank) * K + jnp.arange(K, dtype=jnp.int32)
        class_order = jnp.argsort(-class_score)
        chosen = class_order[:used_classes]
        item_rows = jnp.repeat(chosen, MOST, total_repeat_length=used_classes * MOST).reshape(LIST, P_BLK)
        row_perms = jax.vmap(lambda sub_key: jax.random.permutation(sub_key, P_BLK))(jax.random.split(perm_key, LIST))
        list_rows = jnp.take_along_axis(item_rows, jnp.argsort(row_perms, axis=1), axis=1)
        return list_rows.T
    tables = jax.vmap(one_block)(jax.random.split(base_key, block_count))
    return tables.reshape(P_SIZE, LIST).astype(jnp.int32)


def reference_field(key):
    values = jax.random.normal(jax.random.fold_in(key, 31), (K, NSHELL, 2 * NANG), jnp.float32)
    return jnp.clip(values, -4.0, 4.0)


def draw_pose_slot(key, part):
    return pose_table(key)


def draw_class_lists(key, part):
    return list_table(key)


def draw_references(key, part):
    return reference_field(key).astype(jnp.bfloat16)


def draw_rotation_response(key, part):
    amplitude = jax.random.uniform(jax.random.fold_in(key, 41), (NROT, NANG), jnp.float32, 0.4, 1.0)
    frequency = jnp.arange(NANG, dtype=jnp.int32)
    signed = jnp.where(frequency < NANG // 2, frequency, frequency - NANG).astype(jnp.float32)
    rot_angle = jnp.arange(NROT, dtype=jnp.int32).astype(jnp.float32) * (2.0 * math.pi / NROT)
    phase_shift = -signed[None, :] * rot_angle[:, None]
    return jnp.concatenate([amplitude * jnp.cos(phase_shift), amplitude * jnp.sin(phase_shift)], axis=1)


def draw_images(key, part):
    drawn_rows = jnp.clip(jax.random.normal(jax.random.fold_in(key, 21), (P_SIZE, NSHELL, 2 * NANG), jnp.float32), -4.0, 4.0)
    ref_field = reference_field(key)
    pose_rows = pose_table(key)
    picked = list_table(key)[pose_rows]
    strength = jnp.array([0.5, 1.0, 2.0], jnp.float32)[jnp.arange(P_SIZE) % 3]
    aligned = strength[:, None, None] * (ref_field[picked[:, 0]] + ref_field[picked[:, 1]]) * 0.7071
    chosen_rows = jnp.arange(P_SIZE) % 4 == 0
    drawn_rows = jnp.where(chosen_rows[:, None, None], aligned, drawn_rows)
    return drawn_rows.astype(jnp.bfloat16)


def plant(entries, own_key, low, top_value):
    index_at = [jax.random.randint(jax.random.fold_in(own_key, axis), (), 0, length) for axis, length in enumerate(entries.shape)]
    longest = entries.shape.index(max(entries.shape))
    next_to = index_at[:longest] + [(index_at[longest] + 1) % entries.shape[longest]] + index_at[longest + 1:]
    return entries.at[tuple(index_at)].set(low).at[tuple(next_to)].set(top_value)


def setup_inputs(seed: int = 0) -> dict:
    splits = jax.random.split(jax.random.key(seed), 8)
    return {
        "images": draw_images(jax.random.fold_in(splits[7], 71), 0),
        "pose_slot": draw_pose_slot(jax.random.fold_in(splits[7], 71), 0),
        "references": draw_references(jax.random.fold_in(splits[7], 71), 0),
        "rotation_response": draw_rotation_response(jax.random.fold_in(splits[7], 71), 0),
        "shell_weight": jnp.clip(jnp.exp(jax.random.uniform(splits[4], (NSHELL,), jnp.float32, math.log(0.003), math.log(0.03))), 0.003, 0.03),
        "class_lists": draw_class_lists(jax.random.fold_in(splits[7], 71), 0),
        "class_counts": plant(jax.random.randint(splits[6], (K,), 0, 20000), jax.random.fold_in(splits[6], 1), 0, 19999).astype(jnp.int32),
    }


def angular_tables(points):
    positions = jnp.arange(points, dtype=jnp.int32)
    product = positions[:, None] * positions[None, :] % points
    angles = product.astype(jnp.float32) * (2.0 * math.pi / points)
    cosine = jnp.cos(angles) / math.sqrt(points)
    sine_part = jnp.sin(angles) / math.sqrt(points)
    upper_half = jnp.concatenate([cosine, -sine_part], axis=1)
    lower_half = jnp.concatenate([sine_part, cosine], axis=1)
    return jnp.concatenate([upper_half, lower_half], axis=0)

def reference(images, pose_slot, references, rotation_response, shell_weight, class_lists, class_counts):
    full_table = angular_tables(NANG)
    forward = full_table.astype(jnp.bfloat16)
    inverse = full_table.T
    row_width = 2 * NANG
    total_rows = images.shape[0]
    placed = jnp.zeros_like(images).at[pose_slot].set(images)
    image_hat = jnp.dot(placed.reshape(-1, row_width), forward, preferred_element_type=jnp.float32).astype(jnp.bfloat16).reshape(total_rows, NSHELL, row_width)
    ref_hat = jnp.dot(references.reshape(-1, row_width), forward, preferred_element_type=jnp.float32).astype(jnp.bfloat16).reshape(K, NSHELL, row_width)
    weighted = (ref_hat.astype(jnp.float32) * shell_weight[None, :, None]).astype(jnp.bfloat16)
    log_prior = jnp.log1p(class_counts.astype(jnp.float32))
    rot_re = rotation_response[:, :NANG]
    rot_im = rotation_response[:, NANG:]
    coef_table = jnp.concatenate([rot_re, -rot_im, rot_re * rot_re + rot_im * rot_im], axis=1)
    blocks_hat = image_hat.reshape(N_DP, P_BLK, NSHELL, row_width)
    blocks_list = class_lists.reshape(N_DP, P_BLK, LIST)

    def scan_block(carry_sums, inputs):
        numer_sum, denom_sum = carry_sums
        block_hat, block_list = inputs
        image_f = block_hat.astype(jnp.float32)[:, None]
        near_ref = weighted[block_list].astype(jnp.float32)
        cross_re = lax.optimization_barrier(jnp.sum(image_f[..., :NANG] * near_ref[..., :NANG] + image_f[..., NANG:] * near_ref[..., NANG:], axis=2))
        cross_im = lax.optimization_barrier(jnp.sum(image_f[..., NANG:] * near_ref[..., :NANG] - image_f[..., :NANG] * near_ref[..., NANG:], axis=2))
        cross_term = jnp.concatenate([cross_re, cross_im], axis=-1)
        scores = jnp.einsum('bln,rn->blr', cross_term, rotation_response, precision=lax.Precision.HIGHEST) + log_prior[block_list][..., None]
        top_score = lax.optimization_barrier(jnp.max(scores, axis=(1, 2)))
        expo_terms = jnp.exp(scores - top_score[:, None, None])
        total_sum = lax.optimization_barrier(jnp.sum(expo_terms, axis=(1, 2)))
        posterior = expo_terms / total_sum[:, None, None]
        evidence = top_score + jnp.log(total_sum)
        coef_rows = jnp.einsum('blr,rn->bln', posterior, coef_table, precision=lax.Precision.HIGHEST)
        coef_re = coef_rows[..., None, :NANG]
        coef_im = coef_rows[..., None, NANG:2 * NANG]
        volume = coef_rows[..., None, 2 * NANG:]
        post_sum = lax.optimization_barrier(jnp.sum(posterior, axis=2))
        own_ref = ref_hat[block_list].astype(jnp.float32)
        grad_re = image_f[..., :NANG] * coef_re - image_f[..., NANG:] * coef_im - volume * own_ref[..., :NANG]
        grad_im = image_f[..., :NANG] * coef_im + image_f[..., NANG:] * coef_re - volume * own_ref[..., NANG:]
        grad_rows = jnp.concatenate([grad_re, grad_im], axis=-1).reshape(-1, NSHELL, row_width)
        flat_list = block_list.reshape(-1)
        numer_sum = numer_sum + jax.ops.segment_sum(grad_rows, flat_list, num_segments=K)
        denom_sum = denom_sum + jax.ops.segment_sum(post_sum.reshape(-1), flat_list, num_segments=K)
        return ((numer_sum, denom_sum), evidence)
    start_sums = (jnp.zeros((K, NSHELL, row_width), jnp.float32), jnp.zeros((K,), jnp.float32))
    (numer_sum, denom_sum), evidence = lax.scan(scan_block, start_sums, (blocks_hat, blocks_list))
    scaled = numer_sum / (1.0 + denom_sum)[:, None, None]
    gradient = jnp.dot(scaled.reshape(-1, row_width), inverse, precision=lax.Precision.HIGHEST)
    gradient = gradient.reshape(N_CLS, KCOL, NSHELL, row_width)
    return (gradient, evidence.reshape(-1))
```

```python
import functools
import math

import jax
import jax.numpy as jnp
import numpy as np
from jax import lax
from jax.experimental import pallas as pl
from jax.experimental.pallas import tpu as pltpu
from jax.sharding import PartitionSpec as P

NSHELL = 64
NANG = 256
LIST = 2
LANES = 128
ROWS = 16
MESH = pl.DeviceIdType.MESH
HIGHEST = lax.Precision.HIGHEST
VMEM_LIMIT = 56 * 1024 * 1024


def angular_tables(points):
    positions = np.arange(points)
    angles = (positions[:, None] * positions[None, :] % points).astype(np.float64) * (
        2.0 * math.pi / points
    )
    cosine = np.cos(angles) / math.sqrt(points)
    sine_part = np.sin(angles) / math.sqrt(points)
    upper_half = np.concatenate([cosine, -sine_part], axis=1)
    lower_half = np.concatenate([sine_part, cosine], axis=1)
    return np.concatenate([upper_half, lower_half], axis=0).astype(np.float32)


def score_kernel(cls_ref, xh_ref, rh_ref, sw_ref, rr_ref, bias_ref, scores_ref, stats_ref, cross):
    step = pl.program_id(0)
    block = bias_ref.shape[0] // LIST
    classes = rh_ref.shape[0]

    @pl.when(step == 0)
    def _():
        cross[...] = jnp.zeros_like(cross)

    def entry(i, carry):
        p = i // LIST
        row = (i % LIST) * block + step * ROWS + p
        k = cls_ref[row]

        @pl.when((k >= 0) & (k < classes))
        def _():
            x_re = xh_ref[p, :, :NANG].astype(jnp.float32)
            x_im = xh_ref[p, :, NANG:].astype(jnp.float32)
            c_re = rh_ref[k, :, :NANG].astype(jnp.float32)
            c_im = rh_ref[k, :, NANG:].astype(jnp.float32)
            sw = sw_ref[...]
            cross[pl.ds(row, 1), :NANG] = jnp.sum(
                (x_re * c_re + x_im * c_im) * sw, axis=0, keepdims=True
            )
            cross[pl.ds(row, 1), NANG:] = jnp.sum(
                (x_im * c_re - x_re * c_im) * sw, axis=0, keepdims=True
            )

        return carry

    lax.fori_loop(0, ROWS * LIST, entry, 0)

    @pl.when(step == pl.num_programs(0) - 1)
    def _():
        scores = (
            lax.dot_general(
                cross[...],
                rr_ref[...],
                (((1,), (1,)), ((), ())),
                precision=HIGHEST,
                preferred_element_type=jnp.float32,
            )
            + bias_ref[...]
        )
        scores_ref[...] = scores
        first, second = scores[:block], scores[block:]
        top = jnp.max(jnp.maximum(first, second), axis=1, keepdims=True)
        total = jnp.sum(jnp.exp(first - top) + jnp.exp(second - top), axis=1, keepdims=True)
        lane = lax.broadcasted_iota(jnp.int32, (block, LANES), 1)
        stats = jnp.where(lane == 0, top, total)
        stats_ref[...] = jnp.transpose(stats)[:8]


def grad_kernel(
    cls_ref, xh_ref, rh_ref, scores_ref, stats_ref, ct_ref,
    part_ref, weight_ref, evid_ref, acc, coef, post_sum, volume,
):
    step = pl.program_id(0)
    block = scores_ref.shape[0] // LIST
    classes = rh_ref.shape[0]

    @pl.when(step == 0)
    def _():
        stats = stats_ref[...]
        tops = stats[:, 0:1, :]
        top = jnp.max(tops, axis=0)
        total = jnp.sum(stats[:, 1:2, :] * jnp.exp(tops - top[None]), axis=0)
        evid_ref[...] = top + jnp.log(total)
        top_col = jnp.transpose(jnp.broadcast_to(top, (LANES, block)))
        total_col = jnp.transpose(jnp.broadcast_to(total, (LANES, block)))
        for a in range(LIST):
            rows = slice(a * block, (a + 1) * block)
            posterior = jnp.exp(scores_ref[rows] - top_col) / total_col
            post_sum[rows] = jnp.broadcast_to(
                jnp.sum(posterior, axis=1, keepdims=True), (block, LANES)
            )
            coef[rows] = jnp.dot(
                posterior, ct_ref[...], precision=HIGHEST, preferred_element_type=jnp.float32
            )
        volume[...] = jnp.zeros_like(volume)
        weight_ref[...] = jnp.zeros_like(weight_ref)

        def clear(k, carry):
            acc[k] = jnp.zeros(acc.shape[1:], jnp.float32)
            return carry

        lax.fori_loop(0, classes, clear, 0)

    def entry(i, carry):
        p = i // LIST
        row = (i % LIST) * block + step * ROWS + p
        k = cls_ref[row]

        @pl.when((k >= 0) & (k < classes))
        def _():
            x_re = xh_ref[p, :, :NANG].astype(jnp.float32)
            x_im = xh_ref[p, :, NANG:].astype(jnp.float32)
            re = coef[pl.ds(row, 1), :NANG]
            im = coef[pl.ds(row, 1), NANG : 2 * NANG]
            acc[k, :, :NANG] += x_re * re - x_im * im
            acc[k, :, NANG:] += x_re * im + x_im * re
            volume[pl.ds(k, 1), :] += coef[pl.ds(row, 1), 2 * NANG :]
            weight_ref[pl.ds(k, 1), :] += post_sum[pl.ds(row, 1), :]

        return carry

    lax.fori_loop(0, ROWS * LIST, entry, 0)

    @pl.when(step == pl.num_programs(0) - 1)
    def _():
        def finish(k, carry):
            vol = volume[pl.ds(k, 1), :]
            for half in (slice(0, NANG), slice(NANG, 2 * NANG)):
                part_ref[k, :, half] = (
                    acc[k, :, half] - vol * rh_ref[k, :, half].astype(jnp.float32)
                ).astype(jnp.bfloat16)
            return carry

        lax.fori_loop(0, classes, finish, 0)


def reduce_kernel(
    lines, groups, p_ref, out_ref, held, from_left, from_right,
    pair_send, pair_recv, right_send, right_recv, left_send, left_recv,
):
    me = lax.axis_index("dp")
    x = lax.rem(me, 2)
    z = lax.div(me, 2)
    partner = me + 1 - 2 * x
    has_left = z > 0
    has_right = z < lines - 1
    per_group = p_ref.shape[3]

    barrier = pltpu.get_barrier_semaphore()
    pl.semaphore_signal(barrier, inc=1, device_id={"dp": partner}, device_id_type=MESH)

    @pl.when(has_left)
    def _():
        pl.semaphore_signal(barrier, inc=1, device_id={"dp": me - 2}, device_id_type=MESH)

    @pl.when(has_right)
    def _():
        pl.semaphore_signal(barrier, inc=1, device_id={"dp": me + 2}, device_id_type=MESH)

    peers = 1 + has_left.astype(jnp.int32) + has_right.astype(jnp.int32)
    pl.semaphore_wait(barrier, peers)

    def where_is(t):
        g, i = lax.div(t, lines), lax.rem(t, lines)
        odd, half = lax.rem(i, 2), lax.div(i, 2)
        return (1 - odd) * (lines - 1 - half) + odd * half, g

    def pair(b, g):
        return pltpu.make_async_remote_copy(
            src_ref=p_ref.at[b, 1 - x, g], dst_ref=held.at[b, g],
            send_sem=pair_send.at[b, g], recv_sem=pair_recv.at[b, g],
            device_id={"dp": partner}, device_id_type=MESH,
        )

    def right(b, g):
        return pltpu.make_async_remote_copy(
            src_ref=held.at[b, g], dst_ref=from_left.at[b, g],
            send_sem=right_send.at[b, g], recv_sem=right_recv.at[b, g],
            device_id={"dp": me + 2}, device_id_type=MESH,
        )

    def left(b, g):
        return pltpu.make_async_remote_copy(
            src_ref=held.at[b, g], dst_ref=from_right.at[b, g],
            send_sem=left_send.at[b, g], recv_sem=left_recv.at[b, g],
            device_id={"dp": me - 2}, device_id_type=MESH,
        )

    def add(b, g, other):
        def one(c, carry):
            held[b, g, c] = (
                held[b, g, c].astype(jnp.float32) + other(c).astype(jnp.float32)
            ).astype(jnp.bfloat16)
            return carry

        lax.fori_loop(0, per_group, one, 0)

    def begin(t, carry):
        pair(*where_is(t)).start()
        return carry

    def relay(t, carry):
        b, g = where_is(t)
        pair(b, g).wait_recv()
        add(b, g, lambda c: p_ref[b, x, g, c])

        @pl.when(z < b)
        def _():
            @pl.when(has_left)
            def _():
                right(b, g).wait_recv()
                add(b, g, lambda c: from_left[b, g, c])

            right(b, g).start()

        @pl.when(z > b)
        def _():
            @pl.when(has_right)
            def _():
                left(b, g).wait_recv()
                add(b, g, lambda c: from_right[b, g, c])

            left(b, g).start()

        return carry

    def finish(g, carry):
        def own(c, inner):
            out_ref[g, c] = held[z, g, c].astype(jnp.float32)
            return inner

        lax.fori_loop(0, per_group, own, 0)

        @pl.when(has_left)
        def _():
            right(z, g).wait_recv()

            def one(c, inner):
                out_ref[g, c] += from_left[z, g, c].astype(jnp.float32)
                return inner

            lax.fori_loop(0, per_group, one, 0)

        @pl.when(has_right)
        def _():
            left(z, g).wait_recv()

            def one(c, inner):
                out_ref[g, c] += from_right[z, g, c].astype(jnp.float32)
                return inner

            lax.fori_loop(0, per_group, one, 0)

        return carry

    def drain(t, carry):
        b, g = where_is(t)
        pair(b, g).wait_send()

        @pl.when(z < b)
        def _():
            right(b, g).wait_send()

        @pl.when(z > b)
        def _():
            left(b, g).wait_send()

        return carry

    lax.fori_loop(0, lines * groups, begin, 0)
    lax.fori_loop(0, lines * groups, relay, 0)
    lax.fori_loop(0, groups, finish, 0)
    lax.fori_loop(0, lines * groups, drain, 0)


def reduce_scatter(part, dp_count):
    classes = part.shape[0]
    lines = dp_count // 2
    owned = classes // dp_count
    groups = math.gcd(4, owned)
    shape = (owned // groups,) + part.shape[1:]
    whole = pltpu.VMEM((lines, groups) + shape, jnp.bfloat16)
    sems = pltpu.SemaphoreType.DMA((lines, groups))
    out = pl.pallas_call(
        functools.partial(reduce_kernel, lines, groups),
        out_shape=jax.ShapeDtypeStruct((groups,) + shape, jnp.float32),
        in_specs=[pl.BlockSpec(memory_space=pltpu.VMEM)],
        out_specs=pl.BlockSpec(memory_space=pltpu.VMEM),
        scratch_shapes=[whole, whole, whole] + [sems] * 6,
        compiler_params=pltpu.CompilerParams(
            collective_id=0, has_side_effects=True, vmem_limit_bytes=VMEM_LIMIT
        ),
        name="reduce_over_dp",
    )(part.reshape((lines, 2, groups) + shape))
    return out.reshape((owned,) + part.shape[1:])


def local(
    images, pose_slot, references, rotation_response, shell_weight, class_lists, class_counts
):
    dp_count = lax.axis_size("dp")
    here = lax.axis_index("dp")
    column = lax.axis_index("cls")
    block = images.shape[0]
    classes = references.shape[0]
    width = 2 * NANG
    entries = block * LIST
    full_table = angular_tables(NANG)
    forward = jnp.asarray(full_table.astype(jnp.bfloat16))
    inverse = jnp.asarray(np.ascontiguousarray(full_table.T))

    def transform(rows):
        out = jnp.dot(rows.reshape(-1, width), forward, preferred_element_type=jnp.float32)
        return out.astype(jnp.bfloat16).reshape(rows.shape)

    tags = jnp.concatenate([pose_slot[None, :], class_lists.T], axis=0)
    all_tags = lax.all_gather(tags, "dp", axis=1, tiled=True)
    image_hat = transform(images)
    ref_hat = transform(references)

    positions = jnp.arange(dp_count * block, dtype=jnp.int32)
    at_slot = pose_slot[:, None] == positions[None, :]
    own_lists = jnp.stack(
        [jnp.sum(jnp.where(at_slot, all_tags[1 + a][None, :], 0), axis=1) for a in range(LIST)]
    )
    local_class = (own_lists - column * classes).reshape(entries)
    log_prior = jnp.log1p(class_counts.astype(jnp.float32))
    picked = local_class[:, None] == jnp.arange(classes, dtype=jnp.int32)[None, :]
    prior = jnp.sum(jnp.where(picked, log_prior[None, :], 0.0), axis=1)
    inside = (local_class >= 0) & (local_class < classes)
    rotations = rotation_response.shape[0]
    lane = jnp.arange(LANES, dtype=jnp.int32)
    bias = jnp.where(inside[:, None] & (lane < rotations)[None, :], prior[:, None], -1e30)
    spread = jnp.broadcast_to(shell_weight[:, None], (NSHELL, NANG))
    rot_re = rotation_response[:, :NANG]
    rot_im = rotation_response[:, NANG:]
    pad = ((0, LANES - rotations), (0, 0))
    response = jnp.pad(rotation_response, pad)
    coef_table = jnp.pad(
        jnp.concatenate([rot_re, -rot_im, rot_re * rot_re + rot_im * rot_im], axis=1), pad
    )

    def whole(shape):
        return pl.BlockSpec(shape, lambda i, c: (0,) * len(shape))

    image_spec = pl.BlockSpec((ROWS, NSHELL, width), lambda i, c: (i, 0, 0))
    params = pltpu.CompilerParams(
        dimension_semantics=("arbitrary",), vmem_limit_bytes=VMEM_LIMIT
    )
    scores, stats = pl.pallas_call(
        score_kernel,
        grid_spec=pltpu.PrefetchScalarGridSpec(
            num_scalar_prefetch=1,
            grid=(block // ROWS,),
            in_specs=[
                image_spec,
                whole((classes, NSHELL, width)),
                whole((NSHELL, NANG)),
                whole((LANES, width)),
                whole((entries, LANES)),
            ],
            out_specs=[whole((entries, LANES)), whole((8, block))],
            scratch_shapes=[pltpu.VMEM((entries, width), jnp.float32)],
        ),
        out_shape=[
            jax.ShapeDtypeStruct((entries, LANES), jnp.float32),
            jax.ShapeDtypeStruct((8, block), jnp.float32),
        ],
        compiler_params=params,
        name="scores",
    )(local_class, image_hat, ref_hat, spread, response, bias)
    all_stats = lax.all_gather(stats, "cls")
    columns = all_stats.shape[0]
    part, weight, evidence = pl.pallas_call(
        grad_kernel,
        grid_spec=pltpu.PrefetchScalarGridSpec(
            num_scalar_prefetch=1,
            grid=(block // ROWS,),
            in_specs=[
                image_spec,
                whole((classes, NSHELL, width)),
                whole((entries, LANES)),
                whole((columns, 8, block)),
                whole((LANES, 3 * NANG)),
            ],
            out_specs=[
                whole((classes, NSHELL, width)),
                whole((classes, LANES)),
                whole((1, block)),
            ],
            scratch_shapes=[
                pltpu.VMEM((classes, NSHELL, width), jnp.float32),
                pltpu.VMEM((entries, 3 * NANG), jnp.float32),
                pltpu.VMEM((entries, LANES), jnp.float32),
                pltpu.VMEM((classes, NANG), jnp.float32),
            ],
        ),
        out_shape=[
            jax.ShapeDtypeStruct((classes, NSHELL, width), jnp.bfloat16),
            jax.ShapeDtypeStruct((classes, LANES), jnp.float32),
            jax.ShapeDtypeStruct((1, block), jnp.float32),
        ],
        compiler_params=params,
        name="gradient",
    )(local_class, image_hat, ref_hat, scores, all_stats, coef_table)

    small = jnp.concatenate([evidence[0], weight[:, 0]])
    all_small = lax.all_gather(small, "dp")
    owned = classes // dp_count
    weights = jnp.sum(all_small[:, block:], axis=0)
    denom = 1.0 + lax.dynamic_slice_in_dim(weights, here * owned, owned, 0)
    mine = here * block + jnp.arange(block, dtype=jnp.int32)
    log_evidence = jnp.sum(
        jnp.where(
            all_tags[0][None, :] == mine[:, None], all_small[:, :block].reshape(1, -1), 0.0
        ),
        axis=1,
    )

    numer = reduce_scatter(part, dp_count)
    scaled = numer / denom[:, None, None]
    result = jnp.dot(scaled.reshape(-1, width), inverse, precision=HIGHEST)
    return (result.reshape((1,) + numer.shape), log_evidence)


def solution(mesh):
    return jax.shard_map(
        local,
        mesh=mesh,
        in_specs=(
            P("dp", None, None),
            P("dp"),
            P("cls", None, None),
            P(),
            P(),
            P("dp", None),
            P("cls"),
        ),
        out_specs=(P("cls", "dp", None, None), P("dp")),
        check_vma=False,
    )
```

```python
import functools
import math

import jax
import jax.numpy as jnp
import numpy as np
from jax import lax
from jax.experimental import pallas as pl
from jax.experimental.pallas import tpu as pltpu
from jax.sharding import PartitionSpec as P

NSHELL = 64
NANG = 256
LIST = 2
LANES = 128
ROWS = 16
MESH = pl.DeviceIdType.MESH
HIGHEST = lax.Precision.HIGHEST
VMEM_LIMIT = 56 * 1024 * 1024


def angular_tables(points):
    positions = np.arange(points)
    angles = (positions[:, None] * positions[None, :] % points).astype(np.float64) * (
        2.0 * math.pi / points
    )
    cosine = np.cos(angles) / math.sqrt(points)
    sine_part = np.sin(angles) / math.sqrt(points)
    upper_half = np.concatenate([cosine, -sine_part], axis=1)
    lower_half = np.concatenate([sine_part, cosine], axis=1)
    return np.concatenate([upper_half, lower_half], axis=0).astype(np.float32)


def everyone(axis):
    me, count = lax.axis_index(axis), lax.axis_size(axis)

    def peer(step):
        return lax.rem(me + step, count)

    return me, count, peer


def greet(axis):
    _, count, peer = everyone(axis)
    barrier = pltpu.get_barrier_semaphore()

    def one(step, carry):
        pl.semaphore_signal(barrier, inc=1, device_id={axis: peer(step)}, device_id_type=MESH)
        return carry

    lax.fori_loop(1, count, one, 0)


def greeted(axis):
    pl.semaphore_wait(pltpu.get_barrier_semaphore(), lax.axis_size(axis) - 1)


def share(axis, src, dst, send, recv):
    me, count, peer = everyone(axis)

    def outgoing(step):
        return pltpu.make_async_remote_copy(
            src_ref=src(peer(step)), dst_ref=dst.at[me],
            send_sem=send.at[peer(step)], recv_sem=recv.at[me],
            device_id={axis: peer(step)}, device_id_type=MESH,
        )

    def incoming(step):
        return pltpu.make_async_remote_copy(
            src_ref=src(peer(step)), dst_ref=dst.at[peer(step)],
            send_sem=send.at[peer(step)], recv_sem=recv.at[peer(step)],
            device_id={axis: peer(step)}, device_id_type=MESH,
        )

    def loop(act):
        def one(step, carry):
            act(step)
            return carry

        lax.fori_loop(1, count, one, 0)

    return (
        lambda: loop(lambda step: outgoing(step).start()),
        lambda: loop(lambda step: incoming(step).wait_recv()),
        lambda: loop(lambda step: outgoing(step).wait_send()),
    )


def transform_kernel(
    image_steps, classes, image_ref, refs_ref, table_ref, tags_ref,
    image_out, refs_out, ids_out, slots_out, all_tags, send, recv,
):
    step = pl.program_id(0)
    start, arrive, sent = share("dp", lambda _: tags_ref, all_tags, send, recv)
    me = lax.axis_index("dp")
    count = lax.axis_size("dp")
    block = tags_ref.shape[1]

    @pl.when(step == 0)
    def _():
        greet("dp")

    @pl.when(step == image_steps // 2)
    def _():
        greeted("dp")
        start()

    def multiply(source, target):
        def one(i, carry):
            some = pl.ds(i * 4, 4)
            out = jnp.dot(
                source[some].reshape(4 * NSHELL, 2 * NANG),
                table_ref[...],
                preferred_element_type=jnp.float32,
            )
            target[some] = out.astype(jnp.bfloat16).reshape(4, NSHELL, 2 * NANG)
            return carry

        lax.fori_loop(0, ROWS // 4, one, 0)

    @pl.when(step < image_steps)
    def _():
        multiply(image_ref, image_out)

    @pl.when(step >= image_steps)
    def _():
        multiply(refs_ref, refs_out)

    @pl.when(step == pl.num_programs(0) - 1)
    def _():
        arrive()
        all_tags[me] = tags_ref[...]
        own = tags_ref[0:1, :].astype(jnp.float32)
        slot = jnp.transpose(jnp.broadcast_to(own, (LANES, block))).astype(jnp.int32)
        lane = lax.broadcasted_iota(jnp.int32, (block, block), 1)

        def look(d, found):
            rows = all_tags[d]
            hit = slot == lane + d * block
            slots_out[pl.ds(d, 1), :] = rows[0:1]
            return tuple(
                total + jnp.where(hit, rows[1 + a : 2 + a], 0) for a, total in enumerate(found)
            )

        found = lax.fori_loop(
            0, count, look, (jnp.zeros((block, block), jnp.int32),) * LIST
        )
        column = lax.axis_index("cls")
        ids_out[...] = jnp.zeros_like(ids_out)
        for a in range(LIST):
            total = jnp.sum(found[a].astype(jnp.float32), axis=1, keepdims=True)
            row = jnp.transpose(jnp.broadcast_to(total, (block, LANES)))[0:1]
            ids_out[a : a + 1, :] = row.astype(jnp.int32) - column * classes
        sent()


def listed(ids_ref, chosen, step, classes):
    count = jnp.int32(0)
    for i in range(ROWS * LIST):
        k = ids_ref[i % LIST, step * ROWS + i // LIST]
        chosen[count] = i
        count = count + jnp.where((k >= 0) & (k < classes), 1, 0)
    return count


def score_kernel(
    ids_ref, xh_ref, rh_ref, sw_ref, rr_ref, prior_ref,
    scores_ref, stats_ref, cross, bias, response, chosen,
):
    step = pl.program_id(0)
    block = ids_ref.shape[1]
    classes = rh_ref.shape[0]
    rotations = rr_ref.shape[0]

    @pl.when(step == 0)
    def _():
        cross[...] = jnp.zeros_like(cross)
        bias[...] = jnp.full_like(bias, -1e30)
        response[...] = jnp.zeros_like(response)
        response[:rotations] = rr_ref[...]

    def entry(n, carry):
        i = chosen[n]
        p = lax.div(i, LIST)
        a = lax.rem(i, LIST)
        row = a * block + step * ROWS + p
        k = ids_ref[a, step * ROWS + p]
        bias[pl.ds(row, 1), :] = prior_ref[pl.ds(k, 1), :]
        re = jnp.zeros((8, NANG), jnp.float32)
        im = jnp.zeros((8, NANG), jnp.float32)
        for j in range(0, NSHELL, ROWS):
            x = xh_ref[p, j : j + ROWS].astype(jnp.float32)
            c = rh_ref[k, j : j + ROWS].astype(jnp.float32)
            sw = sw_ref[j : j + ROWS]
            x_re, x_im, c_re, c_im = x[:, :NANG], x[:, NANG:], c[:, :NANG], c[:, NANG:]
            one = (x_re * c_re + x_im * c_im) * sw
            two = (x_im * c_re - x_re * c_im) * sw
            re = re + one[:8] + one[8:]
            im = im + two[:8] + two[8:]
        cross[pl.ds(row, 1), :NANG] = jnp.sum(re, axis=0, keepdims=True)
        cross[pl.ds(row, 1), NANG:] = jnp.sum(im, axis=0, keepdims=True)
        return carry

    lax.fori_loop(0, listed(ids_ref, chosen, step, classes), entry, 0)

    @pl.when(step == pl.num_programs(0) - 1)
    def _():
        lane = lax.broadcasted_iota(jnp.int32, (block, LANES), 1)
        scores = lax.dot_general(
            cross[...],
            response[...],
            (((1,), (1,)), ((), ())),
            precision=HIGHEST,
            preferred_element_type=jnp.float32,
        ) + bias[...]
        first = jnp.where(lane < rotations, scores[:block], -1e30)
        second = jnp.where(lane < rotations, scores[block:], -1e30)
        scores_ref[:block] = first
        scores_ref[block:] = second
        top = jnp.max(jnp.maximum(first, second), axis=1, keepdims=True)
        total = jnp.sum(jnp.exp(first - top) + jnp.exp(second - top), axis=1, keepdims=True)
        stats = jnp.where(lane == 0, top, total)
        stats_ref[...] = jnp.transpose(stats)[:8]


def posterior_kernel(
    scores_ref, stats_ref, rr_ref, coef_ref, post_ref, evid_ref, all_stats, table, send, recv
):
    start, arrive, sent = share("cls", lambda _: stats_ref, all_stats, send, recv)
    block = scores_ref.shape[0] // LIST
    rotations = rr_ref.shape[0]
    greet("cls")
    table[...] = jnp.zeros_like(table)
    rot_re = rr_ref[:, :NANG]
    rot_im = rr_ref[:, NANG:]
    table[:rotations, :NANG] = rot_re
    table[:rotations, NANG : 2 * NANG] = -rot_im
    table[:rotations, 2 * NANG :] = rot_re * rot_re + rot_im * rot_im
    greeted("cls")
    start()
    all_stats[lax.axis_index("cls")] = stats_ref[...]
    arrive()
    stats = all_stats[...]
    tops = stats[:, 0:1, :]
    top = jnp.max(tops, axis=0)
    total = jnp.sum(stats[:, 1:2, :] * jnp.exp(tops - top[None]), axis=0)
    evid_ref[...] = top + jnp.log(total)
    top_col = jnp.transpose(jnp.broadcast_to(top, (LANES, block)))
    total_col = jnp.transpose(jnp.broadcast_to(total, (LANES, block)))
    for a in range(LIST):
        rows = slice(a * block, (a + 1) * block)
        posterior = jnp.exp(scores_ref[rows] - top_col) / total_col
        post_ref[rows] = jnp.broadcast_to(
            jnp.sum(posterior, axis=1, keepdims=True), (block, LANES)
        )
        coef_ref[rows] = jnp.dot(
            posterior, table[...], precision=HIGHEST, preferred_element_type=jnp.float32
        )
    sent()


def grad_kernel(
    ids_ref, xh_ref, rh_ref, coef, post_sum, part_ref, weight_ref, acc, volume, chosen
):
    step = pl.program_id(0)
    block = ids_ref.shape[1]
    classes = rh_ref.shape[0]

    @pl.when(step == 0)
    def _():
        volume[...] = jnp.zeros_like(volume)
        weight_ref[...] = jnp.zeros_like(weight_ref)

        def clear(k, carry):
            acc[k] = jnp.zeros(acc.shape[1:], jnp.float32)
            return carry

        lax.fori_loop(0, classes, clear, 0)

    def entry(n, carry):
        i = chosen[n]
        p = lax.div(i, LIST)
        a = lax.rem(i, LIST)
        row = a * block + step * ROWS + p
        k = ids_ref[a, step * ROWS + p]
        re = coef[pl.ds(row, 1), :NANG]
        im = coef[pl.ds(row, 1), NANG : 2 * NANG]
        for j in range(0, NSHELL, ROWS):
            x = xh_ref[p, j : j + ROWS].astype(jnp.float32)
            x_re, x_im = x[:, :NANG], x[:, NANG:]
            acc[k, j : j + ROWS, :NANG] += x_re * re - x_im * im
            acc[k, j : j + ROWS, NANG:] += x_re * im + x_im * re
        volume[pl.ds(k, 1), :] += coef[pl.ds(row, 1), 2 * NANG :]
        weight_ref[pl.ds(k, 1), :] += post_sum[pl.ds(row, 1), :]
        return carry

    lax.fori_loop(0, listed(ids_ref, chosen, step, classes), entry, 0)

    @pl.when(step == pl.num_programs(0) - 1)
    def _():
        def finish(k, carry):
            vol = volume[pl.ds(k, 1), :]
            for j in range(0, NSHELL, ROWS):
                for half in (slice(0, NANG), slice(NANG, 2 * NANG)):
                    part_ref[k, j : j + ROWS, half] = (
                        acc[k, j : j + ROWS, half]
                        - vol * rh_ref[k, j : j + ROWS, half].astype(jnp.float32)
                    ).astype(jnp.bfloat16)
            return carry

        lax.fori_loop(0, classes, finish, 0)


def reduce_kernel(
    lines, groups, p_ref, weight_ref, evid_ref, slots_ref, out_ref, log_ref,
    held, from_left, from_right, weights, evids,
    pair_send, pair_recv, right_send, right_recv, left_send, left_recv,
    weight_send, weight_recv, evid_send, evid_recv,
):
    me = lax.axis_index("dp")
    x = lax.rem(me, 2)
    z = lax.div(me, 2)
    partner = me + 1 - 2 * x
    has_left = z > 0
    has_right = z < lines - 1
    per_group = p_ref.shape[3]

    weight_start, weight_arrive, weight_sent = share(
        "dp", lambda d: weight_ref.at[d], weights, weight_send, weight_recv
    )
    evid_start, evid_arrive, evid_sent = share(
        "dp", lambda _: evid_ref, evids, evid_send, evid_recv
    )
    greet("dp")
    greeted("dp")

    def where_is(t):
        g, i = lax.div(t, lines), lax.rem(t, lines)
        odd, half = lax.rem(i, 2), lax.div(i, 2)
        return (1 - odd) * (lines - 1 - half) + odd * half, g

    def pair(b, g):
        return pltpu.make_async_remote_copy(
            src_ref=p_ref.at[b, 1 - x, g], dst_ref=held.at[b, g],
            send_sem=pair_send.at[b, g], recv_sem=pair_recv.at[b, g],
            device_id={"dp": partner}, device_id_type=MESH,
        )

    def right(b, g):
        return pltpu.make_async_remote_copy(
            src_ref=held.at[b, g], dst_ref=from_left.at[b, g],
            send_sem=right_send.at[b, g], recv_sem=right_recv.at[b, g],
            device_id={"dp": me + 2}, device_id_type=MESH,
        )

    def left(b, g):
        return pltpu.make_async_remote_copy(
            src_ref=held.at[b, g], dst_ref=from_right.at[b, g],
            send_sem=left_send.at[b, g], recv_sem=left_recv.at[b, g],
            device_id={"dp": me - 2}, device_id_type=MESH,
        )

    def add(b, g, other):
        def one(c, carry):
            held[b, g, c] = (
                held[b, g, c].astype(jnp.float32) + other(c).astype(jnp.float32)
            ).astype(jnp.bfloat16)
            return carry

        lax.fori_loop(0, per_group, one, 0)

    def begin(t, carry):
        pair(*where_is(t)).start()
        return carry

    def relay(t, carry):
        b, g = where_is(t)
        pair(b, g).wait_recv()
        add(b, g, lambda c: p_ref[b, x, g, c])

        @pl.when(z < b)
        def _():
            @pl.when(has_left)
            def _():
                right(b, g).wait_recv()
                add(b, g, lambda c: from_left[b, g, c])

            right(b, g).start()

        @pl.when(z > b)
        def _():
            @pl.when(has_right)
            def _():
                left(b, g).wait_recv()
                add(b, g, lambda c: from_right[b, g, c])

            left(b, g).start()

        return carry

    def finish(g, carry):
        @pl.when(has_left)
        def _():
            right(z, g).wait_recv()

        @pl.when(has_right)
        def _():
            left(z, g).wait_recv()

        def own(c, inner):
            out_ref[g, c] = held[z, g, c].astype(jnp.float32)

            @pl.when(has_left)
            def _():
                out_ref[g, c] += from_left[z, g, c].astype(jnp.float32)

            @pl.when(has_right)
            def _():
                out_ref[g, c] += from_right[z, g, c].astype(jnp.float32)

            return inner

        lax.fori_loop(0, per_group, own, 0)
        return carry

    def small():
        count = weights.shape[0]
        weight_arrive()
        evid_arrive()
        weights[me] = weight_ref[me]
        evids[me] = evid_ref[...]
        block = evid_ref.shape[1]
        mine = me * block + lax.broadcasted_iota(jnp.int32, (block, block), 0)

        def look(d, total):
            return total + jnp.where(slots_ref[pl.ds(d, 1), :] == mine, evids[d], 0.0)

        found = lax.fori_loop(0, count, look, jnp.zeros((block, block), jnp.float32))
        summed = jnp.sum(found, axis=1, keepdims=True)
        log_ref[...] = jnp.transpose(jnp.broadcast_to(summed, (block, LANES)))[0:1]
        denom = 1.0 + jnp.sum(weights[...], axis=0)
        for n in range(weights.shape[1]):
            g, c = n // per_group, n % per_group
            row = denom[n : n + 1, :]
            out_ref[g, c] = out_ref[g, c] / jnp.concatenate([row] * (2 * NANG // LANES), axis=1)
        weight_sent()
        evid_sent()

    def drain(t, carry):
        b, g = where_is(t)
        pair(b, g).wait_send()

        @pl.when(z < b)
        def _():
            right(b, g).wait_send()

        @pl.when(z > b)
        def _():
            left(b, g).wait_send()

        return carry

    lax.fori_loop(0, lines * groups, begin, 0)
    weight_start()
    evid_start()
    lax.fori_loop(0, lines * groups, relay, 0)
    lax.fori_loop(0, groups, finish, 0)
    small()
    lax.fori_loop(0, lines * groups, drain, 0)


def vmem():
    return pl.BlockSpec(memory_space=pltpu.VMEM)


def remote(collective_id):
    return pltpu.CompilerParams(
        collective_id=collective_id, has_side_effects=True, vmem_limit_bytes=VMEM_LIMIT
    )


def reduce_scatter(part, weight, evidence, slots, dp_count):
    classes = part.shape[0]
    block = evidence.shape[1]
    lines = dp_count // 2
    owned = classes // dp_count
    groups = math.gcd(4, owned)
    shape = (owned // groups,) + part.shape[1:]
    whole = pltpu.VMEM((lines, groups) + shape, jnp.bfloat16)
    sems = pltpu.SemaphoreType.DMA((lines, groups))
    row_sems = pltpu.SemaphoreType.DMA((dp_count,))
    out, log_evidence = pl.pallas_call(
        functools.partial(reduce_kernel, lines, groups),
        out_shape=[
            jax.ShapeDtypeStruct((groups,) + shape, jnp.float32),
            jax.ShapeDtypeStruct((1, block), jnp.float32),
        ],
        in_specs=[vmem()] * 4,
        out_specs=[vmem()] * 2,
        scratch_shapes=[
            whole, whole, whole,
            pltpu.VMEM((dp_count, owned, LANES), jnp.float32),
            pltpu.VMEM((dp_count, 1, block), jnp.float32),
        ]
        + [sems] * 6
        + [row_sems] * 4,
        compiler_params=remote(2),
        name="reduce_over_dp",
    )(
        part.reshape((lines, 2, groups) + shape),
        weight.reshape(dp_count, owned, LANES),
        evidence,
        slots,
    )
    return out.reshape((owned,) + part.shape[1:]), log_evidence[0]


def local(
    images, pose_slot, references, rotation_response, shell_weight, class_lists, class_counts
):
    dp_count = lax.axis_size("dp")
    columns = lax.axis_size("cls")
    block = images.shape[0]
    classes = references.shape[0]
    width = 2 * NANG
    entries = block * LIST
    rotations = rotation_response.shape[0]
    full_table = angular_tables(NANG)
    forward = jnp.asarray(full_table.astype(jnp.bfloat16))
    inverse = jnp.asarray(np.ascontiguousarray(full_table.T))
    tags = jnp.concatenate(
        [pose_slot[None, :], class_lists.T, jnp.zeros((7 - LIST, block), jnp.int32)], axis=0
    )
    prior = jnp.broadcast_to(
        jnp.log1p(class_counts.astype(jnp.float32))[:, None], (classes, LANES)
    )
    spread = jnp.broadcast_to(shell_weight[:, None], (NSHELL, NANG))

    image_steps = block // ROWS
    ref_steps = classes // ROWS
    cube = (ROWS, NSHELL, width)

    def fixed(shape):
        return pl.BlockSpec(shape, lambda i: (0,) * len(shape))

    def image_block():
        return pl.BlockSpec(cube, lambda i: (jnp.minimum(i, image_steps - 1), 0, 0))

    def ref_block():
        return pl.BlockSpec(cube, lambda i: (jnp.maximum(i - image_steps, 0), 0, 0))

    image_hat, ref_hat, ids, slots = pl.pallas_call(
        functools.partial(transform_kernel, image_steps, classes),
        grid=(image_steps + ref_steps,),
        in_specs=[image_block(), ref_block(), fixed((width, width)), fixed((8, block))],
        out_specs=[image_block(), ref_block(), fixed((8, block)), fixed((dp_count, block))],
        out_shape=[
            jax.ShapeDtypeStruct(images.shape, jnp.bfloat16),
            jax.ShapeDtypeStruct(references.shape, jnp.bfloat16),
            jax.ShapeDtypeStruct((8, block), jnp.int32),
            jax.ShapeDtypeStruct((dp_count, block), jnp.int32),
        ],
        scratch_shapes=[
            pltpu.VMEM((dp_count, 8, block), jnp.int32),
            pltpu.SemaphoreType.DMA((dp_count,)),
            pltpu.SemaphoreType.DMA((dp_count,)),
        ],
        compiler_params=remote(0),
        name="transform",
    )(images, references, forward, tags)

    def whole(shape):
        return pl.BlockSpec(shape, lambda i, c: (0,) * len(shape))

    image_spec = pl.BlockSpec(cube, lambda i, c: (i, 0, 0))
    params = pltpu.CompilerParams(
        dimension_semantics=("arbitrary",), vmem_limit_bytes=VMEM_LIMIT
    )
    chosen = pltpu.SMEM((ROWS * LIST + 1,), jnp.int32)
    scores, stats = pl.pallas_call(
        score_kernel,
        grid_spec=pltpu.PrefetchScalarGridSpec(
            num_scalar_prefetch=1,
            grid=(image_steps,),
            in_specs=[
                image_spec,
                whole((classes, NSHELL, width)),
                whole((NSHELL, NANG)),
                whole((rotations, width)),
                whole((classes, LANES)),
            ],
            out_specs=[whole((entries, LANES)), whole((8, block))],
            scratch_shapes=[
                pltpu.VMEM((entries, width), jnp.float32),
                pltpu.VMEM((entries, LANES), jnp.float32),
                pltpu.VMEM((LANES, width), jnp.float32),
                chosen,
            ],
        ),
        out_shape=[
            jax.ShapeDtypeStruct((entries, LANES), jnp.float32),
            jax.ShapeDtypeStruct((8, block), jnp.float32),
        ],
        compiler_params=params,
        name="scores",
    )(ids, image_hat, ref_hat, spread, rotation_response, prior)

    coef, post_sum, evidence = pl.pallas_call(
        posterior_kernel,
        in_specs=[vmem()] * 3,
        out_specs=[vmem()] * 3,
        out_shape=[
            jax.ShapeDtypeStruct((entries, 3 * NANG), jnp.float32),
            jax.ShapeDtypeStruct((entries, LANES), jnp.float32),
            jax.ShapeDtypeStruct((1, block), jnp.float32),
        ],
        scratch_shapes=[
            pltpu.VMEM((columns, 8, block), jnp.float32),
            pltpu.VMEM((LANES, 3 * NANG), jnp.float32),
            pltpu.SemaphoreType.DMA((columns,)),
            pltpu.SemaphoreType.DMA((columns,)),
        ],
        compiler_params=remote(1),
        name="posterior",
    )(scores, stats, rotation_response)

    part, weight = pl.pallas_call(
        grad_kernel,
        grid_spec=pltpu.PrefetchScalarGridSpec(
            num_scalar_prefetch=1,
            grid=(image_steps,),
            in_specs=[
                image_spec,
                whole((classes, NSHELL, width)),
                whole((entries, 3 * NANG)),
                whole((entries, LANES)),
            ],
            out_specs=[whole((classes, NSHELL, width)), whole((classes, LANES))],
            scratch_shapes=[
                pltpu.VMEM((classes, NSHELL, width), jnp.float32),
                pltpu.VMEM((classes, NANG), jnp.float32),
                chosen,
            ],
        ),
        out_shape=[
            jax.ShapeDtypeStruct((classes, NSHELL, width), jnp.bfloat16),
            jax.ShapeDtypeStruct((classes, LANES), jnp.float32),
        ],
        compiler_params=params,
        name="gradient",
    )(ids, image_hat, ref_hat, coef, post_sum)

    scaled, log_evidence = reduce_scatter(part, weight, evidence, slots, dp_count)
    result = jnp.dot(scaled.reshape(-1, width), inverse, precision=HIGHEST)
    return (result.reshape((1,) + scaled.shape), log_evidence)


def solution(mesh):
    return jax.shard_map(
        local,
        mesh=mesh,
        in_specs=(
            P("dp", None, None),
            P("dp"),
            P("cls", None, None),
            P(),
            P(),
            P("dp", None),
            P("cls"),
        ),
        out_specs=(P("cls", "dp", None, None), P("dp")),
        check_vma=False,
    )
```

```python
import functools
import math

import jax
import jax.numpy as jnp
import numpy as np
from jax import lax
from jax.experimental import pallas as pl
from jax.experimental.pallas import tpu as pltpu
from jax.sharding import PartitionSpec as P

NSHELL = 64
NANG = 256
LIST = 2
LANES = 128
ROWS = 16
MESH = pl.DeviceIdType.MESH
HIGHEST = lax.Precision.HIGHEST
VMEM_LIMIT = 56 * 1024 * 1024
WINDOW = 4


def angular_tables(points):
    positions = np.arange(points)
    angles = (positions[:, None] * positions[None, :] % points).astype(np.float64) * (
        2.0 * math.pi / points
    )
    cosine = np.cos(angles) / math.sqrt(points)
    sine_part = np.sin(angles) / math.sqrt(points)
    upper_half = np.concatenate([cosine, -sine_part], axis=1)
    lower_half = np.concatenate([sine_part, cosine], axis=1)
    return np.concatenate([upper_half, lower_half], axis=0).astype(np.float32)


def everyone(axis):
    me, count = lax.axis_index(axis), lax.axis_size(axis)

    def peer(step):
        return lax.rem(me + step, count)

    return me, count, peer


def greet(axis):
    _, count, peer = everyone(axis)
    barrier = pltpu.get_barrier_semaphore()

    def one(step, carry):
        pl.semaphore_signal(barrier, inc=1, device_id={axis: peer(step)}, device_id_type=MESH)
        return carry

    lax.fori_loop(1, count, one, 0)


def greeted(axis):
    pl.semaphore_wait(pltpu.get_barrier_semaphore(), lax.axis_size(axis) - 1)


def share(axis, src, dst, send, recv):
    me, count, peer = everyone(axis)

    def outgoing(step):
        return pltpu.make_async_remote_copy(
            src_ref=src(peer(step)), dst_ref=dst.at[me],
            send_sem=send.at[peer(step)], recv_sem=recv.at[me],
            device_id={axis: peer(step)}, device_id_type=MESH,
        )

    def incoming(step):
        return pltpu.make_async_remote_copy(
            src_ref=src(peer(step)), dst_ref=dst.at[peer(step)],
            send_sem=send.at[peer(step)], recv_sem=recv.at[peer(step)],
            device_id={axis: peer(step)}, device_id_type=MESH,
        )

    def loop(act):
        def one(step, carry):
            act(step)
            return carry

        lax.fori_loop(1, count, one, 0)

    return (
        lambda: loop(lambda step: outgoing(step).start()),
        lambda: loop(lambda step: incoming(step).wait_recv()),
        lambda: loop(lambda step: outgoing(step).wait_send()),
    )


def transform_kernel(
    image_steps, classes, image_ref, refs_ref, table_ref, slot_ref, lists_ref,
    image_out, refs_out, ids_out, slots_out, tags_ref, all_tags, send, recv,
):
    step = pl.program_id(0)
    start, arrive, sent = share("dp", lambda _: tags_ref, all_tags, send, recv)
    me = lax.axis_index("dp")
    count = lax.axis_size("dp")
    block = tags_ref.shape[1]

    @pl.when(step == 0)
    def _():
        greet("dp")
        tags_ref[...] = jnp.zeros_like(tags_ref)
        tags_ref[0:1, :] = slot_ref[...]
        for a in range(LIST):
            own = lists_ref[:, a : a + 1].astype(jnp.float32)
            row = jnp.transpose(jnp.broadcast_to(own, (block, LANES)))[0:1]
            tags_ref[1 + a : 2 + a, :] = row.astype(jnp.int32)

    @pl.when(step == image_steps // 2)
    def _():
        greeted("dp")
        start()

    def multiply(source, target):
        out = jnp.dot(
            source[...].reshape(ROWS * NSHELL, 2 * NANG),
            table_ref[...],
            preferred_element_type=jnp.float32,
        )
        target[...] = out.astype(jnp.bfloat16).reshape(ROWS, NSHELL, 2 * NANG)

    @pl.when(step < image_steps)
    def _():
        multiply(image_ref, image_out)

    @pl.when(step >= image_steps)
    def _():
        multiply(refs_ref, refs_out)

    @pl.when(step == pl.num_programs(0) - 1)
    def _():
        arrive()
        all_tags[me] = tags_ref[...]
        own = tags_ref[0:1, :].astype(jnp.float32)
        slot = jnp.transpose(jnp.broadcast_to(own, (LANES, block))).astype(jnp.int32)
        lane = lax.broadcasted_iota(jnp.int32, (block, block), 1)

        def look(d, found):
            rows = all_tags[d]
            hit = slot == lane + d * block
            slots_out[pl.ds(d, 1), :] = rows[0:1]
            return tuple(
                total + jnp.where(hit, rows[1 + a : 2 + a], 0) for a, total in enumerate(found)
            )

        found = lax.fori_loop(
            0, count, look, (jnp.zeros((block, block), jnp.int32),) * LIST
        )
        column = lax.axis_index("cls")
        ids_out[...] = jnp.zeros_like(ids_out)
        for a in range(LIST):
            total = jnp.sum(found[a].astype(jnp.float32), axis=1, keepdims=True)
            row = jnp.transpose(jnp.broadcast_to(total, (block, LANES)))[0:1]
            ids_out[a : a + 1, :] = row.astype(jnp.int32) - column * classes
        sent()


def listed(ids_ref, chosen, step, classes):
    count = jnp.int32(0)
    for i in range(ROWS * LIST):
        k = ids_ref[i % LIST, step * ROWS + i // LIST]
        chosen[count] = i
        count = count + jnp.where((k >= 0) & (k < classes), 1, 0)
    return count


def score_kernel(
    ids_ref, xh_ref, rh_ref, shells_ref, rr_ref, counts_ref,
    scores_ref, stats_ref, cross, bias, response, prior_ref, sw_ref, chosen,
):
    step = pl.program_id(0)
    block = ids_ref.shape[1]
    classes = rh_ref.shape[0]
    rotations = rr_ref.shape[0]

    @pl.when(step == 0)
    def _():
        cross[...] = jnp.zeros_like(cross)
        bias[...] = jnp.full_like(bias, -1e30)
        response[...] = jnp.zeros_like(response)
        response[:rotations] = rr_ref[...]
        row = jnp.log1p(counts_ref[...].astype(jnp.float32))
        prior_ref[...] = jnp.transpose(jnp.broadcast_to(row, (LANES, classes)))
        sw_ref[...] = jnp.transpose(jnp.broadcast_to(shells_ref[...], (NANG, NSHELL)))

    def entry(n, carry):
        i = chosen[n]
        p = lax.div(i, LIST)
        a = lax.rem(i, LIST)
        row = a * block + step * ROWS + p
        k = ids_ref[a, step * ROWS + p]
        bias[pl.ds(row, 1), :] = prior_ref[pl.ds(k, 1), :]
        re = jnp.zeros((8, NANG), jnp.float32)
        im = jnp.zeros((8, NANG), jnp.float32)
        for j in range(0, NSHELL, ROWS):
            x = xh_ref[p, j : j + ROWS].astype(jnp.float32)
            c = rh_ref[k, j : j + ROWS].astype(jnp.float32)
            sw = sw_ref[j : j + ROWS]
            x_re, x_im, c_re, c_im = x[:, :NANG], x[:, NANG:], c[:, :NANG], c[:, NANG:]
            one = (x_re * c_re + x_im * c_im) * sw
            two = (x_im * c_re - x_re * c_im) * sw
            re = re + one[:8] + one[8:]
            im = im + two[:8] + two[8:]
        cross[pl.ds(row, 1), :NANG] = jnp.sum(re, axis=0, keepdims=True)
        cross[pl.ds(row, 1), NANG:] = jnp.sum(im, axis=0, keepdims=True)
        return carry

    lax.fori_loop(0, listed(ids_ref, chosen, step, classes), entry, 0)

    @pl.when(step == pl.num_programs(0) - 1)
    def _():
        lane = lax.broadcasted_iota(jnp.int32, (block, LANES), 1)
        scores = lax.dot_general(
            cross[...],
            response[...],
            (((1,), (1,)), ((), ())),
            precision=HIGHEST,
            preferred_element_type=jnp.float32,
        ) + bias[...]
        first = jnp.where(lane < rotations, scores[:block], -1e30)
        second = jnp.where(lane < rotations, scores[block:], -1e30)
        scores_ref[:block] = first
        scores_ref[block:] = second
        top = jnp.max(jnp.maximum(first, second), axis=1, keepdims=True)
        total = jnp.sum(jnp.exp(first - top) + jnp.exp(second - top), axis=1, keepdims=True)
        stats = jnp.where(lane == 0, top, total)
        stats_ref[...] = jnp.transpose(stats)[:8]


def posterior_kernel(
    scores_ref, stats_ref, rr_ref, coef_ref, post_ref, evid_ref, all_stats, table, send, recv
):
    start, arrive, sent = share("cls", lambda _: stats_ref, all_stats, send, recv)
    block = scores_ref.shape[0] // LIST
    rotations = rr_ref.shape[0]
    greet("cls")
    table[...] = jnp.zeros_like(table)
    rot_re = rr_ref[:, :NANG]
    rot_im = rr_ref[:, NANG:]
    table[:rotations, :NANG] = rot_re
    table[:rotations, NANG : 2 * NANG] = -rot_im
    table[:rotations, 2 * NANG :] = rot_re * rot_re + rot_im * rot_im
    greeted("cls")
    start()
    all_stats[lax.axis_index("cls")] = stats_ref[...]
    arrive()
    stats = all_stats[...]
    tops = stats[:, 0:1, :]
    top = jnp.max(tops, axis=0)
    total = jnp.sum(stats[:, 1:2, :] * jnp.exp(tops - top[None]), axis=0)
    evid_ref[...] = top + jnp.log(total)
    top_col = jnp.transpose(jnp.broadcast_to(top, (LANES, block)))
    total_col = jnp.transpose(jnp.broadcast_to(total, (LANES, block)))
    for a in range(LIST):
        rows = slice(a * block, (a + 1) * block)
        posterior = jnp.exp(scores_ref[rows] - top_col) / total_col
        post_ref[rows] = jnp.broadcast_to(
            jnp.sum(posterior, axis=1, keepdims=True), (block, LANES)
        )
        coef_ref[rows] = jnp.dot(
            posterior, table[...], precision=HIGHEST, preferred_element_type=jnp.float32
        )
    sent()


def grad_kernel(
    ids_ref, images_ref, rh_ref, coef, post_sum, part_ref, weight_ref, xh_ref, head, nxt, sem
):
    step = pl.program_id(0)
    block = ids_ref.shape[1]
    per_step = rh_ref.shape[0]
    classes = per_step * pl.num_programs(0)
    fetch = pltpu.make_async_copy(images_ref, xh_ref, sem)

    @pl.when(step == 0)
    def _():
        fetch.start()

        def clear(k, carry):
            head[k] = -1
            return carry

        lax.fori_loop(0, classes + 1, clear, 0)

        def link(n, carry):
            for i in range(ROWS):
                for a in range(LIST):
                    p = n * ROWS + i
                    k = ids_ref[a, p]
                    slot = jnp.where((k >= 0) & (k < classes), k, classes)
                    nxt[a * block + p] = head[slot]
                    head[slot] = a * block + p
            return carry

        lax.fori_loop(0, block // ROWS, link, 0)
        fetch.wait()

    def one_class(c, carry):
        first = head[step * per_step + c]

        def more(state):
            return state[0] >= 0

        def tally(state):
            row, vol, weight = state
            return (
                nxt[row],
                vol + coef[pl.ds(row, 1), 2 * NANG :],
                weight + post_sum[pl.ds(row, 1), :],
            )

        _, vol, weight = lax.while_loop(
            more, tally, (first, jnp.zeros((1, NANG), jnp.float32), jnp.zeros((1, LANES), jnp.float32))
        )
        weight_ref[pl.ds(c, 1), :] = weight
        for j in range(0, NSHELL, 2 * ROWS):
            rows = slice(j, j + 2 * ROWS)

            def add(state):
                row, g_re, g_im = state
                p = lax.rem(row, block)
                re = coef[pl.ds(row, 1), :NANG]
                im = coef[pl.ds(row, 1), NANG : 2 * NANG]
                x_re = xh_ref[p, rows, :NANG].astype(jnp.float32)
                x_im = xh_ref[p, rows, NANG:].astype(jnp.float32)
                return (
                    nxt[row], g_re + (x_re * re - x_im * im), g_im + (x_re * im + x_im * re)
                )

            start = (
                first,
                -vol * rh_ref[c, rows, :NANG].astype(jnp.float32),
                -vol * rh_ref[c, rows, NANG:].astype(jnp.float32),
            )
            _, g_re, g_im = lax.while_loop(more, add, start)
            part_ref[c, rows, :NANG] = g_re.astype(jnp.bfloat16)
            part_ref[c, rows, NANG:] = g_im.astype(jnp.bfloat16)
        return carry

    lax.fori_loop(0, per_step, one_class, 0)


def reduce_kernel(
    lines, groups, p_ref, weight_ref, evid_ref, slots_ref, table_ref, out_ref, log_ref,
    held, own, from_left, from_right, weights, evids, scale,
    own_sem, pair_send, pair_recv, right_send, right_recv, left_send, left_recv,
    weight_send, weight_recv, evid_send, evid_recv,
):
    me = lax.axis_index("dp")
    x = lax.rem(me, 2)
    z = lax.div(me, 2)
    partner = me + 1 - 2 * x
    has_left = z > 0
    has_right = z < lines - 1
    chunks = lines * groups

    weight_start, weight_arrive, weight_sent = share(
        "dp", lambda d: weight_ref.at[d], weights, weight_send, weight_recv
    )
    evid_start, evid_arrive, evid_sent = share(
        "dp", lambda _: evid_ref, evids, evid_send, evid_recv
    )

    def where_is(t):
        g, i = lax.div(t, lines), lax.rem(t, lines)
        odd, half = lax.rem(i, 2), lax.div(i, 2)
        return (1 - odd) * (lines - 1 - half) + odd * half, g

    def keep(b, g):
        return pltpu.make_async_copy(p_ref.at[b, x, g], own.at[b, g], own_sem.at[b, g])

    def pair(b, g):
        return pltpu.make_async_remote_copy(
            src_ref=p_ref.at[b, 1 - x, g], dst_ref=held.at[b, g],
            send_sem=pair_send.at[b, g], recv_sem=pair_recv.at[b, g],
            device_id={"dp": partner}, device_id_type=MESH,
        )

    def right(b, g):
        return pltpu.make_async_remote_copy(
            src_ref=held.at[b, g], dst_ref=from_left.at[b, g],
            send_sem=right_send.at[b, g], recv_sem=right_recv.at[b, g],
            device_id={"dp": me + 2}, device_id_type=MESH,
        )

    def left(b, g):
        return pltpu.make_async_remote_copy(
            src_ref=held.at[b, g], dst_ref=from_right.at[b, g],
            send_sem=left_send.at[b, g], recv_sem=left_recv.at[b, g],
            device_id={"dp": me - 2}, device_id_type=MESH,
        )

    def add(b, g, other):
        held[b, g] = (
            held[b, g].astype(jnp.float32) + other[b, g].astype(jnp.float32)
        ).astype(jnp.bfloat16)

    def each(act):
        def one(t, carry):
            act(*where_is(t))
            return carry

        lax.fori_loop(0, chunks, one, 0)

    def relay(t):
        b, g = where_is(t)
        keep(b, g).wait()
        pair(b, g).wait_recv()

        @pl.when(t + WINDOW < chunks)
        def _():
            pair(*where_is(t + WINDOW)).start()

        add(b, g, own)

        @pl.when(z < b)
        def _():
            @pl.when(has_left)
            def _():
                right(b, g).wait_recv()
                add(b, g, from_left)

            right(b, g).start()

        @pl.when(z > b)
        def _():
            @pl.when(has_right)
            def _():
                left(b, g).wait_recv()
                add(b, g, from_right)

            left(b, g).start()

    def small():
        count = weights.shape[0]
        weight_arrive()
        evid_arrive()
        weights[me] = weight_ref[me]
        evids[me] = evid_ref[...]
        block = evid_ref.shape[1]
        mine = me * block + lax.broadcasted_iota(jnp.int32, (block, block), 0)

        def look(d, total):
            return total + jnp.where(slots_ref[pl.ds(d, 1), :] == mine, evids[d], 0.0)

        found = lax.fori_loop(0, count, look, jnp.zeros((block, block), jnp.float32))
        summed = jnp.sum(found, axis=1, keepdims=True)
        log_ref[...] = jnp.transpose(jnp.broadcast_to(summed, (block, LANES)))[0:1]
        inverse = 1.0 / (1.0 + jnp.sum(weights[...], axis=0))
        for n in range(2 * NANG // LANES):
            scale[:, n * LANES : (n + 1) * LANES] = inverse

    def finish(g):
        out_ref[g] = held[z, g].astype(jnp.float32)

        @pl.when(has_left)
        def _():
            right(z, g).wait_recv()
            out_ref[g] += from_left[z, g].astype(jnp.float32)

        @pl.when(has_right)
        def _():
            left(z, g).wait_recv()
            out_ref[g] += from_right[z, g].astype(jnp.float32)

        scaled = out_ref[g] * scale[pl.ds(g, 1), :]
        out_ref[g] = jnp.dot(
            scaled.astype(jnp.bfloat16), table_ref[...], preferred_element_type=jnp.float32
        )

    each(lambda b, g: keep(b, g).start())
    greet("dp")
    greeted("dp")

    def begin(t, carry):
        pair(*where_is(t)).start()
        return carry

    lax.fori_loop(0, min(WINDOW, chunks), begin, 0)
    weight_start()
    evid_start()

    def round_of(g, carry):
        def one(i, inner):
            relay(g * lines + i)
            return inner

        lax.fori_loop(0, lines, one, 0)

        @pl.when(g == 0)
        def _():
            small()

        @pl.when(g > 0)
        def _():
            finish(g - 1)

        return carry

    lax.fori_loop(0, groups, round_of, 0)
    finish(groups - 1)

    def drain(b, g):
        pair(b, g).wait_send()

        @pl.when(z < b)
        def _():
            right(b, g).wait_send()

        @pl.when(z > b)
        def _():
            left(b, g).wait_send()

    each(drain)
    weight_sent()
    evid_sent()


def vmem():
    return pl.BlockSpec(memory_space=pltpu.VMEM)


def remote(collective_id):
    return pltpu.CompilerParams(
        collective_id=collective_id, has_side_effects=True, vmem_limit_bytes=VMEM_LIMIT
    )


def reduce_scatter(part, weight, evidence, slots, table, dp_count):
    classes = part.shape[0]
    block = evidence.shape[1]
    lines = dp_count // 2
    owned = classes // dp_count
    shape = part.shape[1:]
    whole = pltpu.VMEM((lines, owned) + shape, jnp.bfloat16)
    sems = pltpu.SemaphoreType.DMA((lines, owned))
    row_sems = pltpu.SemaphoreType.DMA((dp_count,))
    out, log_evidence = pl.pallas_call(
        functools.partial(reduce_kernel, lines, owned),
        out_shape=[
            jax.ShapeDtypeStruct((owned,) + shape, jnp.float32),
            jax.ShapeDtypeStruct((1, block), jnp.float32),
        ],
        in_specs=[pl.BlockSpec(memory_space=pl.ANY)] + [vmem()] * 4,
        out_specs=[vmem()] * 2,
        scratch_shapes=[
            whole, whole, whole, whole,
            pltpu.VMEM((dp_count, owned, LANES), jnp.float32),
            pltpu.VMEM((dp_count, 1, block), jnp.float32),
            pltpu.VMEM((owned, 2 * NANG), jnp.float32),
        ]
        + [sems] * 7
        + [row_sems] * 4,
        compiler_params=remote(2),
        name="reduce_over_dp",
    )(
        part.reshape((lines, 2, owned) + shape),
        weight.reshape(dp_count, owned, LANES),
        evidence,
        slots,
        table,
    )
    return out, log_evidence[0]


def local(
    images, pose_slot, references, rotation_response, shell_weight, class_lists, class_counts
):
    dp_count = lax.axis_size("dp")
    columns = lax.axis_size("cls")
    block = images.shape[0]
    classes = references.shape[0]
    width = 2 * NANG
    entries = block * LIST
    rotations = rotation_response.shape[0]
    full_table = angular_tables(NANG)
    forward = jnp.asarray(full_table.astype(jnp.bfloat16))
    inverse = jnp.asarray(np.ascontiguousarray(full_table.T).astype(jnp.bfloat16))

    image_steps = block // ROWS
    ref_steps = classes // ROWS
    cube = (ROWS, NSHELL, width)

    def fixed(shape):
        return pl.BlockSpec(shape, lambda i: (0,) * len(shape))

    def image_block():
        return pl.BlockSpec(cube, lambda i: (jnp.minimum(i, image_steps - 1), 0, 0))

    def ref_block():
        return pl.BlockSpec(cube, lambda i: (jnp.maximum(i - image_steps, 0), 0, 0))

    image_hat, ref_hat, ids, slots = pl.pallas_call(
        functools.partial(transform_kernel, image_steps, classes),
        grid=(image_steps + ref_steps,),
        in_specs=[
            image_block(),
            ref_block(),
            fixed((width, width)),
            fixed((1, block)),
            fixed((block, LIST)),
        ],
        out_specs=[image_block(), ref_block(), fixed((8, block)), fixed((dp_count, block))],
        out_shape=[
            jax.ShapeDtypeStruct(images.shape, jnp.bfloat16),
            jax.ShapeDtypeStruct(references.shape, jnp.bfloat16),
            jax.ShapeDtypeStruct((8, block), jnp.int32),
            jax.ShapeDtypeStruct((dp_count, block), jnp.int32),
        ],
        scratch_shapes=[
            pltpu.VMEM((8, block), jnp.int32),
            pltpu.VMEM((dp_count, 8, block), jnp.int32),
            pltpu.SemaphoreType.DMA((dp_count,)),
            pltpu.SemaphoreType.DMA((dp_count,)),
        ],
        compiler_params=remote(0),
        name="transform",
    )(images, references, forward, pose_slot[None, :], class_lists)

    def whole(shape):
        return pl.BlockSpec(shape, lambda i, c: (0,) * len(shape))

    image_spec = pl.BlockSpec(cube, lambda i, c: (i, 0, 0))
    params = pltpu.CompilerParams(
        dimension_semantics=("arbitrary",), vmem_limit_bytes=VMEM_LIMIT
    )
    scores, stats = pl.pallas_call(
        score_kernel,
        grid_spec=pltpu.PrefetchScalarGridSpec(
            num_scalar_prefetch=1,
            grid=(image_steps,),
            in_specs=[
                image_spec,
                whole((classes, NSHELL, width)),
                whole((1, NSHELL)),
                whole((rotations, width)),
                whole((1, classes)),
            ],
            out_specs=[whole((entries, LANES)), whole((8, block))],
            scratch_shapes=[
                pltpu.VMEM((entries, width), jnp.float32),
                pltpu.VMEM((entries, LANES), jnp.float32),
                pltpu.VMEM((LANES, width), jnp.float32),
                pltpu.VMEM((classes, LANES), jnp.float32),
                pltpu.VMEM((NSHELL, NANG), jnp.float32),
                pltpu.SMEM((ROWS * LIST + 1,), jnp.int32),
            ],
        ),
        out_shape=[
            jax.ShapeDtypeStruct((entries, LANES), jnp.float32),
            jax.ShapeDtypeStruct((8, block), jnp.float32),
        ],
        compiler_params=params,
        name="scores",
    )(ids, image_hat, ref_hat, shell_weight[None, :], rotation_response, class_counts[None, :])

    coef, post_sum, evidence = pl.pallas_call(
        posterior_kernel,
        in_specs=[vmem()] * 3,
        out_specs=[vmem()] * 3,
        out_shape=[
            jax.ShapeDtypeStruct((entries, 3 * NANG), jnp.float32),
            jax.ShapeDtypeStruct((entries, LANES), jnp.float32),
            jax.ShapeDtypeStruct((1, block), jnp.float32),
        ],
        scratch_shapes=[
            pltpu.VMEM((columns, 8, block), jnp.float32),
            pltpu.VMEM((LANES, 3 * NANG), jnp.float32),
            pltpu.SemaphoreType.DMA((columns,)),
            pltpu.SemaphoreType.DMA((columns,)),
        ],
        compiler_params=remote(1),
        name="posterior",
    )(scores, stats, rotation_response)

    some = (8, NSHELL, width)
    part, weight = pl.pallas_call(
        grad_kernel,
        grid_spec=pltpu.PrefetchScalarGridSpec(
            num_scalar_prefetch=1,
            grid=(classes // 8,),
            in_specs=[
                pl.BlockSpec(memory_space=pl.ANY),
                pl.BlockSpec(some, lambda i, c: (i, 0, 0)),
                whole((entries, 3 * NANG)),
                whole((entries, LANES)),
            ],
            out_specs=[
                pl.BlockSpec(some, lambda i, c: (i, 0, 0)),
                pl.BlockSpec((8, LANES), lambda i, c: (i, 0)),
            ],
            scratch_shapes=[
                pltpu.VMEM((block, NSHELL, width), jnp.bfloat16),
                pltpu.SMEM((classes + 1,), jnp.int32),
                pltpu.SMEM((entries,), jnp.int32),
                pltpu.SemaphoreType.DMA(()),
            ],
        ),
        out_shape=[
            jax.ShapeDtypeStruct((classes, NSHELL, width), jnp.bfloat16),
            jax.ShapeDtypeStruct((classes, LANES), jnp.float32),
        ],
        compiler_params=params,
        name="gradient",
    )(ids, image_hat, ref_hat, coef, post_sum)

    gradient, log_evidence = reduce_scatter(part, weight, evidence, slots, inverse, dp_count)
    return (gradient[None], log_evidence)


def solution(mesh):
    return jax.shard_map(
        local,
        mesh=mesh,
        in_specs=(
            P("dp", None, None),
            P("dp"),
            P("cls", None, None),
            P(),
            P(),
            P("dp", None),
            P("cls"),
        ),
        out_specs=(P("cls", "dp", None, None), P("dp")),
        check_vma=False,
    )
```

```python
import functools
import math

import jax
import jax.numpy as jnp
import numpy as np
from jax import lax
from jax.experimental import pallas as pl
from jax.experimental.pallas import tpu as pltpu
from jax.sharding import PartitionSpec as P

NSHELL = 64
NANG = 256
LIST = 2
LANES = 128
ROWS = 16
MESH = pl.DeviceIdType.MESH
HIGHEST = lax.Precision.HIGHEST
FIRST = 4
MIB = 1024 * 1024


def angular_tables(points):
    positions = np.arange(points)
    angles = (positions[:, None] * positions[None, :] % points).astype(np.float64) * (
        2.0 * math.pi / points
    )
    cosine = np.cos(angles) / math.sqrt(points)
    sine_part = np.sin(angles) / math.sqrt(points)
    upper_half = np.concatenate([cosine, -sine_part], axis=1)
    lower_half = np.concatenate([sine_part, cosine], axis=1)
    return np.concatenate([upper_half, lower_half], axis=0).astype(np.float32)


def everyone(axis):
    me, count = lax.axis_index(axis), lax.axis_size(axis)

    def peer(step):
        return lax.rem(me + step, count)

    return me, count, peer


def greet(axis):
    _, count, peer = everyone(axis)
    barrier = pltpu.get_barrier_semaphore()

    def one(step, carry):
        pl.semaphore_signal(barrier, inc=1, device_id={axis: peer(step)}, device_id_type=MESH)
        return carry

    lax.fori_loop(1, count, one, 0)


def greeted(axis):
    pl.semaphore_wait(pltpu.get_barrier_semaphore(), lax.axis_size(axis) - 1)


def share(axis, src, dst, send, recv):
    me, count, peer = everyone(axis)

    def outgoing(step):
        return pltpu.make_async_remote_copy(
            src_ref=src(peer(step)), dst_ref=dst.at[me],
            send_sem=send.at[peer(step)], recv_sem=recv.at[me],
            device_id={axis: peer(step)}, device_id_type=MESH,
        )

    def incoming(step):
        return pltpu.make_async_remote_copy(
            src_ref=src(peer(step)), dst_ref=dst.at[peer(step)],
            send_sem=send.at[peer(step)], recv_sem=recv.at[peer(step)],
            device_id={axis: peer(step)}, device_id_type=MESH,
        )

    def loop(act):
        def one(step, carry):
            act(step)
            return carry

        lax.fori_loop(1, count, one, 0)

    return (
        lambda: loop(lambda step: outgoing(step).start()),
        lambda: loop(lambda step: incoming(step).wait_recv()),
        lambda: loop(lambda step: outgoing(step).wait_send()),
    )


def transform_kernel(
    image_steps, classes, image_ref, refs_ref, even_ref, odd_ref, slot_ref, lists_ref,
    image_out, refs_out, ids_out, slots_out, tags_ref, all_tags, send, recv,
):
    step = pl.program_id(0)
    start, arrive, sent = share("dp", lambda _: tags_ref, all_tags, send, recv)
    me = lax.axis_index("dp")
    count = lax.axis_size("dp")
    block = tags_ref.shape[1]

    @pl.when(step == 0)
    def _():
        greet("dp")
        tags_ref[...] = jnp.zeros_like(tags_ref)
        tags_ref[0:1, :] = slot_ref[...]
        tags_ref[1 : 1 + LIST, :] = lists_ref[...]

    @pl.when(step == image_steps // 2)
    def _():
        greeted("dp")
        start()

    def multiply(source, target):
        rows = source[...].reshape(ROWS * NSHELL, 2 * NANG)
        half = NANG // 2
        re_low, re_high, im_low, im_high = (rows[:, i * half : (i + 1) * half] for i in range(4))
        plus = jnp.concatenate([re_low + re_high, im_low + im_high], axis=1)
        minus = jnp.concatenate([re_low - re_high, im_low - im_high], axis=1)
        for n, (mixed, table) in enumerate(((plus, even_ref), (minus, odd_ref))):
            out = jnp.dot(mixed, table[...], preferred_element_type=jnp.float32)
            out = out.astype(jnp.bfloat16).reshape(ROWS, NSHELL, NANG)
            target[:, :, n * half : (n + 1) * half] = out[:, :, :half]
            target[:, :, NANG + n * half : NANG + (n + 1) * half] = out[:, :, half:]

    @pl.when(step < image_steps)
    def _():
        multiply(image_ref, image_out)

    @pl.when(step >= image_steps)
    def _():
        multiply(refs_ref, refs_out)

    @pl.when(step == pl.num_programs(0) - 1)
    def _():
        arrive()
        all_tags[me] = tags_ref[...]
        own = tags_ref[0:1, :].astype(jnp.float32)
        slot = jnp.transpose(jnp.broadcast_to(own, (LANES, block))).astype(jnp.int32)
        lane = lax.broadcasted_iota(jnp.int32, (block, block), 1)

        def look(d, found):
            rows = all_tags[d]
            hit = slot == lane + d * block
            slots_out[pl.ds(d, 1), :] = rows[0:1]
            return tuple(
                total + jnp.where(hit, rows[1 + a : 2 + a], 0) for a, total in enumerate(found)
            )

        found = lax.fori_loop(
            0, count, look, (jnp.zeros((block, block), jnp.int32),) * LIST
        )
        column = lax.axis_index("cls")
        ids_out[...] = jnp.zeros_like(ids_out)
        for a in range(LIST):
            total = jnp.sum(found[a].astype(jnp.float32), axis=1, keepdims=True)
            row = jnp.transpose(jnp.broadcast_to(total, (block, LANES)))[0:1]
            ids_out[a : a + 1, :] = row.astype(jnp.int32) - column * classes
        sent()


def listed(ids_ref, chosen, step, classes):
    count = jnp.int32(0)
    for i in range(ROWS * LIST):
        k = ids_ref[i % LIST, step * ROWS + i // LIST]
        chosen[count] = i
        count = count + jnp.where((k >= 0) & (k < classes), 1, 0)
    return count


def score_kernel(
    ids_ref, xh_ref, rh_ref, shells_ref, rr_ref, counts_ref,
    scores_ref, stats_ref, head, nxt, cross, bias, response, prior_ref, sw_ref, chosen,
):
    step = pl.program_id(0)
    block = ids_ref.shape[1]
    classes = rh_ref.shape[0]
    rotations = rr_ref.shape[0]

    @pl.when(step == 0)
    def _():
        cross[...] = jnp.zeros_like(cross)
        bias[...] = jnp.full_like(bias, -1e30)
        response[...] = jnp.zeros_like(response)
        response[:rotations] = rr_ref[...]
        row = jnp.log1p(counts_ref[...].astype(jnp.float32))
        prior_ref[...] = jnp.transpose(jnp.broadcast_to(row, (LANES, classes)))
        sw_ref[...] = jnp.transpose(jnp.broadcast_to(shells_ref[...], (NANG, NSHELL)))

        def clear(k, carry):
            head[k] = -1
            return carry

        lax.fori_loop(0, classes, clear, 0, unroll=True)

    def entry(n, carry):
        i = chosen[n]
        p = lax.div(i, LIST)
        a = lax.rem(i, LIST)
        row = a * block + step * ROWS + p
        k = ids_ref[a, step * ROWS + p]
        nxt[row] = head[k]
        head[k] = row
        bias[pl.ds(row, 1), :] = prior_ref[pl.ds(k, 1), :]
        re = jnp.zeros((8, NANG), jnp.float32)
        im = jnp.zeros((8, NANG), jnp.float32)
        for j in range(0, NSHELL, ROWS):
            x = xh_ref[p, j : j + ROWS].astype(jnp.float32)
            c = rh_ref[k, j : j + ROWS].astype(jnp.float32)
            sw = sw_ref[j : j + ROWS]
            x_re, x_im, c_re, c_im = x[:, :NANG], x[:, NANG:], c[:, :NANG], c[:, NANG:]
            one = (x_re * c_re + x_im * c_im) * sw
            two = (x_im * c_re - x_re * c_im) * sw
            re = re + one[:8] + one[8:]
            im = im + two[:8] + two[8:]
        cross[pl.ds(row, 1), :NANG] = jnp.sum(re, axis=0, keepdims=True)
        cross[pl.ds(row, 1), NANG:] = jnp.sum(im, axis=0, keepdims=True)
        return carry

    lax.fori_loop(0, listed(ids_ref, chosen, step, classes), entry, 0)

    @pl.when(step == pl.num_programs(0) - 1)
    def _():
        lane = lax.broadcasted_iota(jnp.int32, (block, LANES), 1)
        scores = lax.dot_general(
            cross[...],
            response[...],
            (((1,), (1,)), ((), ())),
            precision=HIGHEST,
            preferred_element_type=jnp.float32,
        ) + bias[...]
        first = jnp.where(lane < rotations, scores[:block], -1e30)
        second = jnp.where(lane < rotations, scores[block:], -1e30)
        scores_ref[:block] = first
        scores_ref[block:] = second
        top = jnp.max(jnp.maximum(first, second), axis=1, keepdims=True)
        total = jnp.sum(jnp.exp(first - top) + jnp.exp(second - top), axis=1, keepdims=True)
        stats = jnp.where(lane == 0, top, total)
        stats_ref[...] = jnp.transpose(stats)[:8]


def posterior_kernel(
    scores_ref, stats_ref, rr_ref, coef_ref, post_ref, evid_ref, all_stats, table, send, recv
):
    start, arrive, sent = share("cls", lambda _: stats_ref, all_stats, send, recv)
    block = scores_ref.shape[0] // LIST
    rotations = rr_ref.shape[0]
    greet("cls")
    table[...] = jnp.zeros_like(table)
    rot_re = rr_ref[:, :NANG]
    rot_im = rr_ref[:, NANG:]
    table[:rotations, :NANG] = rot_re
    table[:rotations, NANG : 2 * NANG] = -rot_im
    table[:rotations, 2 * NANG :] = rot_re * rot_re + rot_im * rot_im
    greeted("cls")
    start()
    all_stats[lax.axis_index("cls")] = stats_ref[...]
    arrive()
    stats = all_stats[...]
    tops = stats[:, 0:1, :]
    top = jnp.max(tops, axis=0)
    total = jnp.sum(stats[:, 1:2, :] * jnp.exp(tops - top[None]), axis=0)
    evid_ref[...] = top + jnp.log(total)
    top_col = jnp.transpose(jnp.broadcast_to(top, (LANES, block)))
    total_col = jnp.transpose(jnp.broadcast_to(total, (LANES, block)))
    for a in range(LIST):
        rows = slice(a * block, (a + 1) * block)
        posterior = jnp.exp(scores_ref[rows] - top_col) / total_col
        post_ref[rows] = jnp.broadcast_to(
            jnp.sum(posterior, axis=1, keepdims=True), (block, LANES)
        )
        coef_ref[rows] = jnp.dot(
            posterior, table[...], precision=HIGHEST, preferred_element_type=jnp.float32
        )
    sent()


def grad_kernel(head, nxt, xh_ref, rh_ref, coef, post_sum, part_ref, weight_ref):
    step = pl.program_id(0)
    block = xh_ref.shape[0]
    per_step = rh_ref.shape[0]
    pieces = [slice(j, j + ROWS) for j in range(0, NSHELL, ROWS)]

    def one_class(c, carry):
        def more(state):
            return state[0] >= 0

        def add(state):
            row, vol, weight, g_re, g_im = state
            p = lax.rem(row, block)
            re = coef[pl.ds(row, 1), :NANG]
            im = coef[pl.ds(row, 1), NANG : 2 * NANG]
            new_re, new_im = [], []
            for rows, one, two in zip(pieces, g_re, g_im):
                x_re = xh_ref[p, rows, :NANG].astype(jnp.float32)
                x_im = xh_ref[p, rows, NANG:].astype(jnp.float32)
                new_re.append(one + (x_re * re - x_im * im))
                new_im.append(two + (x_re * im + x_im * re))
            return (
                nxt[row],
                vol + coef[pl.ds(row, 1), 2 * NANG :],
                weight + post_sum[pl.ds(row, 1), :],
                tuple(new_re),
                tuple(new_im),
            )

        zeros = (jnp.zeros((ROWS, NANG), jnp.float32),) * len(pieces)
        _, vol, weight, g_re, g_im = lax.while_loop(
            more,
            add,
            (
                head[step * per_step + c],
                jnp.zeros((1, NANG), jnp.float32),
                jnp.zeros((1, LANES), jnp.float32),
                zeros,
                zeros,
            ),
        )
        weight_ref[pl.ds(c, 1), :] = weight
        for rows, one, two in zip(pieces, g_re, g_im):
            c_re = rh_ref[c, rows, :NANG].astype(jnp.float32)
            c_im = rh_ref[c, rows, NANG:].astype(jnp.float32)
            part_ref[c, rows, :NANG] = (one - vol * c_re).astype(jnp.bfloat16)
            part_ref[c, rows, NANG:] = (two - vol * c_im).astype(jnp.bfloat16)
        return carry

    lax.fori_loop(0, per_step, one_class, 0)


def reduce_kernel(
    lines, groups, p_ref, weight_ref, evid_ref, slots_ref, out_ref, log_ref,
    held, own, from_left, from_right, weights, evids, scale,
    own_sem, pair_send, pair_recv, right_send, right_recv, left_send, left_recv,
    weight_send, weight_recv, evid_send, evid_recv,
):
    me = lax.axis_index("dp")
    x = lax.rem(me, 2)
    z = lax.div(me, 2)
    partner = me + 1 - 2 * x
    has_left = z > 0
    has_right = z < lines - 1
    chunks = lines * groups

    weight_start, weight_arrive, weight_sent = share(
        "dp", lambda d: weight_ref.at[d], weights, weight_send, weight_recv
    )
    evid_start, evid_arrive, evid_sent = share(
        "dp", lambda _: evid_ref, evids, evid_send, evid_recv
    )

    def where_is(t):
        layer, i = lax.div(t, 2 * groups), lax.rem(t, 2 * groups)
        low = lax.rem(i, 2)
        return (1 - low) * (lines - 1 - layer) + low * layer, lax.div(i, 2)

    def keep(b, g):
        return pltpu.make_async_copy(p_ref.at[b, x, g], own.at[b, g], own_sem.at[b, g])

    def pair(b, g):
        return pltpu.make_async_remote_copy(
            src_ref=p_ref.at[b, 1 - x, g], dst_ref=held.at[b, g],
            send_sem=pair_send.at[b, g], recv_sem=pair_recv.at[b, g],
            device_id={"dp": partner}, device_id_type=MESH,
        )

    def right(b, g):
        return pltpu.make_async_remote_copy(
            src_ref=held.at[b, g], dst_ref=from_left.at[b, g],
            send_sem=right_send.at[b, g], recv_sem=right_recv.at[b, g],
            device_id={"dp": me + 2}, device_id_type=MESH,
        )

    def left(b, g):
        return pltpu.make_async_remote_copy(
            src_ref=held.at[b, g], dst_ref=from_right.at[b, g],
            send_sem=left_send.at[b, g], recv_sem=left_recv.at[b, g],
            device_id={"dp": me - 2}, device_id_type=MESH,
        )

    def add(b, g, other):
        held[b, g] = (
            held[b, g].astype(jnp.float32) + other[b, g].astype(jnp.float32)
        ).astype(jnp.bfloat16)

    def each(act):
        def one(t, carry):
            act(*where_is(t))
            return carry

        lax.fori_loop(0, chunks, one, 0)

    def relay(t):
        b, g = where_is(t)
        keep(b, g).wait()
        pair(b, g).wait_recv()

        add(b, g, own)

        @pl.when(z < b)
        def _():
            @pl.when(has_left)
            def _():
                right(b, g).wait_recv()
                add(b, g, from_left)

            right(b, g).start()

        @pl.when(z > b)
        def _():
            @pl.when(has_right)
            def _():
                left(b, g).wait_recv()
                add(b, g, from_right)

            left(b, g).start()

    def small():
        count = weights.shape[0]
        weight_arrive()
        evid_arrive()
        weights[me] = weight_ref[me]
        evids[me] = evid_ref[...]
        block = evid_ref.shape[1]
        mine = me * block + lax.broadcasted_iota(jnp.int32, (block, block), 0)

        def look(d, total):
            return total + jnp.where(slots_ref[pl.ds(d, 1), :] == mine, evids[d], 0.0)

        found = lax.fori_loop(0, count, look, jnp.zeros((block, block), jnp.float32))
        summed = jnp.sum(found, axis=1, keepdims=True)
        log_ref[...] = jnp.transpose(jnp.broadcast_to(summed, (block, LANES)))[0:1]
        inverse = 1.0 / (1.0 + jnp.sum(weights[...], axis=0))
        for n in range(2 * NANG // LANES):
            scale[:, n * LANES : (n + 1) * LANES] = inverse

    def finish(g, carry):
        @pl.when(has_left)
        def _():
            right(z, g).wait_recv()
            held[z, g] = (
                held[z, g].astype(jnp.float32) + from_left[z, g].astype(jnp.float32)
            ).astype(jnp.bfloat16)

        @pl.when(has_right)
        def _():
            left(z, g).wait_recv()
            held[z, g] = (
                held[z, g].astype(jnp.float32) + from_right[z, g].astype(jnp.float32)
            ).astype(jnp.bfloat16)

        out_ref[g] = (held[z, g].astype(jnp.float32) * scale[pl.ds(g, 1), :]).astype(jnp.bfloat16)
        return carry

    each(lambda b, g: keep(b, g).start())
    greet("dp")
    greeted("dp")

    def begin(t, carry):
        pair(*where_is(t)).start()
        return carry

    lax.fori_loop(0, FIRST, begin, 0)
    weight_start()
    evid_start()
    lax.fori_loop(FIRST, chunks, begin, 0)

    def passing(t, carry):
        relay(t)
        return carry

    lax.fori_loop(0, chunks, passing, 0)
    small()
    lax.fori_loop(0, groups, finish, 0)

    def drain(b, g):
        pair(b, g).wait_send()

        @pl.when(z < b)
        def _():
            right(b, g).wait_send()

        @pl.when(z > b)
        def _():
            left(b, g).wait_send()

    each(drain)
    weight_sent()
    evid_sent()


def vmem():
    return pl.BlockSpec(memory_space=pltpu.VMEM)


def remote(collective_id, mebibytes):
    return pltpu.CompilerParams(
        collective_id=collective_id, has_side_effects=True, vmem_limit_bytes=mebibytes * MIB
    )


def reduce_scatter(part, weight, evidence, slots, dp_count):
    classes = part.shape[0]
    block = evidence.shape[1]
    lines = dp_count // 2
    owned = classes // dp_count
    shape = part.shape[1:]
    whole = pltpu.VMEM((lines, owned) + shape, jnp.bfloat16)
    sems = pltpu.SemaphoreType.DMA((lines, owned))
    row_sems = pltpu.SemaphoreType.DMA((dp_count,))
    out, log_evidence = pl.pallas_call(
        functools.partial(reduce_kernel, lines, owned),
        out_shape=[
            jax.ShapeDtypeStruct((owned,) + shape, jnp.bfloat16),
            jax.ShapeDtypeStruct((1, block), jnp.float32),
        ],
        in_specs=[pl.BlockSpec(memory_space=pl.ANY)] + [vmem()] * 3,
        out_specs=[vmem()] * 2,
        scratch_shapes=[
            whole, whole, whole, whole,
            pltpu.VMEM((dp_count, owned, LANES), jnp.float32),
            pltpu.VMEM((dp_count, 1, block), jnp.float32),
            pltpu.VMEM((owned, 2 * NANG), jnp.float32),
        ]
        + [sems] * 7
        + [row_sems] * 4,
        compiler_params=remote(2, 20),
        name="reduce_over_dp",
    )(
        part.reshape((lines, 2, owned) + shape),
        weight.reshape(dp_count, owned, LANES),
        evidence,
        slots,
    )
    return out, log_evidence[0]


def local(
    images, pose_slot, references, rotation_response, shell_weight, class_lists, class_counts
):
    dp_count = lax.axis_size("dp")
    columns = lax.axis_size("cls")
    block = images.shape[0]
    classes = references.shape[0]
    width = 2 * NANG
    entries = block * LIST
    rotations = rotation_response.shape[0]
    full_table = angular_tables(NANG)
    parity = np.concatenate([np.arange(0, NANG, 2), np.arange(1, NANG, 2)])
    order = np.concatenate([parity, NANG + parity])
    low = np.concatenate([np.arange(NANG // 2), NANG + np.arange(NANG // 2)])
    evens = np.concatenate([np.arange(0, NANG, 2), NANG + np.arange(0, NANG, 2)])
    even = jnp.asarray(full_table[np.ix_(low, evens)].astype(jnp.bfloat16))
    odd = jnp.asarray(full_table[np.ix_(low, evens + 1)].astype(jnp.bfloat16))
    inverse = jnp.asarray(np.ascontiguousarray(full_table.T[order]).astype(jnp.bfloat16))
    rotation_response = jnp.transpose(
        rotation_response.reshape(rotations, 2, NANG // 2, 2), (0, 1, 3, 2)
    ).reshape(rotations, width)

    image_steps = block // ROWS
    ref_steps = classes // ROWS
    cube = (ROWS, NSHELL, width)

    def fixed(shape):
        return pl.BlockSpec(shape, lambda i: (0,) * len(shape))

    def image_block():
        return pl.BlockSpec(cube, lambda i: (jnp.minimum(i, image_steps - 1), 0, 0))

    def ref_block():
        return pl.BlockSpec(cube, lambda i: (jnp.maximum(i - image_steps, 0), 0, 0))

    image_hat, ref_hat, ids, slots = pl.pallas_call(
        functools.partial(transform_kernel, image_steps, classes),
        grid=(image_steps + ref_steps,),
        in_specs=[
            image_block(),
            ref_block(),
            fixed((NANG, NANG)),
            fixed((NANG, NANG)),
            fixed((1, block)),
            fixed((LIST, block)),
        ],
        out_specs=[image_block(), ref_block(), fixed((8, block)), fixed((dp_count, block))],
        out_shape=[
            jax.ShapeDtypeStruct(images.shape, jnp.bfloat16),
            jax.ShapeDtypeStruct(references.shape, jnp.bfloat16),
            jax.ShapeDtypeStruct((8, block), jnp.int32),
            jax.ShapeDtypeStruct((dp_count, block), jnp.int32),
        ],
        scratch_shapes=[
            pltpu.VMEM((8, block), jnp.int32),
            pltpu.VMEM((dp_count, 8, block), jnp.int32),
            pltpu.SemaphoreType.DMA((dp_count,)),
            pltpu.SemaphoreType.DMA((dp_count,)),
        ],
        compiler_params=remote(0, 24),
        name="transform",
    )(images, references, even, odd, pose_slot[None, :], class_lists.T)

    def whole(shape):
        return pl.BlockSpec(shape, lambda i, c: (0,) * len(shape))

    image_spec = pl.BlockSpec(cube, lambda i, c: (i, 0, 0))

    def plain(mebibytes):
        return pltpu.CompilerParams(
            dimension_semantics=("arbitrary",), vmem_limit_bytes=mebibytes * MIB
        )

    scores, stats, head, nxt = pl.pallas_call(
        score_kernel,
        grid_spec=pltpu.PrefetchScalarGridSpec(
            num_scalar_prefetch=1,
            grid=(image_steps,),
            in_specs=[
                image_spec,
                whole((classes, NSHELL, width)),
                whole((1, NSHELL)),
                whole((rotations, width)),
                whole((1, classes)),
            ],
            out_specs=[
                whole((entries, LANES)),
                whole((8, block)),
                pl.BlockSpec(memory_space=pltpu.SMEM),
                pl.BlockSpec(memory_space=pltpu.SMEM),
            ],
            scratch_shapes=[
                pltpu.VMEM((entries, width), jnp.float32),
                pltpu.VMEM((entries, LANES), jnp.float32),
                pltpu.VMEM((LANES, width), jnp.float32),
                pltpu.VMEM((classes, LANES), jnp.float32),
                pltpu.VMEM((NSHELL, NANG), jnp.float32),
                pltpu.SMEM((ROWS * LIST + 1,), jnp.int32),
            ],
        ),
        out_shape=[
            jax.ShapeDtypeStruct((entries, LANES), jnp.float32),
            jax.ShapeDtypeStruct((8, block), jnp.float32),
            jax.ShapeDtypeStruct((classes,), jnp.int32),
            jax.ShapeDtypeStruct((entries,), jnp.int32),
        ],
        compiler_params=plain(24),
        name="scores",
    )(ids, image_hat, ref_hat, shell_weight[None, :], rotation_response, class_counts[None, :])

    coef, post_sum, evidence = pl.pallas_call(
        posterior_kernel,
        in_specs=[vmem()] * 3,
        out_specs=[vmem()] * 3,
        out_shape=[
            jax.ShapeDtypeStruct((entries, 3 * NANG), jnp.float32),
            jax.ShapeDtypeStruct((entries, LANES), jnp.float32),
            jax.ShapeDtypeStruct((1, block), jnp.float32),
        ],
        scratch_shapes=[
            pltpu.VMEM((columns, 8, block), jnp.float32),
            pltpu.VMEM((LANES, 3 * NANG), jnp.float32),
            pltpu.SemaphoreType.DMA((columns,)),
            pltpu.SemaphoreType.DMA((columns,)),
        ],
        compiler_params=remote(1, 8),
        name="posterior",
    )(scores, stats, rotation_response)

    some = (8, NSHELL, width)

    def listed_whole(shape):
        return pl.BlockSpec(shape, lambda i, h, n: (0,) * len(shape))

    part, weight = pl.pallas_call(
        grad_kernel,
        grid_spec=pltpu.PrefetchScalarGridSpec(
            num_scalar_prefetch=2,
            grid=(classes // 8,),
            in_specs=[
                vmem(),
                pl.BlockSpec(some, lambda i, h, n: (i, 0, 0)),
                listed_whole((entries, 3 * NANG)),
                listed_whole((entries, LANES)),
            ],
            out_specs=[
                pl.BlockSpec(some, lambda i, h, n: (i, 0, 0)),
                pl.BlockSpec((8, LANES), lambda i, h, n: (i, 0)),
            ],
        ),
        out_shape=[
            jax.ShapeDtypeStruct((classes, NSHELL, width), jnp.bfloat16),
            jax.ShapeDtypeStruct((classes, LANES), jnp.float32),
        ],
        compiler_params=plain(24),
        name="gradient",
    )(head, nxt, image_hat, ref_hat, coef, post_sum)

    scaled, log_evidence = reduce_scatter(part, weight, evidence, slots, dp_count)
    result = jnp.dot(
        scaled.reshape(-1, width), inverse, preferred_element_type=jnp.float32
    )
    return (result.reshape((1,) + scaled.shape), log_evidence)


def solution(mesh):
    return jax.shard_map(
        local,
        mesh=mesh,
        in_specs=(
            P("dp", None, None),
            P("dp"),
            P("cls", None, None),
            P(),
            P(),
            P("dp", None),
            P("cls"),
        ),
        out_specs=(P("cls", "dp", None, None), P("dp")),
        check_vma=False,
    )
```

```python
import functools
import math

import jax
import jax.numpy as jnp
import numpy as np
from jax import lax
from jax.experimental import pallas as pl
from jax.experimental.pallas import tpu as pltpu
from jax.sharding import PartitionSpec as P

NSHELL = 64
NANG = 256
LIST = 2
LANES = 128
ROWS = 16
MESH = pl.DeviceIdType.MESH
HIGHEST = lax.Precision.HIGHEST
MIB = 1024 * 1024


def angular_tables(points):
    positions = np.arange(points)
    angles = (positions[:, None] * positions[None, :] % points).astype(np.float64) * (
        2.0 * math.pi / points
    )
    cosine = np.cos(angles) / math.sqrt(points)
    sine_part = np.sin(angles) / math.sqrt(points)
    upper_half = np.concatenate([cosine, -sine_part], axis=1)
    lower_half = np.concatenate([sine_part, cosine], axis=1)
    return np.concatenate([upper_half, lower_half], axis=0).astype(np.float32)


def everyone(axis):
    me, count = lax.axis_index(axis), lax.axis_size(axis)

    def peer(step):
        return lax.rem(me + step, count)

    return me, count, peer


def greet(axis):
    _, count, peer = everyone(axis)
    barrier = pltpu.get_barrier_semaphore()

    def one(step, carry):
        pl.semaphore_signal(barrier, inc=1, device_id={axis: peer(step)}, device_id_type=MESH)
        return carry

    lax.fori_loop(1, count, one, 0)


def greeted(axis):
    pl.semaphore_wait(pltpu.get_barrier_semaphore(), lax.axis_size(axis) - 1)


def share(axis, src, dst, send, recv):
    me, count, peer = everyone(axis)

    def outgoing(step):
        return pltpu.make_async_remote_copy(
            src_ref=src(peer(step)), dst_ref=dst.at[me],
            send_sem=send.at[peer(step)], recv_sem=recv.at[me],
            device_id={axis: peer(step)}, device_id_type=MESH,
        )

    def incoming(step):
        return pltpu.make_async_remote_copy(
            src_ref=src(peer(step)), dst_ref=dst.at[peer(step)],
            send_sem=send.at[peer(step)], recv_sem=recv.at[peer(step)],
            device_id={axis: peer(step)}, device_id_type=MESH,
        )

    def loop(act):
        def one(step, carry):
            act(step)
            return carry

        lax.fori_loop(1, count, one, 0)

    return (
        lambda: loop(lambda step: outgoing(step).start()),
        lambda: loop(lambda step: incoming(step).wait_recv()),
        lambda: loop(lambda step: outgoing(step).wait_send()),
    )


def transform_kernel(
    image_ref, refs_ref, table_hbm, slot_ref, lists_ref,
    image_out, refs_out, ids_out, slots_out,
    image_in, refs_in, table_ref, tags_ref, all_tags, block_sems, small_sems, send, recv,
):
    start, arrive, sent = share("dp", lambda _: tags_ref, all_tags, send, recv)
    me = lax.axis_index("dp")
    count = lax.axis_size("dp")
    block = tags_ref.shape[1]
    classes = refs_ref.shape[0]
    image_steps = image_ref.shape[0] // ROWS
    half = NANG // 2

    def rows_of(i):
        return pl.ds(pl.multiple_of(i * ROWS, ROWS), ROWS)

    def fetch_image(i):
        return pltpu.make_async_copy(
            image_ref.at[rows_of(i)], image_in.at[rows_of(i)], block_sems.at[i]
        )

    def fetch_refs(i):
        return pltpu.make_async_copy(
            refs_ref.at[rows_of(i)], refs_in.at[rows_of(i)], block_sems.at[image_steps + i]
        )

    small = (
        pltpu.make_async_copy(table_hbm, table_ref, small_sems.at[0]),
        pltpu.make_async_copy(slot_ref, tags_ref.at[pl.ds(0, 1)], small_sems.at[1]),
        pltpu.make_async_copy(lists_ref, tags_ref.at[pl.ds(1, LIST)], small_sems.at[2]),
    )

    def multiply(source, target, i):
        block_rows = source[rows_of(i)].reshape(ROWS * NSHELL, 2 * NANG)
        re_low, re_high, im_low, im_high = (
            block_rows[:, n * half : (n + 1) * half] for n in range(4)
        )
        plus = jnp.concatenate([re_low + re_high, im_low + im_high], axis=1)
        minus = jnp.concatenate([re_low - re_high, im_low - im_high], axis=1)
        for n, mixed in enumerate((plus, minus)):
            out = jnp.dot(mixed, table_ref[n], preferred_element_type=jnp.float32)
            out = out.astype(jnp.bfloat16).reshape(ROWS, NSHELL, NANG)
            target[rows_of(i), :, n * half : (n + 1) * half] = out[:, :, :half]
            target[rows_of(i), :, NANG + n * half : NANG + (n + 1) * half] = out[:, :, half:]

    def loop(low, high, act):
        def one(i, carry):
            act(i)
            return carry

        lax.fori_loop(low, high, one, 0)

    def image_step(i):
        fetch_image(i).wait()
        multiply(image_in, image_out, i)

    def refs_step(i):
        fetch_refs(i).wait()
        multiply(refs_in, refs_out, i)

    small[0].start()
    loop(0, 2, lambda i: fetch_image(i).start())
    small[1].start()
    small[2].start()
    loop(2, image_steps, lambda i: fetch_image(i).start())
    loop(0, classes // ROWS, lambda i: fetch_refs(i).start())
    greet("dp")
    small[0].wait()
    loop(0, image_steps // 2, image_step)
    small[1].wait()
    small[2].wait()
    greeted("dp")
    start()
    loop(image_steps // 2, image_steps, image_step)
    loop(0, classes // ROWS, refs_step)

    arrive()
    all_tags[me] = tags_ref[...]
    own = tags_ref[0:1, :].astype(jnp.float32)
    slot = jnp.transpose(jnp.broadcast_to(own, (LANES, block))).astype(jnp.int32)
    lane = lax.broadcasted_iota(jnp.int32, (block, block), 1)

    def look(d, found):
        rows = all_tags[d]
        hit = slot == lane + d * block
        slots_out[pl.ds(d, 1), :] = rows[0:1]
        return tuple(
            total + jnp.where(hit, rows[1 + a : 2 + a], 0) for a, total in enumerate(found)
        )

    found = lax.fori_loop(0, count, look, (jnp.zeros((block, block), jnp.int32),) * LIST)
    column = lax.axis_index("cls")
    ids_out[...] = jnp.zeros_like(ids_out)
    for a in range(LIST):
        total = jnp.sum(found[a].astype(jnp.float32), axis=1, keepdims=True)
        row = jnp.transpose(jnp.broadcast_to(total, (block, LANES)))[0:1]
        ids_out[a : a + 1, :] = row.astype(jnp.int32) - column * classes
    sent()


def listed(ids_ref, chosen, step, classes):
    count = jnp.int32(0)
    for i in range(ROWS * LIST):
        k = ids_ref[i % LIST, step * ROWS + i // LIST]
        chosen[count] = i
        count = count + jnp.where((k >= 0) & (k < classes), 1, 0)
    return count


def score_kernel(
    ids_ref, xh_ref, rh_ref, shells_ref, rr_ref, counts_ref,
    scores_ref, stats_ref, head, nxt, cross, bias, response, prior_ref, sw_ref, chosen,
):
    step = pl.program_id(0)
    block = ids_ref.shape[1]
    classes = rh_ref.shape[0]
    rotations = rr_ref.shape[0]

    @pl.when(step == 0)
    def _():
        cross[...] = jnp.zeros_like(cross)
        bias[...] = jnp.full_like(bias, -1e30)
        response[...] = jnp.zeros_like(response)
        response[:rotations] = rr_ref[...]
        row = jnp.log1p(counts_ref[...].astype(jnp.float32))
        prior_ref[...] = jnp.transpose(jnp.broadcast_to(row, (LANES, classes)))
        sw_ref[...] = jnp.transpose(jnp.broadcast_to(shells_ref[...], (NANG, NSHELL)))

        def clear(k, carry):
            head[k] = -1
            return carry

        lax.fori_loop(0, classes, clear, 0, unroll=True)

    def entry(n, carry):
        i = chosen[n]
        p = lax.div(i, LIST)
        a = lax.rem(i, LIST)
        row = a * block + step * ROWS + p
        k = ids_ref[a, step * ROWS + p]
        nxt[row] = head[k]
        head[k] = row
        bias[pl.ds(row, 1), :] = prior_ref[pl.ds(k, 1), :]
        re = jnp.zeros((8, NANG), jnp.float32)
        im = jnp.zeros((8, NANG), jnp.float32)
        for j in range(0, NSHELL, ROWS):
            x = xh_ref[p, j : j + ROWS].astype(jnp.float32)
            c = rh_ref[k, j : j + ROWS].astype(jnp.float32)
            sw = sw_ref[j : j + ROWS]
            x_re, x_im, c_re, c_im = x[:, :NANG], x[:, NANG:], c[:, :NANG], c[:, NANG:]
            one = (x_re * c_re + x_im * c_im) * sw
            two = (x_im * c_re - x_re * c_im) * sw
            re = re + one[:8] + one[8:]
            im = im + two[:8] + two[8:]
        cross[pl.ds(row, 1), :NANG] = jnp.sum(re, axis=0, keepdims=True)
        cross[pl.ds(row, 1), NANG:] = jnp.sum(im, axis=0, keepdims=True)
        return carry

    lax.fori_loop(0, listed(ids_ref, chosen, step, classes), entry, 0)

    @pl.when(step == pl.num_programs(0) - 1)
    def _():
        lane = lax.broadcasted_iota(jnp.int32, (block, LANES), 1)
        scores = lax.dot_general(
            cross[...],
            response[...],
            (((1,), (1,)), ((), ())),
            precision=HIGHEST,
            preferred_element_type=jnp.float32,
        ) + bias[...]
        first = jnp.where(lane < rotations, scores[:block], -1e30)
        second = jnp.where(lane < rotations, scores[block:], -1e30)
        scores_ref[:block] = first
        scores_ref[block:] = second
        top = jnp.max(jnp.maximum(first, second), axis=1, keepdims=True)
        total = jnp.sum(jnp.exp(first - top) + jnp.exp(second - top), axis=1, keepdims=True)
        stats = jnp.where(lane == 0, top, total)
        stats_ref[...] = jnp.transpose(stats)[:8]


def posterior_kernel(
    scores_ref, stats_ref, rr_ref, coef_ref, post_ref, evid_ref, all_stats, table, send, recv
):
    start, arrive, sent = share("cls", lambda _: stats_ref, all_stats, send, recv)
    block = scores_ref.shape[0] // LIST
    rotations = rr_ref.shape[0]
    greet("cls")
    table[...] = jnp.zeros_like(table)
    rot_re = rr_ref[:, :NANG]
    rot_im = rr_ref[:, NANG:]
    table[:rotations, :NANG] = rot_re
    table[:rotations, NANG : 2 * NANG] = -rot_im
    table[:rotations, 2 * NANG :] = rot_re * rot_re + rot_im * rot_im
    greeted("cls")
    start()
    all_stats[lax.axis_index("cls")] = stats_ref[...]
    arrive()
    stats = all_stats[...]
    tops = stats[:, 0:1, :]
    top = jnp.max(tops, axis=0)
    total = jnp.sum(stats[:, 1:2, :] * jnp.exp(tops - top[None]), axis=0)
    evid_ref[...] = top + jnp.log(total)
    top_col = jnp.transpose(jnp.broadcast_to(top, (LANES, block)))
    total_col = jnp.transpose(jnp.broadcast_to(total, (LANES, block)))
    for a in range(LIST):
        rows = slice(a * block, (a + 1) * block)
        posterior = jnp.exp(scores_ref[rows] - top_col) / total_col
        post_ref[rows] = jnp.broadcast_to(
            jnp.sum(posterior, axis=1, keepdims=True), (block, LANES)
        )
        coef_ref[rows] = jnp.dot(
            posterior, table[...], precision=HIGHEST, preferred_element_type=jnp.float32
        )
    sent()


def grad_kernel(head, nxt, xh_ref, rh_ref, coef, post_sum, part_ref, weight_ref):
    step = pl.program_id(0)
    block = xh_ref.shape[0]
    per_step = rh_ref.shape[0]
    pieces = [slice(j, j + ROWS) for j in range(0, NSHELL, ROWS)]

    def one_class(c, carry):
        def more(state):
            return state[0] >= 0

        def add(state):
            row, vol, weight, g_re, g_im = state
            p = lax.rem(row, block)
            re = coef[pl.ds(row, 1), :NANG]
            im = coef[pl.ds(row, 1), NANG : 2 * NANG]
            new_re, new_im = [], []
            for rows, one, two in zip(pieces, g_re, g_im):
                x_re = xh_ref[p, rows, :NANG].astype(jnp.float32)
                x_im = xh_ref[p, rows, NANG:].astype(jnp.float32)
                new_re.append(one + (x_re * re - x_im * im))
                new_im.append(two + (x_re * im + x_im * re))
            return (
                nxt[row],
                vol + coef[pl.ds(row, 1), 2 * NANG :],
                weight + post_sum[pl.ds(row, 1), :],
                tuple(new_re),
                tuple(new_im),
            )

        zeros = (jnp.zeros((ROWS, NANG), jnp.float32),) * len(pieces)
        _, vol, weight, g_re, g_im = lax.while_loop(
            more,
            add,
            (
                head[step * per_step + c],
                jnp.zeros((1, NANG), jnp.float32),
                jnp.zeros((1, LANES), jnp.float32),
                zeros,
                zeros,
            ),
        )
        weight_ref[pl.ds(c, 1), :] = weight
        for rows, one, two in zip(pieces, g_re, g_im):
            c_re = rh_ref[c, rows, :NANG].astype(jnp.float32)
            c_im = rh_ref[c, rows, NANG:].astype(jnp.float32)
            part_ref[c, rows, :NANG] = (one - vol * c_re).astype(jnp.bfloat16)
            part_ref[c, rows, NANG:] = (two - vol * c_im).astype(jnp.bfloat16)
        return carry

    lax.fori_loop(0, per_step, one_class, 0)


def reduce_kernel(
    lines, groups, p_ref, weight_ref, evid_ref, slots_ref, out_ref, log_ref,
    held, from_left, from_right, weights, evids, scale,
    pair_send, pair_recv, right_send, right_recv, left_send, left_recv,
    weight_send, weight_recv, evid_send, evid_recv,
):
    me = lax.axis_index("dp")
    x = lax.rem(me, 2)
    z = lax.div(me, 2)
    partner = me + 1 - 2 * x
    has_left = z > 0
    has_right = z < lines - 1

    weight_start, weight_arrive, weight_sent = share(
        "dp", lambda d: weight_ref.at[d], weights, weight_send, weight_recv
    )
    evid_start, evid_arrive, evid_sent = share(
        "dp", lambda _: evid_ref, evids, evid_send, evid_recv
    )

    def some(g):
        first, size = groups[g]
        return pl.ds(first, size)

    def pair(b, g):
        return pltpu.make_async_remote_copy(
            src_ref=p_ref.at[b, 1 - x, some(g)], dst_ref=held.at[b, some(g)],
            send_sem=pair_send.at[b, g], recv_sem=pair_recv.at[b, g],
            device_id={"dp": partner}, device_id_type=MESH,
        )

    def right(b, g):
        return pltpu.make_async_remote_copy(
            src_ref=held.at[b, some(g)], dst_ref=from_left.at[b, some(g)],
            send_sem=right_send.at[b, g], recv_sem=right_recv.at[b, g],
            device_id={"dp": me + 2}, device_id_type=MESH,
        )

    def left(b, g):
        return pltpu.make_async_remote_copy(
            src_ref=held.at[b, some(g)], dst_ref=from_right.at[b, some(g)],
            send_sem=left_send.at[b, g], recv_sem=left_recv.at[b, g],
            device_id={"dp": me - 2}, device_id_type=MESH,
        )

    def add(b, g, other):
        first, size = groups[g]
        for c in range(first, first + size):
            held[b, c] = (
                held[b, c].astype(jnp.float32) + other(c).astype(jnp.float32)
            ).astype(jnp.bfloat16)

    def each(g, act):
        def one(i, carry):
            odd, half = lax.rem(i, 2), lax.div(i, 2)
            act((1 - odd) * (lines - 1 - half) + odd * half, g)
            return carry

        lax.fori_loop(0, lines, one, 0)

    def relay(b, g):
        pair(b, g).wait_recv()
        add(b, g, lambda c: p_ref[b, x, c])

        @pl.when(z < b)
        def _():
            @pl.when(has_left)
            def _():
                right(b, g).wait_recv()
                add(b, g, lambda c: from_left[b, c])

            right(b, g).start()

        @pl.when(z > b)
        def _():
            @pl.when(has_right)
            def _():
                left(b, g).wait_recv()
                add(b, g, lambda c: from_right[b, c])

            left(b, g).start()

    def small():
        count = weights.shape[0]
        weight_arrive()
        evid_arrive()
        weights[me] = weight_ref[me]
        evids[me] = evid_ref[...]
        block = evid_ref.shape[1]
        mine = me * block + lax.broadcasted_iota(jnp.int32, (block, block), 0)

        def look(d, total):
            return total + jnp.where(slots_ref[pl.ds(d, 1), :] == mine, evids[d], 0.0)

        found = lax.fori_loop(0, count, look, jnp.zeros((block, block), jnp.float32))
        summed = jnp.sum(found, axis=1, keepdims=True)
        log_ref[...] = jnp.transpose(jnp.broadcast_to(summed, (block, LANES)))[0:1]
        inverse = 1.0 / (1.0 + jnp.sum(weights[...], axis=0))
        for n in range(2 * NANG // LANES):
            scale[:, n * LANES : (n + 1) * LANES] = inverse

    def finish(g):
        @pl.when(has_left)
        def _():
            right(z, g).wait_recv()
            add(z, g, lambda c: from_left[z, c])

        @pl.when(has_right)
        def _():
            left(z, g).wait_recv()
            add(z, g, lambda c: from_right[z, c])

        first, size = groups[g]
        for c in range(first, first + size):
            out_ref[c] = (held[z, c].astype(jnp.float32) * scale[c : c + 1, :]).astype(
                jnp.bfloat16
            )

    greet("dp")
    greeted("dp")
    last = len(groups) - 1
    each(0, lambda b, g: pair(b, g).start())
    weight_start()
    evid_start()
    for n in range(1, len(groups)):
        each(n, lambda b, g: pair(b, g).start())
    for n in range(last):
        each(n, relay)
    small()
    each(last, relay)
    for n in range(len(groups)):
        finish(n)

    def drain(b, g):
        pair(b, g).wait_send()

        @pl.when(z < b)
        def _():
            right(b, g).wait_send()

        @pl.when(z > b)
        def _():
            left(b, g).wait_send()

    for n in range(len(groups)):
        each(n, drain)
    weight_sent()
    evid_sent()


def vmem():
    return pl.BlockSpec(memory_space=pltpu.VMEM)


def remote(collective_id, mebibytes):
    return pltpu.CompilerParams(
        collective_id=collective_id, has_side_effects=True, vmem_limit_bytes=mebibytes * MIB
    )


def reduce_scatter(part, weight, evidence, slots, dp_count):
    classes = part.shape[0]
    block = evidence.shape[1]
    lines = dp_count // 2
    owned = classes // dp_count
    shape = part.shape[1:]
    whole = pltpu.VMEM((lines, owned) + shape, jnp.bfloat16)
    groups, first = [], 0
    while first < owned:
        size = 2 if owned - first > 2 else 1
        groups.append((first, size))
        first += size
    sems = pltpu.SemaphoreType.DMA((lines, len(groups)))
    row_sems = pltpu.SemaphoreType.DMA((dp_count,))
    out, log_evidence = pl.pallas_call(
        functools.partial(reduce_kernel, lines, tuple(groups)),
        out_shape=[
            jax.ShapeDtypeStruct((owned,) + shape, jnp.bfloat16),
            jax.ShapeDtypeStruct((1, block), jnp.float32),
        ],
        in_specs=[vmem()] * 4,
        out_specs=[vmem()] * 2,
        scratch_shapes=[
            whole, whole, whole,
            pltpu.VMEM((dp_count, owned, LANES), jnp.float32),
            pltpu.VMEM((dp_count, 1, block), jnp.float32),
            pltpu.VMEM((owned, 2 * NANG), jnp.float32),
        ]
        + [sems] * 6
        + [row_sems] * 4,
        compiler_params=remote(2, 20),
        name="reduce_over_dp",
    )(
        part.reshape((lines, 2, owned) + shape),
        weight.reshape(dp_count, owned, LANES),
        evidence,
        slots,
    )
    return out, log_evidence[0]


def local(
    images, pose_slot, references, rotation_response, shell_weight, class_lists, class_counts
):
    dp_count = lax.axis_size("dp")
    columns = lax.axis_size("cls")
    block = images.shape[0]
    classes = references.shape[0]
    width = 2 * NANG
    entries = block * LIST
    rotations = rotation_response.shape[0]
    full_table = angular_tables(NANG)
    parity = np.concatenate([np.arange(0, NANG, 2), np.arange(1, NANG, 2)])
    order = np.concatenate([parity, NANG + parity])
    low = np.concatenate([np.arange(NANG // 2), NANG + np.arange(NANG // 2)])
    evens = np.concatenate([np.arange(0, NANG, 2), NANG + np.arange(0, NANG, 2)])
    table = jnp.asarray(
        np.stack([full_table[np.ix_(low, evens + n)] for n in range(2)]).astype(jnp.bfloat16)
    )
    inverse = jnp.asarray(np.ascontiguousarray(full_table.T[order]).astype(jnp.bfloat16))
    rotation_response = jnp.transpose(
        rotation_response.reshape(rotations, 2, NANG // 2, 2), (0, 1, 3, 2)
    ).reshape(rotations, width)

    image_steps = block // ROWS
    ref_steps = classes // ROWS
    cube = (ROWS, NSHELL, width)

    image_hat, ref_hat, ids, slots = pl.pallas_call(
        transform_kernel,
        in_specs=[pl.BlockSpec(memory_space=pltpu.HBM)] * 5,
        out_specs=[vmem()] * 4,
        out_shape=[
            jax.ShapeDtypeStruct(images.shape, jnp.bfloat16),
            jax.ShapeDtypeStruct(references.shape, jnp.bfloat16),
            jax.ShapeDtypeStruct((8, block), jnp.int32),
            jax.ShapeDtypeStruct((dp_count, block), jnp.int32),
        ],
        scratch_shapes=[
            pltpu.VMEM(images.shape, jnp.bfloat16),
            pltpu.VMEM(references.shape, jnp.bfloat16),
            pltpu.VMEM((2, NANG, NANG), jnp.bfloat16),
            pltpu.VMEM((8, block), jnp.int32),
            pltpu.VMEM((dp_count, 8, block), jnp.int32),
            pltpu.SemaphoreType.DMA((image_steps + ref_steps,)),
            pltpu.SemaphoreType.DMA((3,)),
            pltpu.SemaphoreType.DMA((dp_count,)),
            pltpu.SemaphoreType.DMA((dp_count,)),
        ],
        compiler_params=remote(0, 36),
        name="transform",
    )(images, references, table, pose_slot[None, :], class_lists.T)

    def whole(shape):
        return pl.BlockSpec(shape, lambda i, c: (0,) * len(shape))

    image_spec = pl.BlockSpec(cube, lambda i, c: (i, 0, 0))

    def plain(mebibytes):
        return pltpu.CompilerParams(
            dimension_semantics=("arbitrary",), vmem_limit_bytes=mebibytes * MIB
        )

    scores, stats, head, nxt = pl.pallas_call(
        score_kernel,
        grid_spec=pltpu.PrefetchScalarGridSpec(
            num_scalar_prefetch=1,
            grid=(image_steps,),
            in_specs=[
                image_spec,
                whole((classes, NSHELL, width)),
                whole((1, NSHELL)),
                whole((rotations, width)),
                whole((1, classes)),
            ],
            out_specs=[
                whole((entries, LANES)),
                whole((8, block)),
                pl.BlockSpec(memory_space=pltpu.SMEM),
                pl.BlockSpec(memory_space=pltpu.SMEM),
            ],
            scratch_shapes=[
                pltpu.VMEM((entries, width), jnp.float32),
                pltpu.VMEM((entries, LANES), jnp.float32),
                pltpu.VMEM((LANES, width), jnp.float32),
                pltpu.VMEM((classes, LANES), jnp.float32),
                pltpu.VMEM((NSHELL, NANG), jnp.float32),
                pltpu.SMEM((ROWS * LIST + 1,), jnp.int32),
            ],
        ),
        out_shape=[
            jax.ShapeDtypeStruct((entries, LANES), jnp.float32),
            jax.ShapeDtypeStruct((8, block), jnp.float32),
            jax.ShapeDtypeStruct((classes,), jnp.int32),
            jax.ShapeDtypeStruct((entries,), jnp.int32),
        ],
        compiler_params=plain(24),
        name="scores",
    )(ids, image_hat, ref_hat, shell_weight[None, :], rotation_response, class_counts[None, :])

    coef, post_sum, evidence = pl.pallas_call(
        posterior_kernel,
        in_specs=[vmem()] * 3,
        out_specs=[vmem()] * 3,
        out_shape=[
            jax.ShapeDtypeStruct((entries, 3 * NANG), jnp.float32),
            jax.ShapeDtypeStruct((entries, LANES), jnp.float32),
            jax.ShapeDtypeStruct((1, block), jnp.float32),
        ],
        scratch_shapes=[
            pltpu.VMEM((columns, 8, block), jnp.float32),
            pltpu.VMEM((LANES, 3 * NANG), jnp.float32),
            pltpu.SemaphoreType.DMA((columns,)),
            pltpu.SemaphoreType.DMA((columns,)),
        ],
        compiler_params=remote(1, 8),
        name="posterior",
    )(scores, stats, rotation_response)

    some = (8, NSHELL, width)

    def listed_whole(shape):
        return pl.BlockSpec(shape, lambda i, h, n: (0,) * len(shape))

    part, weight = pl.pallas_call(
        grad_kernel,
        grid_spec=pltpu.PrefetchScalarGridSpec(
            num_scalar_prefetch=2,
            grid=(classes // 8,),
            in_specs=[
                vmem(),
                pl.BlockSpec(some, lambda i, h, n: (i, 0, 0)),
                listed_whole((entries, 3 * NANG)),
                listed_whole((entries, LANES)),
            ],
            out_specs=[
                pl.BlockSpec(some, lambda i, h, n: (i, 0, 0)),
                pl.BlockSpec((8, LANES), lambda i, h, n: (i, 0)),
            ],
        ),
        out_shape=[
            jax.ShapeDtypeStruct((classes, NSHELL, width), jnp.bfloat16),
            jax.ShapeDtypeStruct((classes, LANES), jnp.float32),
        ],
        compiler_params=plain(24),
        name="gradient",
    )(head, nxt, image_hat, ref_hat, coef, post_sum)

    scaled, log_evidence = reduce_scatter(part, weight, evidence, slots, dp_count)
    result = jnp.dot(
        scaled.reshape(-1, width), inverse, preferred_element_type=jnp.float32
    )
    return (result.reshape((1,) + scaled.shape), log_evidence)


def solution(mesh):
    return jax.shard_map(
        local,
        mesh=mesh,
        in_specs=(
            P("dp", None, None),
            P("dp"),
            P("cls", None, None),
            P(),
            P(),
            P("dp", None),
            P("cls"),
        ),
        out_specs=(P("cls", "dp", None, None), P("dp")),
        check_vma=False,
    )
```

```python
import functools
import math

import jax
import jax.numpy as jnp
import numpy as np
from jax import lax
from jax.experimental import pallas as pl
from jax.experimental.pallas import tpu as pltpu
from jax.sharding import PartitionSpec as P

NSHELL = 64
NANG = 256
LIST = 2
LANES = 128
ROWS = 16
MESH = pl.DeviceIdType.MESH
HIGHEST = lax.Precision.HIGHEST
MIB = 1024 * 1024


def angular_tables(points):
    positions = np.arange(points)
    angles = (positions[:, None] * positions[None, :] % points).astype(np.float64) * (
        2.0 * math.pi / points
    )
    cosine = np.cos(angles) / math.sqrt(points)
    sine_part = np.sin(angles) / math.sqrt(points)
    upper_half = np.concatenate([cosine, -sine_part], axis=1)
    lower_half = np.concatenate([sine_part, cosine], axis=1)
    return np.concatenate([upper_half, lower_half], axis=0).astype(np.float32)


def everyone(axis):
    me, count = lax.axis_index(axis), lax.axis_size(axis)

    def peer(step):
        return lax.rem(me + step, count)

    return me, count, peer


def greet(axis):
    _, count, peer = everyone(axis)
    barrier = pltpu.get_barrier_semaphore()

    def one(step, carry):
        pl.semaphore_signal(barrier, inc=1, device_id={axis: peer(step)}, device_id_type=MESH)
        return carry

    lax.fori_loop(1, count, one, 0)


def greeted(axis):
    pl.semaphore_wait(pltpu.get_barrier_semaphore(), lax.axis_size(axis) - 1)


def share(axis, src, dst, send, recv):
    me, count, peer = everyone(axis)

    def outgoing(step):
        return pltpu.make_async_remote_copy(
            src_ref=src(peer(step)), dst_ref=dst.at[me],
            send_sem=send.at[peer(step)], recv_sem=recv.at[me],
            device_id={axis: peer(step)}, device_id_type=MESH,
        )

    def incoming(step):
        return pltpu.make_async_remote_copy(
            src_ref=src(peer(step)), dst_ref=dst.at[peer(step)],
            send_sem=send.at[peer(step)], recv_sem=recv.at[peer(step)],
            device_id={axis: peer(step)}, device_id_type=MESH,
        )

    def loop(act):
        def one(step, carry):
            act(step)
            return carry

        lax.fori_loop(1, count, one, 0)

    return (
        lambda: loop(lambda step: outgoing(step).start()),
        lambda: loop(lambda step: incoming(step).wait_recv()),
        lambda: loop(lambda step: outgoing(step).wait_send()),
    )


def transform_kernel(
    image_ref, refs_ref, table_hbm, slot_ref, lists_ref,
    image_out, refs_out, ids_out, slots_out,
    image_in, refs_in, table_ref, tags_ref, all_tags, block_sems, small_sems, send, recv,
):
    start, arrive, sent = share("dp", lambda _: tags_ref, all_tags, send, recv)
    me = lax.axis_index("dp")
    count = lax.axis_size("dp")
    block = tags_ref.shape[1]
    classes = refs_ref.shape[0]
    image_steps = image_ref.shape[0] // ROWS
    half = NANG // 2

    def rows_of(i):
        return pl.ds(pl.multiple_of(i * ROWS, ROWS), ROWS)

    def fetch_image(i):
        return pltpu.make_async_copy(
            image_ref.at[rows_of(i)], image_in.at[rows_of(i)], block_sems.at[i]
        )

    def fetch_refs(i):
        return pltpu.make_async_copy(
            refs_ref.at[rows_of(i)], refs_in.at[rows_of(i)], block_sems.at[image_steps + i]
        )

    small = (
        pltpu.make_async_copy(table_hbm, table_ref, small_sems.at[0]),
        pltpu.make_async_copy(slot_ref, tags_ref.at[pl.ds(0, 1)], small_sems.at[1]),
        pltpu.make_async_copy(lists_ref, tags_ref.at[pl.ds(1, LIST)], small_sems.at[2]),
    )

    def multiply(source, target, i):
        block_rows = source[rows_of(i)].reshape(ROWS * NSHELL, 2 * NANG)
        re_low, re_high, im_low, im_high = (
            block_rows[:, n * half : (n + 1) * half] for n in range(4)
        )
        plus = jnp.concatenate([re_low + re_high, im_low + im_high], axis=1)
        minus = jnp.concatenate([re_low - re_high, im_low - im_high], axis=1)
        for n, mixed in enumerate((plus, minus)):
            out = jnp.dot(mixed, table_ref[n], preferred_element_type=jnp.float32)
            out = out.astype(jnp.bfloat16).reshape(ROWS, NSHELL, NANG)
            target[rows_of(i), :, n * half : (n + 1) * half] = out[:, :, :half]
            target[rows_of(i), :, NANG + n * half : NANG + (n + 1) * half] = out[:, :, half:]

    def loop(low, high, act):
        def one(i, carry):
            act(i)
            return carry

        lax.fori_loop(low, high, one, 0)

    def image_step(i):
        fetch_image(i).wait()
        multiply(image_in, image_out, i)

    def refs_step(i):
        fetch_refs(i).wait()
        multiply(refs_in, refs_out, i)

    small[0].start()
    loop(0, 2, lambda i: fetch_image(i).start())
    small[1].start()
    small[2].start()
    loop(2, image_steps, lambda i: fetch_image(i).start())
    loop(0, classes // ROWS, lambda i: fetch_refs(i).start())
    greet("dp")
    small[0].wait()
    loop(0, image_steps // 2, image_step)
    small[1].wait()
    small[2].wait()
    greeted("dp")
    start()
    loop(image_steps // 2, image_steps, image_step)
    loop(0, classes // ROWS, refs_step)

    arrive()
    all_tags[me] = tags_ref[...]
    own = tags_ref[0:1, :].astype(jnp.float32)
    slot = jnp.transpose(jnp.broadcast_to(own, (LANES, block))).astype(jnp.int32)
    lane = lax.broadcasted_iota(jnp.int32, (block, block), 1)

    def look(d, found):
        rows = all_tags[d]
        hit = slot == lane + d * block
        slots_out[pl.ds(d, 1), :] = rows[0:1]
        return tuple(
            total + jnp.where(hit, rows[1 + a : 2 + a], 0) for a, total in enumerate(found)
        )

    found = lax.fori_loop(0, count, look, (jnp.zeros((block, block), jnp.int32),) * LIST)
    column = lax.axis_index("cls")
    ids_out[...] = jnp.zeros_like(ids_out)
    for a in range(LIST):
        total = jnp.sum(found[a].astype(jnp.float32), axis=1, keepdims=True)
        row = jnp.transpose(jnp.broadcast_to(total, (block, LANES)))[0:1]
        ids_out[a : a + 1, :] = row.astype(jnp.int32) - column * classes
    sent()


def listed(ids_ref, chosen, step, classes):
    count = jnp.int32(0)
    for i in range(ROWS * LIST):
        k = ids_ref[i % LIST, step * ROWS + i // LIST]
        chosen[count] = i
        count = count + jnp.where((k >= 0) & (k < classes), 1, 0)
    return count


def score_kernel(
    ids_ref, xh_ref, rh_ref, shells_ref, rr_ref, counts_ref,
    scores_ref, stats_ref, head, nxt, cross, bias, response, prior_ref, sw_ref, chosen,
):
    step = pl.program_id(0)
    block = ids_ref.shape[1]
    classes = rh_ref.shape[0]
    rotations = rr_ref.shape[0]

    @pl.when(step == 0)
    def _():
        cross[...] = jnp.zeros_like(cross)
        bias[...] = jnp.full_like(bias, -1e30)
        response[...] = jnp.zeros_like(response)
        response[:rotations] = rr_ref[...]
        row = jnp.log1p(counts_ref[...].astype(jnp.float32))
        prior_ref[...] = jnp.transpose(jnp.broadcast_to(row, (LANES, classes)))
        sw_ref[...] = jnp.transpose(jnp.broadcast_to(shells_ref[...], (NANG, NSHELL)))

        def clear(k, carry):
            head[k] = -1
            return carry

        lax.fori_loop(0, classes, clear, 0, unroll=True)

    def entry(n, carry):
        i = chosen[n]
        p = lax.div(i, LIST)
        a = lax.rem(i, LIST)
        row = a * block + step * ROWS + p
        k = ids_ref[a, step * ROWS + p]
        nxt[row] = head[k]
        head[k] = row
        bias[pl.ds(row, 1), :] = prior_ref[pl.ds(k, 1), :]
        re = jnp.zeros((8, NANG), jnp.float32)
        im = jnp.zeros((8, NANG), jnp.float32)
        for j in range(0, NSHELL, ROWS):
            x = xh_ref[p, j : j + ROWS].astype(jnp.float32)
            c = rh_ref[k, j : j + ROWS].astype(jnp.float32)
            sw = sw_ref[j : j + ROWS]
            x_re, x_im, c_re, c_im = x[:, :NANG], x[:, NANG:], c[:, :NANG], c[:, NANG:]
            one = (x_re * c_re + x_im * c_im) * sw
            two = (x_im * c_re - x_re * c_im) * sw
            re = re + one[:8] + one[8:]
            im = im + two[:8] + two[8:]
        cross[pl.ds(row, 1), :NANG] = jnp.sum(re, axis=0, keepdims=True)
        cross[pl.ds(row, 1), NANG:] = jnp.sum(im, axis=0, keepdims=True)
        return carry

    lax.fori_loop(0, listed(ids_ref, chosen, step, classes), entry, 0)

    @pl.when(step == pl.num_programs(0) - 1)
    def _():
        lane = lax.broadcasted_iota(jnp.int32, (block, LANES), 1)
        scores = lax.dot_general(
            cross[...],
            response[...],
            (((1,), (1,)), ((), ())),
            precision=HIGHEST,
            preferred_element_type=jnp.float32,
        ) + bias[...]
        first = jnp.where(lane < rotations, scores[:block], -1e30)
        second = jnp.where(lane < rotations, scores[block:], -1e30)
        scores_ref[:block] = first
        scores_ref[block:] = second
        top = jnp.max(jnp.maximum(first, second), axis=1, keepdims=True)
        total = jnp.sum(jnp.exp(first - top) + jnp.exp(second - top), axis=1, keepdims=True)
        stats = jnp.where(lane == 0, top, total)
        stats_ref[...] = jnp.transpose(stats)[:8]


def posterior_kernel(
    scores_ref, stats_ref, rr_ref, coef_ref, post_ref, evid_ref, all_stats, table, send, recv
):
    start, arrive, sent = share("cls", lambda _: stats_ref, all_stats, send, recv)
    block = scores_ref.shape[0] // LIST
    rotations = rr_ref.shape[0]
    greet("cls")
    table[...] = jnp.zeros_like(table)
    rot_re = rr_ref[:, :NANG]
    rot_im = rr_ref[:, NANG:]
    table[:rotations, :NANG] = rot_re
    table[:rotations, NANG : 2 * NANG] = -rot_im
    table[:rotations, 2 * NANG :] = rot_re * rot_re + rot_im * rot_im
    greeted("cls")
    start()
    all_stats[lax.axis_index("cls")] = stats_ref[...]
    arrive()
    stats = all_stats[...]
    tops = stats[:, 0:1, :]
    top = jnp.max(tops, axis=0)
    total = jnp.sum(stats[:, 1:2, :] * jnp.exp(tops - top[None]), axis=0)
    evid_ref[...] = top + jnp.log(total)
    top_col = jnp.transpose(jnp.broadcast_to(top, (LANES, block)))
    total_col = jnp.transpose(jnp.broadcast_to(total, (LANES, block)))
    for a in range(LIST):
        rows = slice(a * block, (a + 1) * block)
        posterior = jnp.exp(scores_ref[rows] - top_col) / total_col
        post_ref[rows] = jnp.broadcast_to(
            jnp.sum(posterior, axis=1, keepdims=True), (block, LANES)
        )
        coef_ref[rows] = jnp.dot(
            posterior, table[...], precision=HIGHEST, preferred_element_type=jnp.float32
        )
    sent()


def grad_kernel(head, nxt, xh_ref, rh_ref, coef, post_sum, part_ref, weight_ref):
    step = pl.program_id(0)
    block = xh_ref.shape[0]
    per_step = rh_ref.shape[0]
    pieces = [slice(j, j + ROWS) for j in range(0, NSHELL, ROWS)]

    def one_class(c, carry):
        def more(state):
            return state[0] >= 0

        def add(state):
            row, vol, weight, g_re, g_im = state
            p = lax.rem(row, block)
            re = coef[pl.ds(row, 1), :NANG]
            im = coef[pl.ds(row, 1), NANG : 2 * NANG]
            new_re, new_im = [], []
            for rows, one, two in zip(pieces, g_re, g_im):
                x_re = xh_ref[p, rows, :NANG].astype(jnp.float32)
                x_im = xh_ref[p, rows, NANG:].astype(jnp.float32)
                new_re.append(one + (x_re * re - x_im * im))
                new_im.append(two + (x_re * im + x_im * re))
            return (
                nxt[row],
                vol + coef[pl.ds(row, 1), 2 * NANG :],
                weight + post_sum[pl.ds(row, 1), :],
                tuple(new_re),
                tuple(new_im),
            )

        zeros = (jnp.zeros((ROWS, NANG), jnp.float32),) * len(pieces)
        _, vol, weight, g_re, g_im = lax.while_loop(
            more,
            add,
            (
                head[step * per_step + c],
                jnp.zeros((1, NANG), jnp.float32),
                jnp.zeros((1, LANES), jnp.float32),
                zeros,
                zeros,
            ),
        )
        weight_ref[pl.ds(c, 1), :] = weight
        for rows, one, two in zip(pieces, g_re, g_im):
            c_re = rh_ref[c, rows, :NANG].astype(jnp.float32)
            c_im = rh_ref[c, rows, NANG:].astype(jnp.float32)
            part_ref[c, rows, :NANG] = (one - vol * c_re).astype(jnp.bfloat16)
            part_ref[c, rows, NANG:] = (two - vol * c_im).astype(jnp.bfloat16)
        return carry

    lax.fori_loop(0, per_step, one_class, 0)


def reduce_kernel(
    lines, groups, early, p_ref, weight_ref, evid_ref, slots_ref, out_ref, log_ref,
    held, from_left, from_right, weights, evids, scale,
    both, both_left, both_right, swapped,
    pair_send, pair_recv, right_send, right_recv, left_send, left_recv,
    weight_send, weight_recv, evid_send, evid_recv,
    first_sems, swap_sems,
):
    me = lax.axis_index("dp")
    x = lax.rem(me, 2)
    z = lax.div(me, 2)
    partner = me + 1 - 2 * x
    has_left = z > 0
    has_right = z < lines - 1

    weight_start, weight_arrive, weight_sent = share(
        "dp", lambda d: weight_ref.at[d], weights, weight_send, weight_recv
    )
    evid_start, evid_arrive, evid_sent = share(
        "dp", lambda _: evid_ref, evids, evid_send, evid_recv
    )

    def some(g):
        first, size = groups[g]
        return pl.ds(first, size)

    def pair(b, g):
        return pltpu.make_async_remote_copy(
            src_ref=p_ref.at[b, 1 - x, some(g)], dst_ref=held.at[b, some(g)],
            send_sem=pair_send.at[b, g], recv_sem=pair_recv.at[b, g],
            device_id={"dp": partner}, device_id_type=MESH,
        )

    def right(b, g):
        return pltpu.make_async_remote_copy(
            src_ref=held.at[b, some(g)], dst_ref=from_left.at[b, some(g)],
            send_sem=right_send.at[b, g], recv_sem=right_recv.at[b, g],
            device_id={"dp": me + 2}, device_id_type=MESH,
        )

    def left(b, g):
        return pltpu.make_async_remote_copy(
            src_ref=held.at[b, some(g)], dst_ref=from_right.at[b, some(g)],
            send_sem=left_send.at[b, g], recv_sem=left_recv.at[b, g],
            device_id={"dp": me - 2}, device_id_type=MESH,
        )

    def both_to_right(b):
        return pltpu.make_async_remote_copy(
            src_ref=both.at[b], dst_ref=both_left.at[b],
            send_sem=first_sems.at[0, b], recv_sem=first_sems.at[1, b],
            device_id={"dp": me + 2}, device_id_type=MESH,
        )

    def both_to_left(b):
        return pltpu.make_async_remote_copy(
            src_ref=both.at[b], dst_ref=both_right.at[b],
            send_sem=first_sems.at[2, b], recv_sem=first_sems.at[3, b],
            device_id={"dp": me - 2}, device_id_type=MESH,
        )

    def swap():
        return pltpu.make_async_remote_copy(
            src_ref=both.at[z, 1 - x], dst_ref=swapped,
            send_sem=swap_sems.at[0], recv_sem=swap_sems.at[1],
            device_id={"dp": partner}, device_id_type=MESH,
        )

    def both_own(b):
        for side in range(2):
            both[b, side] = p_ref[b, side, early]

    def both_add(b, other):
        for side in range(2):
            both[b, side] = (
                both[b, side].astype(jnp.float32) + other[b, side].astype(jnp.float32)
            ).astype(jnp.bfloat16)

    def both_ends(b, _):
        @pl.when((z < b) & jnp.logical_not(has_left))
        def _():
            both_own(b)
            both_to_right(b).start()

        @pl.when((z > b) & jnp.logical_not(has_right))
        def _():
            both_own(b)
            both_to_left(b).start()

    def both_relay(b, _):
        @pl.when((z < b) & has_left)
        def _():
            both_own(b)
            both_to_right(b).wait_recv()
            both_add(b, both_left)
            both_to_right(b).start()

        @pl.when((z > b) & has_right)
        def _():
            both_own(b)
            both_to_left(b).wait_recv()
            both_add(b, both_right)
            both_to_left(b).start()

    def both_swap():
        both_own(z)

        @pl.when(has_left)
        def _():
            both_to_right(z).wait_recv()
            both_add(z, both_left)

        @pl.when(has_right)
        def _():
            both_to_left(z).wait_recv()
            both_add(z, both_right)

        swap().start()

    def both_finish():
        swap().wait_recv()
        out_ref[early] = (
            (both[z, x].astype(jnp.float32) + swapped[...].astype(jnp.float32))
            * scale[early : early + 1, :]
        ).astype(jnp.bfloat16)

    def both_drain(b, _):
        @pl.when(z < b)
        def _():
            both_to_right(b).wait_send()

        @pl.when(z > b)
        def _():
            both_to_left(b).wait_send()

    def add(b, g, other):
        first, size = groups[g]
        for c in range(first, first + size):
            held[b, c] = (
                held[b, c].astype(jnp.float32) + other(c).astype(jnp.float32)
            ).astype(jnp.bfloat16)

    def each(g, act):
        def one(i, carry):
            odd, half = lax.rem(i, 2), lax.div(i, 2)
            act((1 - odd) * (lines - 1 - half) + odd * half, g)
            return carry

        lax.fori_loop(0, lines, one, 0)

    def relay(b, g):
        pair(b, g).wait_recv()
        add(b, g, lambda c: p_ref[b, x, c])

        @pl.when(z < b)
        def _():
            @pl.when(has_left)
            def _():
                right(b, g).wait_recv()
                add(b, g, lambda c: from_left[b, c])

            right(b, g).start()

        @pl.when(z > b)
        def _():
            @pl.when(has_right)
            def _():
                left(b, g).wait_recv()
                add(b, g, lambda c: from_right[b, c])

            left(b, g).start()

    def small():
        count = weights.shape[0]
        weight_arrive()
        evid_arrive()
        weights[me] = weight_ref[me]
        evids[me] = evid_ref[...]
        block = evid_ref.shape[1]
        mine = me * block + lax.broadcasted_iota(jnp.int32, (block, block), 0)

        def look(d, total):
            return total + jnp.where(slots_ref[pl.ds(d, 1), :] == mine, evids[d], 0.0)

        found = lax.fori_loop(0, count, look, jnp.zeros((block, block), jnp.float32))
        summed = jnp.sum(found, axis=1, keepdims=True)
        log_ref[...] = jnp.transpose(jnp.broadcast_to(summed, (block, LANES)))[0:1]
        inverse = 1.0 / (1.0 + jnp.sum(weights[...], axis=0))
        for n in range(2 * NANG // LANES):
            scale[:, n * LANES : (n + 1) * LANES] = inverse

    def finish(g):
        @pl.when(has_left)
        def _():
            right(z, g).wait_recv()
            add(z, g, lambda c: from_left[z, c])

        @pl.when(has_right)
        def _():
            left(z, g).wait_recv()
            add(z, g, lambda c: from_right[z, c])

        first, size = groups[g]
        for c in range(first, first + size):
            out_ref[c] = (held[z, c].astype(jnp.float32) * scale[c : c + 1, :]).astype(
                jnp.bfloat16
            )

    greet("dp")
    greeted("dp")
    last = len(groups) - 1
    each(0, lambda b, g: pair(b, g).start())
    if early is not None:
        each(0, both_ends)
    weight_start()
    evid_start()
    for n in range(1, len(groups)):
        each(n, lambda b, g: pair(b, g).start())
    for n in range(last):
        each(n, relay)
        if early is not None and n == 0:
            each(0, both_relay)
        if early is not None and n == last - 1:
            both_swap()
    small()
    each(last, relay)
    if early is not None:
        both_finish()
    for n in range(len(groups)):
        finish(n)

    def drain(b, g):
        pair(b, g).wait_send()

        @pl.when(z < b)
        def _():
            right(b, g).wait_send()

        @pl.when(z > b)
        def _():
            left(b, g).wait_send()

    for n in range(len(groups)):
        each(n, drain)
    if early is not None:
        each(0, both_drain)
        swap().wait_send()
    weight_sent()
    evid_sent()


def vmem():
    return pl.BlockSpec(memory_space=pltpu.VMEM)


def remote(collective_id, mebibytes):
    return pltpu.CompilerParams(
        collective_id=collective_id, has_side_effects=True, vmem_limit_bytes=mebibytes * MIB
    )


def reduce_scatter(part, weight, evidence, slots, dp_count):
    classes = part.shape[0]
    block = evidence.shape[1]
    lines = dp_count // 2
    owned = classes // dp_count
    shape = part.shape[1:]
    whole = pltpu.VMEM((lines, owned) + shape, jnp.bfloat16)
    groups, first = [], 0
    early = owned - 1 if owned >= 8 and lines > 1 else None
    stop = owned if early is None else early
    while first < stop:
        size = 2 if stop - first > 1 else 1
        groups.append((first, size))
        first += size
    sems = pltpu.SemaphoreType.DMA((lines, len(groups)))
    row_sems = pltpu.SemaphoreType.DMA((dp_count,))
    out, log_evidence = pl.pallas_call(
        functools.partial(reduce_kernel, lines, tuple(groups), early),
        out_shape=[
            jax.ShapeDtypeStruct((owned,) + shape, jnp.bfloat16),
            jax.ShapeDtypeStruct((1, block), jnp.float32),
        ],
        in_specs=[vmem()] * 4,
        out_specs=[vmem()] * 2,
        scratch_shapes=[
            whole, whole, whole,
            pltpu.VMEM((dp_count, owned, LANES), jnp.float32),
            pltpu.VMEM((dp_count, 1, block), jnp.float32),
            pltpu.VMEM((owned, 2 * NANG), jnp.float32),
            pltpu.VMEM((lines, 2) + shape, jnp.bfloat16),
            pltpu.VMEM((lines, 2) + shape, jnp.bfloat16),
            pltpu.VMEM((lines, 2) + shape, jnp.bfloat16),
            pltpu.VMEM(shape, jnp.bfloat16),
        ]
        + [sems] * 6
        + [row_sems] * 4
        + [pltpu.SemaphoreType.DMA((4, lines)), pltpu.SemaphoreType.DMA((2,))],
        compiler_params=remote(2, 20),
        name="reduce_over_dp",
    )(
        part.reshape((lines, 2, owned) + shape),
        weight.reshape(dp_count, owned, LANES),
        evidence,
        slots,
    )
    return out, log_evidence[0]


def local(
    images, pose_slot, references, rotation_response, shell_weight, class_lists, class_counts
):
    dp_count = lax.axis_size("dp")
    columns = lax.axis_size("cls")
    block = images.shape[0]
    classes = references.shape[0]
    width = 2 * NANG
    entries = block * LIST
    rotations = rotation_response.shape[0]
    full_table = angular_tables(NANG)
    parity = np.concatenate([np.arange(0, NANG, 2), np.arange(1, NANG, 2)])
    order = np.concatenate([parity, NANG + parity])
    low = np.concatenate([np.arange(NANG // 2), NANG + np.arange(NANG // 2)])
    evens = np.concatenate([np.arange(0, NANG, 2), NANG + np.arange(0, NANG, 2)])
    table = jnp.asarray(
        np.stack([full_table[np.ix_(low, evens + n)] for n in range(2)]).astype(jnp.bfloat16)
    )
    inverse = jnp.asarray(np.ascontiguousarray(full_table.T[order]).astype(jnp.bfloat16))
    rotation_response = jnp.transpose(
        rotation_response.reshape(rotations, 2, NANG // 2, 2), (0, 1, 3, 2)
    ).reshape(rotations, width)

    image_steps = block // ROWS
    ref_steps = classes // ROWS
    cube = (ROWS, NSHELL, width)

    image_hat, ref_hat, ids, slots = pl.pallas_call(
        transform_kernel,
        in_specs=[pl.BlockSpec(memory_space=pltpu.HBM)] * 5,
        out_specs=[vmem()] * 4,
        out_shape=[
            jax.ShapeDtypeStruct(images.shape, jnp.bfloat16),
            jax.ShapeDtypeStruct(references.shape, jnp.bfloat16),
            jax.ShapeDtypeStruct((8, block), jnp.int32),
            jax.ShapeDtypeStruct((dp_count, block), jnp.int32),
        ],
        scratch_shapes=[
            pltpu.VMEM(images.shape, jnp.bfloat16),
            pltpu.VMEM(references.shape, jnp.bfloat16),
            pltpu.VMEM((2, NANG, NANG), jnp.bfloat16),
            pltpu.VMEM((8, block), jnp.int32),
            pltpu.VMEM((dp_count, 8, block), jnp.int32),
            pltpu.SemaphoreType.DMA((image_steps + ref_steps,)),
            pltpu.SemaphoreType.DMA((3,)),
            pltpu.SemaphoreType.DMA((dp_count,)),
            pltpu.SemaphoreType.DMA((dp_count,)),
        ],
        compiler_params=remote(0, 36),
        name="transform",
    )(images, references, table, pose_slot[None, :], class_lists.T)

    def whole(shape):
        return pl.BlockSpec(shape, lambda i, c: (0,) * len(shape))

    image_spec = pl.BlockSpec(cube, lambda i, c: (i, 0, 0))

    def plain(mebibytes):
        return pltpu.CompilerParams(
            dimension_semantics=("arbitrary",), vmem_limit_bytes=mebibytes * MIB
        )

    scores, stats, head, nxt = pl.pallas_call(
        score_kernel,
        grid_spec=pltpu.PrefetchScalarGridSpec(
            num_scalar_prefetch=1,
            grid=(image_steps,),
            in_specs=[
                image_spec,
                whole((classes, NSHELL, width)),
                whole((1, NSHELL)),
                whole((rotations, width)),
                whole((1, classes)),
            ],
            out_specs=[
                whole((entries, LANES)),
                whole((8, block)),
                pl.BlockSpec(memory_space=pltpu.SMEM),
                pl.BlockSpec(memory_space=pltpu.SMEM),
            ],
            scratch_shapes=[
                pltpu.VMEM((entries, width), jnp.float32),
                pltpu.VMEM((entries, LANES), jnp.float32),
                pltpu.VMEM((LANES, width), jnp.float32),
                pltpu.VMEM((classes, LANES), jnp.float32),
                pltpu.VMEM((NSHELL, NANG), jnp.float32),
                pltpu.SMEM((ROWS * LIST + 1,), jnp.int32),
            ],
        ),
        out_shape=[
            jax.ShapeDtypeStruct((entries, LANES), jnp.float32),
            jax.ShapeDtypeStruct((8, block), jnp.float32),
            jax.ShapeDtypeStruct((classes,), jnp.int32),
            jax.ShapeDtypeStruct((entries,), jnp.int32),
        ],
        compiler_params=plain(24),
        name="scores",
    )(ids, image_hat, ref_hat, shell_weight[None, :], rotation_response, class_counts[None, :])

    coef, post_sum, evidence = pl.pallas_call(
        posterior_kernel,
        in_specs=[vmem()] * 3,
        out_specs=[vmem()] * 3,
        out_shape=[
            jax.ShapeDtypeStruct((entries, 3 * NANG), jnp.float32),
            jax.ShapeDtypeStruct((entries, LANES), jnp.float32),
            jax.ShapeDtypeStruct((1, block), jnp.float32),
        ],
        scratch_shapes=[
            pltpu.VMEM((columns, 8, block), jnp.float32),
            pltpu.VMEM((LANES, 3 * NANG), jnp.float32),
            pltpu.SemaphoreType.DMA((columns,)),
            pltpu.SemaphoreType.DMA((columns,)),
        ],
        compiler_params=remote(1, 8),
        name="posterior",
    )(scores, stats, rotation_response)

    some = (8, NSHELL, width)

    def listed_whole(shape):
        return pl.BlockSpec(shape, lambda i, h, n: (0,) * len(shape))

    part, weight = pl.pallas_call(
        grad_kernel,
        grid_spec=pltpu.PrefetchScalarGridSpec(
            num_scalar_prefetch=2,
            grid=(classes // 8,),
            in_specs=[
                vmem(),
                pl.BlockSpec(some, lambda i, h, n: (i, 0, 0)),
                listed_whole((entries, 3 * NANG)),
                listed_whole((entries, LANES)),
            ],
            out_specs=[
                pl.BlockSpec(some, lambda i, h, n: (i, 0, 0)),
                pl.BlockSpec((8, LANES), lambda i, h, n: (i, 0)),
            ],
        ),
        out_shape=[
            jax.ShapeDtypeStruct((classes, NSHELL, width), jnp.bfloat16),
            jax.ShapeDtypeStruct((classes, LANES), jnp.float32),
        ],
        compiler_params=plain(24),
        name="gradient",
    )(head, nxt, image_hat, ref_hat, coef, post_sum)

    scaled, log_evidence = reduce_scatter(part, weight, evidence, slots, dp_count)
    result = jnp.dot(
        scaled.reshape(-1, width), inverse, preferred_element_type=jnp.float32
    )
    return (result.reshape((1,) + scaled.shape), log_evidence)


def solution(mesh):
    return jax.shard_map(
        local,
        mesh=mesh,
        in_specs=(
            P("dp", None, None),
            P("dp"),
            P("cls", None, None),
            P(),
            P(),
            P("dp", None),
            P("cls"),
        ),
        out_specs=(P("cls", "dp", None, None), P("dp")),
        check_vma=False,
    )
```

```python
import functools
import math

import jax
import jax.numpy as jnp
import numpy as np
from jax import lax
from jax.experimental import pallas as pl
from jax.experimental.pallas import tpu as pltpu
from jax.sharding import PartitionSpec as P

NSHELL = 64
NANG = 256
LIST = 2
LANES = 128
ROWS = 16
MESH = pl.DeviceIdType.MESH
HIGHEST = lax.Precision.HIGHEST
MIB = 1024 * 1024


def angular_tables(points):
    positions = np.arange(points)
    angles = (positions[:, None] * positions[None, :] % points).astype(np.float64) * (
        2.0 * math.pi / points
    )
    cosine = np.cos(angles) / math.sqrt(points)
    sine_part = np.sin(angles) / math.sqrt(points)
    upper_half = np.concatenate([cosine, -sine_part], axis=1)
    lower_half = np.concatenate([sine_part, cosine], axis=1)
    return np.concatenate([upper_half, lower_half], axis=0).astype(np.float32)


def everyone(axis):
    me, count = lax.axis_index(axis), lax.axis_size(axis)

    def peer(step):
        return lax.rem(me + step, count)

    return me, count, peer


def greet(axis):
    _, count, peer = everyone(axis)
    barrier = pltpu.get_barrier_semaphore()

    def one(step, carry):
        pl.semaphore_signal(barrier, inc=1, device_id={axis: peer(step)}, device_id_type=MESH)
        return carry

    lax.fori_loop(1, count, one, 0)


def greeted(axis):
    pl.semaphore_wait(pltpu.get_barrier_semaphore(), lax.axis_size(axis) - 1)


def share(axis, src, dst, send, recv):
    me, count, peer = everyone(axis)

    def outgoing(step):
        return pltpu.make_async_remote_copy(
            src_ref=src(peer(step)), dst_ref=dst.at[me],
            send_sem=send.at[peer(step)], recv_sem=recv.at[me],
            device_id={axis: peer(step)}, device_id_type=MESH,
        )

    def incoming(step):
        return pltpu.make_async_remote_copy(
            src_ref=src(peer(step)), dst_ref=dst.at[peer(step)],
            send_sem=send.at[peer(step)], recv_sem=recv.at[peer(step)],
            device_id={axis: peer(step)}, device_id_type=MESH,
        )

    def loop(act):
        def one(step, carry):
            act(step)
            return carry

        lax.fori_loop(1, count, one, 0)

    return (
        lambda: loop(lambda step: outgoing(step).start()),
        lambda: loop(lambda step: incoming(step).wait_recv()),
        lambda: loop(lambda step: outgoing(step).wait_send()),
    )


def transform_kernel(
    image_ref, refs_ref, table_hbm, slot_ref, lists_ref,
    image_out, refs_out, ids_out, slots_out,
    image_in, refs_in, table_ref, tags_ref, all_tags, block_sems, small_sems, send, recv,
):
    start, arrive, sent = share("dp", lambda _: tags_ref, all_tags, send, recv)
    me = lax.axis_index("dp")
    count = lax.axis_size("dp")
    block = tags_ref.shape[1]
    classes = refs_ref.shape[0]
    image_steps = image_ref.shape[0] // ROWS
    half = NANG // 2

    def rows_of(i):
        return pl.ds(pl.multiple_of(i * ROWS, ROWS), ROWS)

    def fetch_image(i):
        return pltpu.make_async_copy(
            image_ref.at[rows_of(i)], image_in.at[rows_of(i)], block_sems.at[i]
        )

    def fetch_refs(i):
        return pltpu.make_async_copy(
            refs_ref.at[rows_of(i)], refs_in.at[rows_of(i)], block_sems.at[image_steps + i]
        )

    small = (
        pltpu.make_async_copy(table_hbm, table_ref, small_sems.at[0]),
        pltpu.make_async_copy(slot_ref, tags_ref.at[pl.ds(0, 1)], small_sems.at[1]),
        pltpu.make_async_copy(lists_ref, tags_ref.at[pl.ds(1, LIST)], small_sems.at[2]),
    )

    def multiply(source, target, i):
        block_rows = source[rows_of(i)].reshape(ROWS * NSHELL, 2 * NANG)
        re_low, re_high, im_low, im_high = (
            block_rows[:, n * half : (n + 1) * half] for n in range(4)
        )
        plus = jnp.concatenate([re_low + re_high, im_low + im_high], axis=1)
        minus = jnp.concatenate([re_low - re_high, im_low - im_high], axis=1)
        for n, mixed in enumerate((plus, minus)):
            out = jnp.dot(mixed, table_ref[n], preferred_element_type=jnp.float32)
            out = out.astype(jnp.bfloat16).reshape(ROWS, NSHELL, NANG)
            target[rows_of(i), :, n * half : (n + 1) * half] = out[:, :, :half]
            target[rows_of(i), :, NANG + n * half : NANG + (n + 1) * half] = out[:, :, half:]

    def loop(low, high, act):
        def one(i, carry):
            act(i)
            return carry

        lax.fori_loop(low, high, one, 0)

    def image_step(i):
        fetch_image(i).wait()
        multiply(image_in, image_out, i)

    def refs_step(i):
        fetch_refs(i).wait()
        multiply(refs_in, refs_out, i)

    small[0].start()
    loop(0, 2, lambda i: fetch_image(i).start())
    small[1].start()
    small[2].start()
    loop(2, image_steps, lambda i: fetch_image(i).start())
    loop(0, classes // ROWS, lambda i: fetch_refs(i).start())
    greet("dp")
    small[0].wait()
    loop(0, image_steps // 2, image_step)
    small[1].wait()
    small[2].wait()
    greeted("dp")
    start()
    loop(image_steps // 2, image_steps, image_step)
    loop(0, classes // ROWS, refs_step)

    arrive()
    all_tags[me] = tags_ref[...]
    own = tags_ref[0:1, :].astype(jnp.float32)
    slot = jnp.transpose(jnp.broadcast_to(own, (LANES, block))).astype(jnp.int32)
    lane = lax.broadcasted_iota(jnp.int32, (block, block), 1)

    def look(d, found):
        rows = all_tags[d]
        hit = slot == lane + d * block
        slots_out[pl.ds(d, 1), :] = rows[0:1]
        return tuple(
            total + jnp.where(hit, rows[1 + a : 2 + a], 0) for a, total in enumerate(found)
        )

    found = lax.fori_loop(0, count, look, (jnp.zeros((block, block), jnp.int32),) * LIST)
    column = lax.axis_index("cls")
    ids_out[...] = jnp.zeros_like(ids_out)
    for a in range(LIST):
        total = jnp.sum(found[a].astype(jnp.float32), axis=1, keepdims=True)
        row = jnp.transpose(jnp.broadcast_to(total, (block, LANES)))[0:1]
        ids_out[a : a + 1, :] = row.astype(jnp.int32) - column * classes
    sent()


def listed(ids_ref, chosen, step, classes):
    count = jnp.int32(0)
    for i in range(ROWS * LIST):
        k = ids_ref[i % LIST, step * ROWS + i // LIST]
        chosen[count] = i
        count = count + jnp.where((k >= 0) & (k < classes), 1, 0)
    return count


def score_kernel(
    ids_ref, xh_ref, rh_ref, shells_ref, rr_ref, counts_ref,
    scores_ref, stats_ref, head, nxt, cross, bias, response, prior_ref, sw_ref, chosen,
):
    step = pl.program_id(0)
    block = ids_ref.shape[1]
    classes = rh_ref.shape[0]
    rotations = rr_ref.shape[0]

    @pl.when(step == 0)
    def _():
        cross[...] = jnp.zeros_like(cross)
        bias[...] = jnp.full_like(bias, -1e30)
        response[...] = jnp.zeros_like(response)
        response[:rotations] = rr_ref[...]
        row = jnp.log1p(counts_ref[...].astype(jnp.float32))
        prior_ref[...] = jnp.transpose(jnp.broadcast_to(row, (LANES, classes)))
        sw_ref[...] = jnp.transpose(jnp.broadcast_to(shells_ref[...], (NANG, NSHELL)))

        def clear(k, carry):
            head[k] = -1
            return carry

        lax.fori_loop(0, classes, clear, 0, unroll=True)

    def entry(n, carry):
        i = chosen[n]
        p = lax.div(i, LIST)
        a = lax.rem(i, LIST)
        row = a * block + step * ROWS + p
        k = ids_ref[a, step * ROWS + p]
        nxt[row] = head[k]
        head[k] = row
        bias[pl.ds(row, 1), :] = prior_ref[pl.ds(k, 1), :]
        re = jnp.zeros((8, NANG), jnp.float32)
        im = jnp.zeros((8, NANG), jnp.float32)
        for j in range(0, NSHELL, ROWS):
            x = xh_ref[p, j : j + ROWS].astype(jnp.float32)
            c = rh_ref[k, j : j + ROWS].astype(jnp.float32)
            sw = sw_ref[j : j + ROWS]
            x_re, x_im, c_re, c_im = x[:, :NANG], x[:, NANG:], c[:, :NANG], c[:, NANG:]
            one = (x_re * c_re + x_im * c_im) * sw
            two = (x_im * c_re - x_re * c_im) * sw
            re = re + one[:8] + one[8:]
            im = im + two[:8] + two[8:]
        cross[pl.ds(row, 1), :NANG] = jnp.sum(re, axis=0, keepdims=True)
        cross[pl.ds(row, 1), NANG:] = jnp.sum(im, axis=0, keepdims=True)
        return carry

    lax.fori_loop(0, listed(ids_ref, chosen, step, classes), entry, 0)

    @pl.when(step == pl.num_programs(0) - 1)
    def _():
        lane = lax.broadcasted_iota(jnp.int32, (block, LANES), 1)
        scores = lax.dot_general(
            cross[...],
            response[...],
            (((1,), (1,)), ((), ())),
            precision=HIGHEST,
            preferred_element_type=jnp.float32,
        ) + bias[...]
        first = jnp.where(lane < rotations, scores[:block], -1e30)
        second = jnp.where(lane < rotations, scores[block:], -1e30)
        scores_ref[:block] = first
        scores_ref[block:] = second
        top = jnp.max(jnp.maximum(first, second), axis=1, keepdims=True)
        total = jnp.sum(jnp.exp(first - top) + jnp.exp(second - top), axis=1, keepdims=True)
        stats = jnp.where(lane == 0, top, total)
        stats_ref[...] = jnp.transpose(stats)[:8]


def posterior_kernel(
    scores_ref, stats_ref, rr_ref, coef_ref, post_ref, evid_ref, all_stats, table, send, recv
):
    start, arrive, sent = share("cls", lambda _: stats_ref, all_stats, send, recv)
    block = scores_ref.shape[0] // LIST
    rotations = rr_ref.shape[0]
    greet("cls")
    table[...] = jnp.zeros_like(table)
    rot_re = rr_ref[:, :NANG]
    rot_im = rr_ref[:, NANG:]
    table[:rotations, :NANG] = rot_re
    table[:rotations, NANG : 2 * NANG] = -rot_im
    table[:rotations, 2 * NANG :] = rot_re * rot_re + rot_im * rot_im
    greeted("cls")
    start()
    all_stats[lax.axis_index("cls")] = stats_ref[...]
    arrive()
    stats = all_stats[...]
    tops = stats[:, 0:1, :]
    top = jnp.max(tops, axis=0)
    total = jnp.sum(stats[:, 1:2, :] * jnp.exp(tops - top[None]), axis=0)
    evid_ref[...] = top + jnp.log(total)
    top_col = jnp.transpose(jnp.broadcast_to(top, (LANES, block)))
    total_col = jnp.transpose(jnp.broadcast_to(total, (LANES, block)))
    for a in range(LIST):
        rows = slice(a * block, (a + 1) * block)
        posterior = jnp.exp(scores_ref[rows] - top_col) / total_col
        post_ref[rows] = jnp.broadcast_to(
            jnp.sum(posterior, axis=1, keepdims=True), (block, LANES)
        )
        coef_ref[rows] = jnp.dot(
            posterior, table[...], precision=HIGHEST, preferred_element_type=jnp.float32
        )
    sent()


def grad_kernel(head, nxt, xh_ref, rh_ref, coef, post_sum, part_ref, weight_ref):
    step = pl.program_id(0)
    block = xh_ref.shape[0]
    per_step = rh_ref.shape[0]
    pieces = [slice(j, j + ROWS) for j in range(0, NSHELL, ROWS)]

    def one_class(c, carry):
        def more(state):
            return state[0] >= 0

        def add(state):
            row, vol, weight, g_re, g_im = state
            p = lax.rem(row, block)
            re = coef[pl.ds(row, 1), :NANG]
            im = coef[pl.ds(row, 1), NANG : 2 * NANG]
            new_re, new_im = [], []
            for rows, one, two in zip(pieces, g_re, g_im):
                x_re = xh_ref[p, rows, :NANG].astype(jnp.float32)
                x_im = xh_ref[p, rows, NANG:].astype(jnp.float32)
                new_re.append(one + (x_re * re - x_im * im))
                new_im.append(two + (x_re * im + x_im * re))
            return (
                nxt[row],
                vol + coef[pl.ds(row, 1), 2 * NANG :],
                weight + post_sum[pl.ds(row, 1), :],
                tuple(new_re),
                tuple(new_im),
            )

        zeros = (jnp.zeros((ROWS, NANG), jnp.float32),) * len(pieces)
        _, vol, weight, g_re, g_im = lax.while_loop(
            more,
            add,
            (
                head[step * per_step + c],
                jnp.zeros((1, NANG), jnp.float32),
                jnp.zeros((1, LANES), jnp.float32),
                zeros,
                zeros,
            ),
        )
        weight_ref[pl.ds(c, 1), :] = weight
        for rows, one, two in zip(pieces, g_re, g_im):
            c_re = rh_ref[c, rows, :NANG].astype(jnp.float32)
            c_im = rh_ref[c, rows, NANG:].astype(jnp.float32)
            part_ref[c, rows, :NANG] = (one - vol * c_re).astype(jnp.bfloat16)
            part_ref[c, rows, NANG:] = (two - vol * c_im).astype(jnp.bfloat16)
        return carry

    lax.fori_loop(0, per_step, one_class, 0)


def reduce_kernel(
    lines, groups, p_ref, weight_ref, evid_ref, slots_ref, out_ref, log_ref,
    held, from_left, from_right, weights, evids, scale,
    pair_send, pair_recv, right_send, right_recv, left_send, left_recv,
    weight_send, weight_recv, evid_send, evid_recv,
):
    me = lax.axis_index("dp")
    x = lax.rem(me, 2)
    z = lax.div(me, 2)
    partner = me + 1 - 2 * x
    has_left = z > 0
    has_right = z < lines - 1

    weight_start, weight_arrive, weight_sent = share(
        "dp", lambda d: weight_ref.at[d], weights, weight_send, weight_recv
    )
    evid_start, evid_arrive, evid_sent = share(
        "dp", lambda _: evid_ref, evids, evid_send, evid_recv
    )

    def some(g):
        first, size = groups[g]
        return pl.ds(first, size)

    def pair(b, g):
        return pltpu.make_async_remote_copy(
            src_ref=p_ref.at[b, 1 - x, some(g)], dst_ref=held.at[b, some(g)],
            send_sem=pair_send.at[b, g], recv_sem=pair_recv.at[b, g],
            device_id={"dp": partner}, device_id_type=MESH,
        )

    def right(b, g):
        return pltpu.make_async_remote_copy(
            src_ref=held.at[b, some(g)], dst_ref=from_left.at[b, some(g)],
            send_sem=right_send.at[b, g], recv_sem=right_recv.at[b, g],
            device_id={"dp": me + 2}, device_id_type=MESH,
        )

    def left(b, g):
        return pltpu.make_async_remote_copy(
            src_ref=held.at[b, some(g)], dst_ref=from_right.at[b, some(g)],
            send_sem=left_send.at[b, g], recv_sem=left_recv.at[b, g],
            device_id={"dp": me - 2}, device_id_type=MESH,
        )

    def add(b, g, other):
        first, size = groups[g]
        for c in range(first, first + size):
            held[b, c] = (
                held[b, c].astype(jnp.float32) + other(c).astype(jnp.float32)
            ).astype(jnp.bfloat16)

    def each(g, act):
        def one(i, carry):
            odd, half = lax.rem(i, 2), lax.div(i, 2)
            act((1 - odd) * (lines - 1 - half) + odd * half, g)
            return carry

        lax.fori_loop(0, lines, one, 0)

    def relay(b, g):
        pair(b, g).wait_recv()
        add(b, g, lambda c: p_ref[b, x, c])

        @pl.when(z < b)
        def _():
            @pl.when(has_left)
            def _():
                right(b, g).wait_recv()
                add(b, g, lambda c: from_left[b, c])

            right(b, g).start()

        @pl.when(z > b)
        def _():
            @pl.when(has_right)
            def _():
                left(b, g).wait_recv()
                add(b, g, lambda c: from_right[b, c])

            left(b, g).start()

    def small():
        count = weights.shape[0]
        weight_arrive()
        evid_arrive()
        weights[me] = weight_ref[me]
        evids[me] = evid_ref[...]
        block = evid_ref.shape[1]
        mine = me * block + lax.broadcasted_iota(jnp.int32, (block, block), 0)

        def look(d, total):
            return total + jnp.where(slots_ref[pl.ds(d, 1), :] == mine, evids[d], 0.0)

        found = lax.fori_loop(0, count, look, jnp.zeros((block, block), jnp.float32))
        summed = jnp.sum(found, axis=1, keepdims=True)
        log_ref[...] = jnp.transpose(jnp.broadcast_to(summed, (block, LANES)))[0:1]
        inverse = 1.0 / (1.0 + jnp.sum(weights[...], axis=0))
        for n in range(2 * NANG // LANES):
            scale[:, n * LANES : (n + 1) * LANES] = inverse

    def finish(g):
        @pl.when(has_left)
        def _():
            right(z, g).wait_recv()
            add(z, g, lambda c: from_left[z, c])

        @pl.when(has_right)
        def _():
            left(z, g).wait_recv()
            add(z, g, lambda c: from_right[z, c])

        first, size = groups[g]
        for c in range(first, first + size):
            out_ref[c] = (held[z, c].astype(jnp.float32) * scale[c : c + 1, :]).astype(
                jnp.bfloat16
            )

    greet("dp")
    greeted("dp")
    last = len(groups) - 1
    each(0, lambda b, g: pair(b, g).start())
    weight_start()
    evid_start()
    for n in range(1, len(groups)):
        each(n, lambda b, g: pair(b, g).start())
    for n in range(last):
        each(n, relay)
    small()
    each(last, relay)
    for n in range(len(groups)):
        finish(n)

    def drain(b, g):
        pair(b, g).wait_send()

        @pl.when(z < b)
        def _():
            right(b, g).wait_send()

        @pl.when(z > b)
        def _():
            left(b, g).wait_send()

    for n in range(len(groups)):
        each(n, drain)
    weight_sent()
    evid_sent()


def vmem():
    return pl.BlockSpec(memory_space=pltpu.VMEM)


def remote(collective_id, mebibytes):
    return pltpu.CompilerParams(
        collective_id=collective_id, has_side_effects=True, vmem_limit_bytes=mebibytes * MIB
    )


def reduce_scatter(part, weight, evidence, slots, dp_count):
    classes = part.shape[0]
    block = evidence.shape[1]
    lines = dp_count // 2
    owned = classes // dp_count
    shape = part.shape[1:]
    whole = pltpu.VMEM((lines, owned) + shape, jnp.bfloat16)
    groups, first = [], 0
    while first < owned:
        size = min(2, owned - first)
        groups.append((first, size))
        first += size
    sems = pltpu.SemaphoreType.DMA((lines, len(groups)))
    row_sems = pltpu.SemaphoreType.DMA((dp_count,))
    out, log_evidence = pl.pallas_call(
        functools.partial(reduce_kernel, lines, tuple(groups)),
        out_shape=[
            jax.ShapeDtypeStruct((owned,) + shape, jnp.bfloat16),
            jax.ShapeDtypeStruct((1, block), jnp.float32),
        ],
        in_specs=[vmem()] * 4,
        out_specs=[vmem()] * 2,
        scratch_shapes=[
            whole, whole, whole,
            pltpu.VMEM((dp_count, owned, LANES), jnp.float32),
            pltpu.VMEM((dp_count, 1, block), jnp.float32),
            pltpu.VMEM((owned, 2 * NANG), jnp.float32),
        ]
        + [sems] * 6
        + [row_sems] * 4,
        compiler_params=remote(2, 20),
        name="reduce_over_dp",
    )(
        part.reshape((lines, 2, owned) + shape),
        weight.reshape(dp_count, owned, LANES),
        evidence,
        slots,
    )
    return out, log_evidence[0]


def local(
    images, pose_slot, references, rotation_response, shell_weight, class_lists, class_counts
):
    dp_count = lax.axis_size("dp")
    columns = lax.axis_size("cls")
    block = images.shape[0]
    classes = references.shape[0]
    width = 2 * NANG
    entries = block * LIST
    rotations = rotation_response.shape[0]
    full_table = angular_tables(NANG)
    parity = np.concatenate([np.arange(0, NANG, 2), np.arange(1, NANG, 2)])
    order = np.concatenate([parity, NANG + parity])
    low = np.concatenate([np.arange(NANG // 2), NANG + np.arange(NANG // 2)])
    evens = np.concatenate([np.arange(0, NANG, 2), NANG + np.arange(0, NANG, 2)])
    table = jnp.asarray(
        np.stack([full_table[np.ix_(low, evens + n)] for n in range(2)]).astype(jnp.bfloat16)
    )
    inverse = jnp.asarray(np.ascontiguousarray(full_table.T[order]).astype(jnp.bfloat16))
    rotation_response = jnp.transpose(
        rotation_response.reshape(rotations, 2, NANG // 2, 2), (0, 1, 3, 2)
    ).reshape(rotations, width)

    image_steps = block // ROWS
    ref_steps = classes // ROWS
    cube = (ROWS, NSHELL, width)

    image_hat, ref_hat, ids, slots = pl.pallas_call(
        transform_kernel,
        in_specs=[pl.BlockSpec(memory_space=pltpu.HBM)] * 5,
        out_specs=[vmem()] * 4,
        out_shape=[
            jax.ShapeDtypeStruct(images.shape, jnp.bfloat16),
            jax.ShapeDtypeStruct(references.shape, jnp.bfloat16),
            jax.ShapeDtypeStruct((8, block), jnp.int32),
            jax.ShapeDtypeStruct((dp_count, block), jnp.int32),
        ],
        scratch_shapes=[
            pltpu.VMEM(images.shape, jnp.bfloat16),
            pltpu.VMEM(references.shape, jnp.bfloat16),
            pltpu.VMEM((2, NANG, NANG), jnp.bfloat16),
            pltpu.VMEM((8, block), jnp.int32),
            pltpu.VMEM((dp_count, 8, block), jnp.int32),
            pltpu.SemaphoreType.DMA((image_steps + ref_steps,)),
            pltpu.SemaphoreType.DMA((3,)),
            pltpu.SemaphoreType.DMA((dp_count,)),
            pltpu.SemaphoreType.DMA((dp_count,)),
        ],
        compiler_params=remote(0, 36),
        name="transform",
    )(images, references, table, pose_slot[None, :], class_lists.T)

    def whole(shape):
        return pl.BlockSpec(shape, lambda i, c: (0,) * len(shape))

    image_spec = pl.BlockSpec(cube, lambda i, c: (i, 0, 0))

    def plain(mebibytes):
        return pltpu.CompilerParams(
            dimension_semantics=("arbitrary",), vmem_limit_bytes=mebibytes * MIB
        )

    scores, stats, head, nxt = pl.pallas_call(
        score_kernel,
        grid_spec=pltpu.PrefetchScalarGridSpec(
            num_scalar_prefetch=1,
            grid=(image_steps,),
            in_specs=[
                image_spec,
                whole((classes, NSHELL, width)),
                whole((1, NSHELL)),
                whole((rotations, width)),
                whole((1, classes)),
            ],
            out_specs=[
                whole((entries, LANES)),
                whole((8, block)),
                pl.BlockSpec(memory_space=pltpu.SMEM),
                pl.BlockSpec(memory_space=pltpu.SMEM),
            ],
            scratch_shapes=[
                pltpu.VMEM((entries, width), jnp.float32),
                pltpu.VMEM((entries, LANES), jnp.float32),
                pltpu.VMEM((LANES, width), jnp.float32),
                pltpu.VMEM((classes, LANES), jnp.float32),
                pltpu.VMEM((NSHELL, NANG), jnp.float32),
                pltpu.SMEM((ROWS * LIST + 1,), jnp.int32),
            ],
        ),
        out_shape=[
            jax.ShapeDtypeStruct((entries, LANES), jnp.float32),
            jax.ShapeDtypeStruct((8, block), jnp.float32),
            jax.ShapeDtypeStruct((classes,), jnp.int32),
            jax.ShapeDtypeStruct((entries,), jnp.int32),
        ],
        compiler_params=plain(24),
        name="scores",
    )(ids, image_hat, ref_hat, shell_weight[None, :], rotation_response, class_counts[None, :])

    coef, post_sum, evidence = pl.pallas_call(
        posterior_kernel,
        in_specs=[vmem()] * 3,
        out_specs=[vmem()] * 3,
        out_shape=[
            jax.ShapeDtypeStruct((entries, 3 * NANG), jnp.float32),
            jax.ShapeDtypeStruct((entries, LANES), jnp.float32),
            jax.ShapeDtypeStruct((1, block), jnp.float32),
        ],
        scratch_shapes=[
            pltpu.VMEM((columns, 8, block), jnp.float32),
            pltpu.VMEM((LANES, 3 * NANG), jnp.float32),
            pltpu.SemaphoreType.DMA((columns,)),
            pltpu.SemaphoreType.DMA((columns,)),
        ],
        compiler_params=remote(1, 8),
        name="posterior",
    )(scores, stats, rotation_response)

    some = (8, NSHELL, width)

    def listed_whole(shape):
        return pl.BlockSpec(shape, lambda i, h, n: (0,) * len(shape))

    part, weight = pl.pallas_call(
        grad_kernel,
        grid_spec=pltpu.PrefetchScalarGridSpec(
            num_scalar_prefetch=2,
            grid=(classes // 8,),
            in_specs=[
                vmem(),
                pl.BlockSpec(some, lambda i, h, n: (i, 0, 0)),
                listed_whole((entries, 3 * NANG)),
                listed_whole((entries, LANES)),
            ],
            out_specs=[
                pl.BlockSpec(some, lambda i, h, n: (i, 0, 0)),
                pl.BlockSpec((8, LANES), lambda i, h, n: (i, 0)),
            ],
        ),
        out_shape=[
            jax.ShapeDtypeStruct((classes, NSHELL, width), jnp.bfloat16),
            jax.ShapeDtypeStruct((classes, LANES), jnp.float32),
        ],
        compiler_params=plain(24),
        name="gradient",
    )(head, nxt, image_hat, ref_hat, coef, post_sum)

    scaled, log_evidence = reduce_scatter(part, weight, evidence, slots, dp_count)
    result = jnp.dot(
        scaled.reshape(-1, width), inverse, preferred_element_type=jnp.float32
    )
    return (result.reshape((1,) + scaled.shape), log_evidence)


def solution(mesh):
    return jax.shard_map(
        local,
        mesh=mesh,
        in_specs=(
            P("dp", None, None),
            P("dp"),
            P("cls", None, None),
            P(),
            P(),
            P("dp", None),
            P("cls"),
        ),
        out_specs=(P("cls", "dp", None, None), P("dp")),
        check_vma=False,
    )
```

```python
import functools
import math

import jax
import jax.numpy as jnp
import numpy as np
from jax import lax
from jax.experimental import pallas as pl
from jax.experimental.pallas import tpu as pltpu
from jax.sharding import PartitionSpec as P

NSHELL = 64
NANG = 256
LIST = 2
LANES = 128
ROWS = 16
MESH = pl.DeviceIdType.MESH
HIGHEST = lax.Precision.HIGHEST
MIB = 1024 * 1024


def angular_tables(points):
    positions = np.arange(points)
    angles = (positions[:, None] * positions[None, :] % points).astype(np.float64) * (
        2.0 * math.pi / points
    )
    cosine = np.cos(angles) / math.sqrt(points)
    sine_part = np.sin(angles) / math.sqrt(points)
    upper_half = np.concatenate([cosine, -sine_part], axis=1)
    lower_half = np.concatenate([sine_part, cosine], axis=1)
    return np.concatenate([upper_half, lower_half], axis=0).astype(np.float32)


def everyone(axis):
    me, count = lax.axis_index(axis), lax.axis_size(axis)

    def peer(step):
        return lax.rem(me + step, count)

    return me, count, peer


def greet(axis):
    _, count, peer = everyone(axis)
    barrier = pltpu.get_barrier_semaphore()

    def one(step, carry):
        pl.semaphore_signal(barrier, inc=1, device_id={axis: peer(step)}, device_id_type=MESH)
        return carry

    lax.fori_loop(1, count, one, 0)


def greeted(axis):
    pl.semaphore_wait(pltpu.get_barrier_semaphore(), lax.axis_size(axis) - 1)


def share(axis, src, dst, send, recv):
    me, count, peer = everyone(axis)

    def outgoing(step):
        return pltpu.make_async_remote_copy(
            src_ref=src(peer(step)), dst_ref=dst.at[me],
            send_sem=send.at[peer(step)], recv_sem=recv.at[me],
            device_id={axis: peer(step)}, device_id_type=MESH,
        )

    def incoming(step):
        return pltpu.make_async_remote_copy(
            src_ref=src(peer(step)), dst_ref=dst.at[peer(step)],
            send_sem=send.at[peer(step)], recv_sem=recv.at[peer(step)],
            device_id={axis: peer(step)}, device_id_type=MESH,
        )

    def loop(act):
        def one(step, carry):
            act(step)
            return carry

        lax.fori_loop(1, count, one, 0)

    return (
        lambda: loop(lambda step: outgoing(step).start()),
        lambda: loop(lambda step: incoming(step).wait_recv()),
        lambda: loop(lambda step: outgoing(step).wait_send()),
    )


def transform_kernel(
    image_ref, refs_ref, table_hbm, slot_ref, lists_ref,
    image_out, refs_out, ids_out, slots_out,
    image_in, refs_in, table_ref, tags_ref, all_tags, block_sems, small_sems, send, recv,
):
    start, arrive, sent = share("dp", lambda _: tags_ref, all_tags, send, recv)
    me = lax.axis_index("dp")
    count = lax.axis_size("dp")
    block = tags_ref.shape[1]
    classes = refs_ref.shape[0]
    image_steps = image_ref.shape[0] // ROWS
    half = NANG // 2

    def rows_of(i):
        return pl.ds(pl.multiple_of(i * ROWS, ROWS), ROWS)

    def fetch_image(i):
        return pltpu.make_async_copy(
            image_ref.at[rows_of(i)], image_in.at[rows_of(i)], block_sems.at[i]
        )

    def fetch_refs(i):
        return pltpu.make_async_copy(
            refs_ref.at[rows_of(i)], refs_in.at[rows_of(i)], block_sems.at[image_steps + i]
        )

    small = (
        pltpu.make_async_copy(table_hbm, table_ref, small_sems.at[0]),
        pltpu.make_async_copy(slot_ref, tags_ref.at[pl.ds(0, 1)], small_sems.at[1]),
        pltpu.make_async_copy(lists_ref, tags_ref.at[pl.ds(1, LIST)], small_sems.at[2]),
    )

    def multiply(source, target, i):
        block_rows = source[rows_of(i)].reshape(ROWS * NSHELL, 2 * NANG)
        re_low, re_high, im_low, im_high = (
            block_rows[:, n * half : (n + 1) * half] for n in range(4)
        )
        plus = jnp.concatenate([re_low + re_high, im_low + im_high], axis=1)
        minus = jnp.concatenate([re_low - re_high, im_low - im_high], axis=1)
        for n, mixed in enumerate((plus, minus)):
            out = jnp.dot(mixed, table_ref[n], preferred_element_type=jnp.float32)
            out = out.astype(jnp.bfloat16).reshape(ROWS, NSHELL, NANG)
            target[rows_of(i), :, n * half : (n + 1) * half] = out[:, :, :half]
            target[rows_of(i), :, NANG + n * half : NANG + (n + 1) * half] = out[:, :, half:]

    def loop(low, high, act):
        def one(i, carry):
            act(i)
            return carry

        lax.fori_loop(low, high, one, 0)

    def image_step(i):
        fetch_image(i).wait()
        multiply(image_in, image_out, i)

    def refs_step(i):
        fetch_refs(i).wait()
        multiply(refs_in, refs_out, i)

    small[0].start()
    loop(0, 2, lambda i: fetch_image(i).start())
    small[1].start()
    small[2].start()
    loop(2, image_steps, lambda i: fetch_image(i).start())
    loop(0, classes // ROWS, lambda i: fetch_refs(i).start())
    greet("dp")
    small[0].wait()
    loop(0, image_steps // 2, image_step)
    small[1].wait()
    small[2].wait()
    greeted("dp")
    start()
    loop(image_steps // 2, image_steps, image_step)
    loop(0, classes // ROWS, refs_step)

    arrive()
    all_tags[me] = tags_ref[...]
    own = tags_ref[0:1, :].astype(jnp.float32)
    slot = jnp.transpose(jnp.broadcast_to(own, (LANES, block))).astype(jnp.int32)
    lane = lax.broadcasted_iota(jnp.int32, (block, block), 1)

    def look(d, found):
        rows = all_tags[d]
        hit = slot == lane + d * block
        slots_out[pl.ds(d, 1), :] = rows[0:1]
        return tuple(
            total + jnp.where(hit, rows[1 + a : 2 + a], 0) for a, total in enumerate(found)
        )

    found = lax.fori_loop(0, count, look, (jnp.zeros((block, block), jnp.int32),) * LIST)
    column = lax.axis_index("cls")
    ids_out[...] = jnp.zeros_like(ids_out)
    for a in range(LIST):
        total = jnp.sum(found[a].astype(jnp.float32), axis=1, keepdims=True)
        row = jnp.transpose(jnp.broadcast_to(total, (block, LANES)))[0:1]
        ids_out[a : a + 1, :] = row.astype(jnp.int32) - column * classes
    sent()


def listed(ids_ref, chosen, step, classes):
    count = jnp.int32(0)
    for i in range(ROWS * LIST):
        k = ids_ref[i % LIST, step * ROWS + i // LIST]
        chosen[count] = i
        count = count + jnp.where((k >= 0) & (k < classes), 1, 0)
    return count


def score_kernel(
    ids_ref, xh_ref, rh_ref, shells_ref, rr_ref, counts_ref,
    scores_ref, stats_ref, head, nxt, cross, bias, response, prior_ref, sw_ref, chosen,
):
    step = pl.program_id(0)
    block = ids_ref.shape[1]
    classes = rh_ref.shape[0]
    rotations = rr_ref.shape[0]

    @pl.when(step == 0)
    def _():
        cross[...] = jnp.zeros_like(cross)
        bias[...] = jnp.full_like(bias, -1e30)
        response[...] = jnp.zeros_like(response)
        response[:rotations] = rr_ref[...]
        row = jnp.log1p(counts_ref[...].astype(jnp.float32))
        prior_ref[...] = jnp.transpose(jnp.broadcast_to(row, (LANES, classes)))
        sw_ref[...] = jnp.transpose(jnp.broadcast_to(shells_ref[...], (NANG, NSHELL)))

        def clear(k, carry):
            head[k] = -1
            return carry

        lax.fori_loop(0, classes, clear, 0, unroll=True)

    def entry(n, carry):
        i = chosen[n]
        p = lax.div(i, LIST)
        a = lax.rem(i, LIST)
        row = a * block + step * ROWS + p
        k = ids_ref[a, step * ROWS + p]
        nxt[row] = head[k]
        head[k] = row
        bias[pl.ds(row, 1), :] = prior_ref[pl.ds(k, 1), :]
        re = jnp.zeros((8, NANG), jnp.float32)
        im = jnp.zeros((8, NANG), jnp.float32)
        for j in range(0, NSHELL, ROWS):
            x = xh_ref[p, j : j + ROWS].astype(jnp.float32)
            c = rh_ref[k, j : j + ROWS].astype(jnp.float32)
            sw = sw_ref[j : j + ROWS]
            x_re, x_im, c_re, c_im = x[:, :NANG], x[:, NANG:], c[:, :NANG], c[:, NANG:]
            one = (x_re * c_re + x_im * c_im) * sw
            two = (x_im * c_re - x_re * c_im) * sw
            re = re + one[:8] + one[8:]
            im = im + two[:8] + two[8:]
        cross[pl.ds(row, 1), :NANG] = jnp.sum(re, axis=0, keepdims=True)
        cross[pl.ds(row, 1), NANG:] = jnp.sum(im, axis=0, keepdims=True)
        return carry

    lax.fori_loop(0, listed(ids_ref, chosen, step, classes), entry, 0)

    @pl.when(step == pl.num_programs(0) - 1)
    def _():
        lane = lax.broadcasted_iota(jnp.int32, (block, LANES), 1)
        scores = lax.dot_general(
            cross[...],
            response[...],
            (((1,), (1,)), ((), ())),
            precision=HIGHEST,
            preferred_element_type=jnp.float32,
        ) + bias[...]
        first = jnp.where(lane < rotations, scores[:block], -1e30)
        second = jnp.where(lane < rotations, scores[block:], -1e30)
        scores_ref[:block] = first
        scores_ref[block:] = second
        top = jnp.max(jnp.maximum(first, second), axis=1, keepdims=True)
        total = jnp.sum(jnp.exp(first - top) + jnp.exp(second - top), axis=1, keepdims=True)
        stats = jnp.where(lane == 0, top, total)
        stats_ref[...] = jnp.transpose(stats)[:8]


def posterior_kernel(
    scores_ref, stats_ref, rr_ref, coef_ref, post_ref, evid_ref, all_stats, table, send, recv
):
    start, arrive, sent = share("cls", lambda _: stats_ref, all_stats, send, recv)
    block = scores_ref.shape[0] // LIST
    rotations = rr_ref.shape[0]
    greet("cls")
    table[...] = jnp.zeros_like(table)
    rot_re = rr_ref[:, :NANG]
    rot_im = rr_ref[:, NANG:]
    table[:rotations, :NANG] = rot_re
    table[:rotations, NANG : 2 * NANG] = -rot_im
    table[:rotations, 2 * NANG :] = rot_re * rot_re + rot_im * rot_im
    greeted("cls")
    start()
    all_stats[lax.axis_index("cls")] = stats_ref[...]
    arrive()
    stats = all_stats[...]
    tops = stats[:, 0:1, :]
    top = jnp.max(tops, axis=0)
    total = jnp.sum(stats[:, 1:2, :] * jnp.exp(tops - top[None]), axis=0)
    evid_ref[...] = top + jnp.log(total)
    top_col = jnp.transpose(jnp.broadcast_to(top, (LANES, block)))
    total_col = jnp.transpose(jnp.broadcast_to(total, (LANES, block)))
    for a in range(LIST):
        rows = slice(a * block, (a + 1) * block)
        posterior = jnp.exp(scores_ref[rows] - top_col) / total_col
        post_ref[rows] = jnp.broadcast_to(
            jnp.sum(posterior, axis=1, keepdims=True), (block, LANES)
        )
        coef_ref[rows] = jnp.dot(
            posterior, table[...], precision=HIGHEST, preferred_element_type=jnp.float32
        )
    sent()


def grad_kernel(head, nxt, xh_ref, rh_ref, coef, post_sum, part_ref, weight_ref):
    step = pl.program_id(0)
    block = xh_ref.shape[0]
    per_step = rh_ref.shape[0]
    pieces = [slice(j, j + ROWS) for j in range(0, NSHELL, ROWS)]

    def one_class(c, carry):
        def more(state):
            return state[0] >= 0

        def add(state):
            row, vol, weight, g_re, g_im = state
            p = lax.rem(row, block)
            re = coef[pl.ds(row, 1), :NANG]
            im = coef[pl.ds(row, 1), NANG : 2 * NANG]
            new_re, new_im = [], []
            for rows, one, two in zip(pieces, g_re, g_im):
                x_re = xh_ref[p, rows, :NANG].astype(jnp.float32)
                x_im = xh_ref[p, rows, NANG:].astype(jnp.float32)
                new_re.append(one + (x_re * re - x_im * im))
                new_im.append(two + (x_re * im + x_im * re))
            return (
                nxt[row],
                vol + coef[pl.ds(row, 1), 2 * NANG :],
                weight + post_sum[pl.ds(row, 1), :],
                tuple(new_re),
                tuple(new_im),
            )

        zeros = (jnp.zeros((ROWS, NANG), jnp.float32),) * len(pieces)
        _, vol, weight, g_re, g_im = lax.while_loop(
            more,
            add,
            (
                head[step * per_step + c],
                jnp.zeros((1, NANG), jnp.float32),
                jnp.zeros((1, LANES), jnp.float32),
                zeros,
                zeros,
            ),
        )
        weight_ref[pl.ds(c, 1), :] = weight
        for rows, one, two in zip(pieces, g_re, g_im):
            c_re = rh_ref[c, rows, :NANG].astype(jnp.float32)
            c_im = rh_ref[c, rows, NANG:].astype(jnp.float32)
            part_ref[c, rows, :NANG] = (one - vol * c_re).astype(jnp.bfloat16)
            part_ref[c, rows, NANG:] = (two - vol * c_im).astype(jnp.bfloat16)
        return carry

    lax.fori_loop(0, per_step, one_class, 0)


def reduce_kernel(
    lines, groups, p_ref, weight_ref, evid_ref, slots_ref, out_ref, log_ref,
    held, from_left, from_right, weights, evids, scale,
    pair_send, pair_recv, right_send, right_recv, left_send, left_recv,
    weight_send, weight_recv, evid_send, evid_recv,
):
    me = lax.axis_index("dp")
    x = lax.rem(me, 2)
    z = lax.div(me, 2)
    partner = me + 1 - 2 * x
    has_left = z > 0
    has_right = z < lines - 1

    weight_start, weight_arrive, weight_sent = share(
        "dp", lambda d: weight_ref.at[d], weights, weight_send, weight_recv
    )
    evid_start, evid_arrive, evid_sent = share(
        "dp", lambda _: evid_ref, evids, evid_send, evid_recv
    )

    def some(g):
        first, size = groups[g]
        return pl.ds(first, size)

    def pair(b, g):
        return pltpu.make_async_remote_copy(
            src_ref=p_ref.at[b, 1 - x, some(g)], dst_ref=held.at[b, some(g)],
            send_sem=pair_send.at[b, g], recv_sem=pair_recv.at[b, g],
            device_id={"dp": partner}, device_id_type=MESH,
        )

    def right(b, g):
        return pltpu.make_async_remote_copy(
            src_ref=held.at[b, some(g)], dst_ref=from_left.at[b, some(g)],
            send_sem=right_send.at[b, g], recv_sem=right_recv.at[b, g],
            device_id={"dp": me + 2}, device_id_type=MESH,
        )

    def left(b, g):
        return pltpu.make_async_remote_copy(
            src_ref=held.at[b, some(g)], dst_ref=from_right.at[b, some(g)],
            send_sem=left_send.at[b, g], recv_sem=left_recv.at[b, g],
            device_id={"dp": me - 2}, device_id_type=MESH,
        )

    def add(b, g, other):
        first, size = groups[g]
        for c in range(first, first + size):
            held[b, c] = (
                held[b, c].astype(jnp.float32) + other(c).astype(jnp.float32)
            ).astype(jnp.bfloat16)

    def each(g, act):
        def one(i, carry):
            odd, half = lax.rem(i, 2), lax.div(i, 2)
            act((1 - odd) * (lines - 1 - half) + odd * half, g)
            return carry

        lax.fori_loop(0, lines, one, 0)

    def relay(b, g):
        pair(b, g).wait_recv()
        add(b, g, lambda c: p_ref[b, x, c])

        @pl.when(z < b)
        def _():
            @pl.when(has_left)
            def _():
                right(b, g).wait_recv()
                add(b, g, lambda c: from_left[b, c])

            right(b, g).start()

        @pl.when(z > b)
        def _():
            @pl.when(has_right)
            def _():
                left(b, g).wait_recv()
                add(b, g, lambda c: from_right[b, c])

            left(b, g).start()

    def small():
        count = weights.shape[0]
        weight_arrive()
        evid_arrive()
        weights[me] = weight_ref[me]
        evids[me] = evid_ref[...]
        block = evid_ref.shape[1]
        mine = me * block + lax.broadcasted_iota(jnp.int32, (block, block), 0)

        def look(d, total):
            return total + jnp.where(slots_ref[pl.ds(d, 1), :] == mine, evids[d], 0.0)

        found = lax.fori_loop(0, count, look, jnp.zeros((block, block), jnp.float32))
        summed = jnp.sum(found, axis=1, keepdims=True)
        log_ref[...] = jnp.transpose(jnp.broadcast_to(summed, (block, LANES)))[0:1]
        inverse = 1.0 / (1.0 + jnp.sum(weights[...], axis=0))
        for n in range(2 * NANG // LANES):
            scale[:, n * LANES : (n + 1) * LANES] = inverse

    def finish(g):
        @pl.when(has_left)
        def _():
            right(z, g).wait_recv()
            add(z, g, lambda c: from_left[z, c])

        @pl.when(has_right)
        def _():
            left(z, g).wait_recv()
            add(z, g, lambda c: from_right[z, c])

        first, size = groups[g]
        for c in range(first, first + size):
            out_ref[c] = (held[z, c].astype(jnp.float32) * scale[c : c + 1, :]).astype(
                jnp.bfloat16
            )

    greet("dp")
    greeted("dp")
    last = len(groups) - 1
    each(0, lambda b, g: pair(b, g).start())
    weight_start()
    evid_start()
    for n in range(1, len(groups)):
        each(n, lambda b, g: pair(b, g).start())
    for n in range(last):
        each(n, relay)
    small()
    each(last, relay)
    for n in range(len(groups)):
        finish(n)

    def drain(b, g):
        pair(b, g).wait_send()

        @pl.when(z < b)
        def _():
            right(b, g).wait_send()

        @pl.when(z > b)
        def _():
            left(b, g).wait_send()

    for n in range(len(groups)):
        each(n, drain)
    weight_sent()
    evid_sent()


def vmem():
    return pl.BlockSpec(memory_space=pltpu.VMEM)


def remote(collective_id, mebibytes):
    return pltpu.CompilerParams(
        collective_id=collective_id, has_side_effects=True, vmem_limit_bytes=mebibytes * MIB
    )


def reduce_scatter(part, weight, evidence, slots, dp_count):
    classes = part.shape[0]
    block = evidence.shape[1]
    lines = dp_count // 2
    owned = classes // dp_count
    shape = part.shape[1:]
    whole = pltpu.VMEM((lines, owned) + shape, jnp.bfloat16)
    groups, first = [], 0
    while first < owned:
        size = min(3, owned - first)
        groups.append((first, size))
        first += size
    sems = pltpu.SemaphoreType.DMA((lines, len(groups)))
    row_sems = pltpu.SemaphoreType.DMA((dp_count,))
    out, log_evidence = pl.pallas_call(
        functools.partial(reduce_kernel, lines, tuple(groups)),
        out_shape=[
            jax.ShapeDtypeStruct((owned,) + shape, jnp.bfloat16),
            jax.ShapeDtypeStruct((1, block), jnp.float32),
        ],
        in_specs=[vmem()] * 4,
        out_specs=[vmem()] * 2,
        scratch_shapes=[
            whole, whole, whole,
            pltpu.VMEM((dp_count, owned, LANES), jnp.float32),
            pltpu.VMEM((dp_count, 1, block), jnp.float32),
            pltpu.VMEM((owned, 2 * NANG), jnp.float32),
        ]
        + [sems] * 6
        + [row_sems] * 4,
        compiler_params=remote(2, 20),
        name="reduce_over_dp",
    )(
        part.reshape((lines, 2, owned) + shape),
        weight.reshape(dp_count, owned, LANES),
        evidence,
        slots,
    )
    return out, log_evidence[0]


def local(
    images, pose_slot, references, rotation_response, shell_weight, class_lists, class_counts
):
    dp_count = lax.axis_size("dp")
    columns = lax.axis_size("cls")
    block = images.shape[0]
    classes = references.shape[0]
    width = 2 * NANG
    entries = block * LIST
    rotations = rotation_response.shape[0]
    full_table = angular_tables(NANG)
    parity = np.concatenate([np.arange(0, NANG, 2), np.arange(1, NANG, 2)])
    order = np.concatenate([parity, NANG + parity])
    low = np.concatenate([np.arange(NANG // 2), NANG + np.arange(NANG // 2)])
    evens = np.concatenate([np.arange(0, NANG, 2), NANG + np.arange(0, NANG, 2)])
    table = jnp.asarray(
        np.stack([full_table[np.ix_(low, evens + n)] for n in range(2)]).astype(jnp.bfloat16)
    )
    inverse = jnp.asarray(np.ascontiguousarray(full_table.T[order]).astype(jnp.bfloat16))
    rotation_response = jnp.transpose(
        rotation_response.reshape(rotations, 2, NANG // 2, 2), (0, 1, 3, 2)
    ).reshape(rotations, width)

    image_steps = block // ROWS
    ref_steps = classes // ROWS
    cube = (ROWS, NSHELL, width)

    image_hat, ref_hat, ids, slots = pl.pallas_call(
        transform_kernel,
        in_specs=[pl.BlockSpec(memory_space=pltpu.HBM)] * 5,
        out_specs=[vmem()] * 4,
        out_shape=[
            jax.ShapeDtypeStruct(images.shape, jnp.bfloat16),
            jax.ShapeDtypeStruct(references.shape, jnp.bfloat16),
            jax.ShapeDtypeStruct((8, block), jnp.int32),
            jax.ShapeDtypeStruct((dp_count, block), jnp.int32),
        ],
        scratch_shapes=[
            pltpu.VMEM(images.shape, jnp.bfloat16),
            pltpu.VMEM(references.shape, jnp.bfloat16),
            pltpu.VMEM((2, NANG, NANG), jnp.bfloat16),
            pltpu.VMEM((8, block), jnp.int32),
            pltpu.VMEM((dp_count, 8, block), jnp.int32),
            pltpu.SemaphoreType.DMA((image_steps + ref_steps,)),
            pltpu.SemaphoreType.DMA((3,)),
            pltpu.SemaphoreType.DMA((dp_count,)),
            pltpu.SemaphoreType.DMA((dp_count,)),
        ],
        compiler_params=remote(0, 36),
        name="transform",
    )(images, references, table, pose_slot[None, :], class_lists.T)

    def whole(shape):
        return pl.BlockSpec(shape, lambda i, c: (0,) * len(shape))

    image_spec = pl.BlockSpec(cube, lambda i, c: (i, 0, 0))

    def plain(mebibytes):
        return pltpu.CompilerParams(
            dimension_semantics=("arbitrary",), vmem_limit_bytes=mebibytes * MIB
        )

    scores, stats, head, nxt = pl.pallas_call(
        score_kernel,
        grid_spec=pltpu.PrefetchScalarGridSpec(
            num_scalar_prefetch=1,
            grid=(image_steps,),
            in_specs=[
                image_spec,
                whole((classes, NSHELL, width)),
                whole((1, NSHELL)),
                whole((rotations, width)),
                whole((1, classes)),
            ],
            out_specs=[
                whole((entries, LANES)),
                whole((8, block)),
                pl.BlockSpec(memory_space=pltpu.SMEM),
                pl.BlockSpec(memory_space=pltpu.SMEM),
            ],
            scratch_shapes=[
                pltpu.VMEM((entries, width), jnp.float32),
                pltpu.VMEM((entries, LANES), jnp.float32),
                pltpu.VMEM((LANES, width), jnp.float32),
                pltpu.VMEM((classes, LANES), jnp.float32),
                pltpu.VMEM((NSHELL, NANG), jnp.float32),
                pltpu.SMEM((ROWS * LIST + 1,), jnp.int32),
            ],
        ),
        out_shape=[
            jax.ShapeDtypeStruct((entries, LANES), jnp.float32),
            jax.ShapeDtypeStruct((8, block), jnp.float32),
            jax.ShapeDtypeStruct((classes,), jnp.int32),
            jax.ShapeDtypeStruct((entries,), jnp.int32),
        ],
        compiler_params=plain(24),
        name="scores",
    )(ids, image_hat, ref_hat, shell_weight[None, :], rotation_response, class_counts[None, :])

    coef, post_sum, evidence = pl.pallas_call(
        posterior_kernel,
        in_specs=[vmem()] * 3,
        out_specs=[vmem()] * 3,
        out_shape=[
            jax.ShapeDtypeStruct((entries, 3 * NANG), jnp.float32),
            jax.ShapeDtypeStruct((entries, LANES), jnp.float32),
            jax.ShapeDtypeStruct((1, block), jnp.float32),
        ],
        scratch_shapes=[
            pltpu.VMEM((columns, 8, block), jnp.float32),
            pltpu.VMEM((LANES, 3 * NANG), jnp.float32),
            pltpu.SemaphoreType.DMA((columns,)),
            pltpu.SemaphoreType.DMA((columns,)),
        ],
        compiler_params=remote(1, 8),
        name="posterior",
    )(scores, stats, rotation_response)

    some = (8, NSHELL, width)

    def listed_whole(shape):
        return pl.BlockSpec(shape, lambda i, h, n: (0,) * len(shape))

    part, weight = pl.pallas_call(
        grad_kernel,
        grid_spec=pltpu.PrefetchScalarGridSpec(
            num_scalar_prefetch=2,
            grid=(classes // 8,),
            in_specs=[
                vmem(),
                pl.BlockSpec(some, lambda i, h, n: (i, 0, 0)),
                listed_whole((entries, 3 * NANG)),
                listed_whole((entries, LANES)),
            ],
            out_specs=[
                pl.BlockSpec(some, lambda i, h, n: (i, 0, 0)),
                pl.BlockSpec((8, LANES), lambda i, h, n: (i, 0)),
            ],
        ),
        out_shape=[
            jax.ShapeDtypeStruct((classes, NSHELL, width), jnp.bfloat16),
            jax.ShapeDtypeStruct((classes, LANES), jnp.float32),
        ],
        compiler_params=plain(24),
        name="gradient",
    )(head, nxt, image_hat, ref_hat, coef, post_sum)

    scaled, log_evidence = reduce_scatter(part, weight, evidence, slots, dp_count)
    result = jnp.dot(
        scaled.reshape(-1, width), inverse, preferred_element_type=jnp.float32
    )
    return (result.reshape((1,) + scaled.shape), log_evidence)


def solution(mesh):
    return jax.shard_map(
        local,
        mesh=mesh,
        in_specs=(
            P("dp", None, None),
            P("dp"),
            P("cls", None, None),
            P(),
            P(),
            P("dp", None),
            P("cls"),
        ),
        out_specs=(P("cls", "dp", None, None), P("dp")),
        check_vma=False,
    )
```
